32 devices in a mesh: dp: 4 (over x, core), tensor: 8 (over z, y).
Axes of the slice: x: 2, y: 2, z: 4, core: 2. Of those that a mesh axis runs over, the one named last changes fastest.
Arguments:
- tokens: bfloat16 [4096, 2048], P(('dp', 'tensor')), may hold values from -6 to 6
- segments: int32 [4, 1024], P('dp'), may hold values from 0 to 4, as said below
- routes: int32 [4096, 8], P(('dp', 'tensor')), may hold values from 0 to 15, all different within a row; in each aligned block of 128 rows (0 to 127, 128 to 255, ...) at most 80 rows name the same one
- gate_values: bfloat16 [4096, 8], P(('dp', 'tensor')), may hold values from 0.039794922 to 0.25
- cotangent: bfloat16 [4096, 2048], P(('dp', 'tensor')), may hold values from -6 to 6
- query_key_value: bfloat16 [3, 2048, 2048], P(None, 'dp', 'tensor'), may hold values from -0.125 to 0.125
- out_weight: bfloat16 [2048, 2048], P('tensor', 'dp'), may hold values from -1 to 1
- head_gain: bfloat16 [2, 16, 128], P(None, 'tensor', 'dp'), may hold values from 0.25 to 1.75
- layer_gain: bfloat16 [2, 2048], P(None, 'dp'), may hold values from 0.25 to 1.75
- gate_up: bfloat16 [16, 2, 2048, 1024], P(None, None, 'dp', 'tensor'), may hold values from -0.125 to 0.125
- down_weight: bfloat16 [16, 1024, 2048], P(None, 'tensor', 'dp'), may hold values from -0.75 to 0.75
Outputs:
- mixed: bfloat16 [4096, 2048], P(('dp', 'tensor'))
- input_grad: float32 [4096, 2048], P(('dp', 'tensor'))
- gate_grad: float32 [4096, 8], P(('dp', 'tensor'))
- query_key_value_grad: float32 [3, 2048, 2048], P(None, 'dp', 'tensor')
- out_weight_grad: float32 [2048, 2048], P('tensor', 'dp')
- head_gain_grad: float32 [2, 16, 128], P(None, 'tensor', 'dp')
- layer_gain_grad: float32 [2, 2048], P(None, ('dp', 'tensor'))
- gate_up_grad: float32 [16, 2, 2048, 1024], P(None, None, 'dp', 'tensor')
- down_weight_grad: float32 [16, 1024, 2048], P(None, 'tensor', 'dp')
The draws below stay inside these ranges and needn't reach their ends.
Inputs may be any that keep to these rules, and one draw needn't show every extreme that they name: `segments`: each row never falls; one document of each row begins within its first 128 positions and ends within its last 128. `routes`: within the 128 rows of one aligned block no expert is named more than 80 times, and each row names 8 different experts.
All inputs are finite; a program needn't handle non-finite values.
Results may differ from the reference program's by a relative error of at most 0.014.
Values may be sent and summed in bfloat16 or wider, within the bound.
No kernel may reach another device: no remote copies, remote signals or barrier semaphores. Data moves between devices by JAX's collectives and lax.ppermute only.
A program may use at most 448 MiB of HBM per device.

```python
import math
import jax
import jax.numpy as jnp
import numpy as np
from jax import lax

D = 2048
HEADS = 16
HD = 128
FF = 1024
E = 16
TOP = 8
SEQ = 1024
SEQS = 4
TOK_DEV = 128
TOKENS = 4096
CAPL = 80
N_TENSOR = 8


def draw_segments(key, part):
    key = jax.random.fold_in(key, 11)
    first_key, second_key = jax.random.split(key)
    begin_doc = jax.random.randint(first_key, (SEQS, 1), 2, TOK_DEV)
    end_doc = jax.random.randint(second_key, (SEQS, 1), SEQ - TOK_DEV + 1, SEQ - 1)
    positions = jnp.arange(SEQ, dtype=jnp.int32)[None, :]
    numbers = (positions >= begin_doc // 2).astype(jnp.int32) + (positions >= begin_doc).astype(jnp.int32)
    numbers = numbers + (positions >= end_doc).astype(jnp.int32)
    numbers = numbers + (positions >= end_doc + (SEQ - end_doc) // 2).astype(jnp.int32)
    return numbers.astype(jnp.int32)


def block_scale(key, shape, cuts, smallest, largest):
    def one(axis_at, blocks):
        steps = jax.random.uniform(jax.random.fold_in(jax.random.fold_in(key, 6), axis_at), (blocks,), jnp.float32, smallest / len(cuts), largest / len(cuts))
        return jnp.repeat(jnp.exp(steps), shape[axis_at] // blocks).reshape((-1,) + (1,) * (len(shape) - axis_at - 1))

    factor_of = one(*cuts[0])
    for cut in cuts[1:]:
        factor_of = factor_of * one(*cut)
    return factor_of


def shared_out(own_key, own, number, rows, number_of, top, reach, skew):
    order = jax.random.permutation(own_key, number_of)
    crowded, ordinary = portions_of(number_of, rows * top, reach, skew, True), portions_of(number_of, rows * top, reach, skew, False)
    places = jnp.arange(number_of)

    def named(tallies, turn):
        used = int((tallies > 0).sum())
        fixed = max(1, used // 4)
        moved = fixed + (places - fixed + turn * (used - fixed)) % max(1, number_of - fixed)
        return jnp.zeros((number_of,), jnp.int32).at[order[jnp.where(places < fixed, places, moved)]].set(jnp.asarray(tallies, jnp.int32))

    tallies = jnp.where(number % 4 == 0, named(crowded, number // 4), named(ordinary, number - number // 4 - 1))
    mixed = jax.random.permutation(jax.random.fold_in(own, 3), number_of)
    donor, receiver = mixed[0:number_of // 2 * 2:2], mixed[1:number_of // 2 * 2:2]
    margin = jnp.minimum(tallies[donor] - 1, reach - tallies[receiver]) // 2
    margin = jnp.where((donor == order[0]) | (receiver == order[0]) | (tallies[receiver] == 0), 0, jnp.maximum(margin, 0))
    moved = jax.random.randint(jax.random.fold_in(own, 4), (number_of // 2,), 0, 1 << 20) % (margin + 1)
    tallies = tallies.at[donor].add(-moved).at[receiver].add(moved)
    labels = jnp.searchsorted(jnp.cumsum(tallies), jnp.arange(rows * top), side="right").astype(jnp.int32)
    grid = labels.reshape(top, rows).T
    grid = grid[jax.random.permutation(jax.random.fold_in(own, 1), rows)]
    turn = jax.random.randint(jax.random.fold_in(own, 2), (rows, 1), 0, top)
    return jnp.take_along_axis(grid, (jnp.arange(top)[None, :] + turn) % top, axis=1)


def portions_of(number_of, total, most, lean, full):
    loads = [(1 << 20) // math.isqrt(standing ** lean) + 1 for standing in range(1, number_of + 1)]
    largest = most if full else min(most, max(-(-total // number_of), total * loads[0] // sum(loads)))
    least = 1 if total - largest >= number_of - 1 else 0
    holding, spare = [largest] + [least] * (number_of - 1), total - largest - least * (number_of - 1)
    while spare > 0:
        free = [i for i in range(1, number_of) if holding[i] < largest] or [i for i in range(1, number_of) if holding[i] < most]
        pool, left = sum([loads[i] for i in free]), spare
        for i in free:
            extra = min(most - holding[i], max(1, left * loads[i] // pool), spare)
            holding[i] = holding[i] + extra
            spare = spare - extra
    return np.array(holding)


def bell_draw(rng, extent, spread, bound, cuts=(), kind=jnp.bfloat16):
    gain = block_scale(rng, extent, cuts, -0.22, 0.18) if cuts else 1.0
    values = jax.random.normal(rng, extent, jnp.float32) * spread * gain
    return jnp.minimum(jnp.maximum(values, -bound), bound).astype(kind)


def setup_inputs(seed: int = 0) -> dict:
    key_list = jax.random.split(jax.random.key(seed), 12)
    tokens = bell_draw(key_list[0], (TOKENS, D), 1.0, 6.0, ((0, 32),))
    segments = draw_segments(jax.random.fold_in(key_list[11], 71), 0)
    routes_keys = jax.random.split(jax.random.fold_in(key_list[2], 1), TOKENS // TOK_DEV)
    routes_turns = jax.random.permutation(jax.random.fold_in(key_list[2], 3), TOKENS // TOK_DEV)
    routes = jax.vmap(lambda own, number: shared_out(jax.random.fold_in(key_list[2], 2), own, number, TOK_DEV, E, TOP, CAPL, 1))(routes_keys, routes_turns).reshape((TOKENS, TOP))
    gate_values = jnp.clip(0.039794922 + 0.21020508 * jax.random.uniform(key_list[3], (TOKENS, TOP), jnp.float32) ** block_scale(key_list[3], (TOKENS, TOP), ((0, 32),), -0.2, 0.2), 0.039794922, 0.25).astype(jnp.bfloat16)
    cotangent = bell_draw(key_list[4], (TOKENS, D), 1.0, 6.0, ((0, 32),))
    query_key_value = bell_draw(key_list[5], (3, D, D), D ** -0.5, 0.125, ((1, 4), (2, 8)))
    out_weight = bell_draw(key_list[6], (D, D), (D // 64) ** -0.5, 1.0, ((0, 8), (1, 4)))
    head_gain = jnp.clip(1.0 + 0.15 * jax.random.normal(key_list[7], (2, HEADS, HD), jnp.float32), 0.25, 1.75).astype(jnp.bfloat16)
    layer_gain = jnp.clip(1.0 + 0.15 * jax.random.normal(key_list[8], (2, D), jnp.float32), 0.25, 1.75).astype(jnp.bfloat16)
    gate_up = bell_draw(key_list[9], (E, 2, D, FF), D ** -0.5, 0.125, ((2, 4), (3, 8)))
    down_weight = bell_draw(key_list[10], (E, FF, D), (FF // 16) ** -0.5, 0.75, ((1, 8), (2, 4)))
    return {"tokens": tokens, "segments": segments, "routes": routes, "gate_values": gate_values, "cotangent": cotangent, "query_key_value": query_key_value, "out_weight": out_weight, "head_gain": head_gain, "layer_gain": layer_gain, "gate_up": gate_up, "down_weight": down_weight}


EPSILON = 1e-05
ROPE_BASE = 10000.0
PRECISE = lax.Precision.HIGHEST

@jax.custom_vjp
def low(v):
    return lax.optimization_barrier(v.astype(jnp.bfloat16)).astype(jnp.float32)

@jax.custom_vjp
def low_back(v):
    return v

def low_keep(v):
    return (low(v), None)

def low_pass(kept, grad):
    return (grad,)

def back_keep(v):
    return (v, None)

def back_low(kept, grad):
    return (low(grad),)
low.defvjp(low_keep, low_pass)
low_back.defvjp(back_keep, back_low)

def rounded_both(values_in):
    return low_back(low(values_in))

def mean_norm(values_in):
    return values_in * lax.rsqrt(lax.optimization_barrier(jnp.mean(values_in * values_in, axis=-1, keepdims=True)) + EPSILON)

def angles():
    positions = jnp.arange(SEQ, dtype=jnp.float32)
    inverse_freq = ROPE_BASE ** (-jnp.arange(HD // 2, dtype=jnp.float32) * 2.0 / HD)
    phases = positions[:, None] * inverse_freq[None, :]
    phases = jnp.concatenate([phases, phases], axis=-1)
    return (jnp.cos(phases)[:, None, :], jnp.sin(phases)[:, None, :])

def rotate(values_in, cosine_table, sine_table):
    half_width = values_in.shape[-1] // 2
    turned = jnp.concatenate([-values_in[..., half_width:], values_in[..., :half_width]], axis=-1)
    return values_in * cosine_table + turned * sine_table

def slot_table(route_rows):
    blocks = route_rows.reshape(N_TENSOR, TOK_DEV * TOP)
    chosen = (blocks[..., None] == jnp.arange(E, dtype=jnp.int32)).astype(jnp.int32)
    earlier = jnp.cumsum(chosen, axis=1) - chosen
    within = lax.optimization_barrier(jnp.sum(earlier * chosen, axis=-1))
    return (blocks * CAPL + within).reshape(N_TENSOR, TOK_DEV, TOP)

def layer_forward(weights, inputs, gates, seg_ids, slots):
    qkv_w, out_w, head_w, gain_w, gate_up_w, down_w = weights
    cosine_table, sine_table = angles()
    normed_in = low(mean_norm(inputs) * gain_w[0])
    query_raw = low_back(jnp.dot(normed_in, qkv_w[0], precision=PRECISE))
    key_raw = low_back(jnp.dot(normed_in, qkv_w[1], precision=PRECISE))
    values_r = rounded_both(jnp.dot(normed_in, qkv_w[2], precision=PRECISE)).reshape(SEQ, HEADS, HD)
    query_in = mean_norm(query_raw.reshape(SEQ, HEADS, HD)) * head_w[0]
    key_in = mean_norm(key_raw.reshape(SEQ, HEADS, HD)) * head_w[1]
    queries = low(rotate(query_in, cosine_table, sine_table))
    keys_r = low(rotate(key_in, cosine_table, sine_table))
    raw_scores = low_back(jnp.einsum('qhd,khd->hqk', queries, keys_r, precision=PRECISE) * HD ** (-0.5))
    positions = jnp.arange(SEQ, dtype=jnp.int32)
    allowed = (seg_ids[:, None] == seg_ids[None, :]) & (positions[None, :] <= positions[:, None])
    scores = jnp.where(allowed[None], raw_scores, -1e+30)
    shifted = jnp.exp(scores - lax.optimization_barrier(jnp.max(scores, axis=-1, keepdims=True)))
    probs_f = shifted / lax.optimization_barrier(jnp.sum(shifted, axis=-1, keepdims=True))
    context = rounded_both(jnp.einsum('hqk,khd->qhd', low(probs_f), values_r, precision=PRECISE)).reshape(SEQ, D)
    middle = inputs + low_back(jnp.dot(context, out_w, precision=PRECISE))
    normed_mid = low(mean_norm(middle) * gain_w[1])
    slot_picks = (slots[..., None] == jnp.arange(E * CAPL, dtype=jnp.int32)).astype(jnp.float32)
    dispatch = lax.optimization_barrier(jnp.sum(slot_picks, axis=2)).reshape(N_TENSOR, TOK_DEV, E, CAPL)
    combine = lax.optimization_barrier(jnp.sum(slot_picks * gates.reshape(N_TENSOR, TOK_DEV, TOP, 1), axis=2)).reshape(N_TENSOR, TOK_DEV, E, CAPL)
    expert_rows = jnp.einsum('ntec,ntd->encd', dispatch, normed_mid.reshape(N_TENSOR, TOK_DEV, D), precision=PRECISE)
    group_width = FF // N_TENSOR
    moe_sum = jnp.zeros((N_TENSOR, TOK_DEV, D), jnp.float32)
    for group_index in range(N_TENSOR):
        first_unit = group_index * group_width
        rows_used = low_back(expert_rows)
        gate_up_out = jnp.einsum('encd,egdf->gencf', rows_used, gate_up_w[:, :, :, first_unit:first_unit + group_width], precision=PRECISE)
        gate_part = low_back(gate_up_out[0])
        up_part = low_back(gate_up_out[1])
        hidden = low(gate_part * jax.nn.sigmoid(gate_part) * up_part)
        expert_out = rounded_both(jnp.einsum('encf,efd->encd', hidden, down_w[:, first_unit:first_unit + group_width], precision=PRECISE))
        moe_sum = moe_sum + jnp.einsum('ntec,encd->ntd', combine, expert_out, precision=PRECISE)
    return middle + moe_sum.reshape(SEQ, D)

def reference(tokens, segments, routes, gate_values, cotangent, query_key_value, out_weight, head_gain, layer_gain, gate_up, down_weight):
    weights = (query_key_value.astype(jnp.float32), out_weight.astype(jnp.float32), head_gain.astype(jnp.float32), layer_gain.astype(jnp.float32), gate_up.astype(jnp.float32), down_weight.astype(jnp.float32))

    def per_sequence(grad_sum, sequence):
        inputs, seg_ids, route_rows, gates, cot_rows = sequence
        slots = slot_table(route_rows)

        def forward(weights_in, inputs_in, gates_in):
            return layer_forward(weights_in, inputs_in, gates_in, seg_ids, slots)
        layer_out, pull_back = jax.vjp(forward, weights, inputs, gates)
        weight_grads, input_grad, gate_grad = pull_back(cot_rows)
        grad_sum = jax.tree.map(jnp.add, grad_sum, weight_grads)
        return (grad_sum, (layer_out.astype(jnp.bfloat16), input_grad, gate_grad))
    start_sum = jax.tree.map(jnp.zeros_like, weights)
    sequences = (tokens.astype(jnp.float32).reshape(SEQS, SEQ, D), segments, routes.reshape(SEQS, SEQ, TOP), gate_values.astype(jnp.float32).reshape(SEQS, SEQ, TOP), cotangent.astype(jnp.float32).reshape(SEQS, SEQ, D))
    grad_sum, outputs = lax.scan(per_sequence, start_sum, sequences)
    mixed_rows, input_rows, gate_rows = outputs
    return (mixed_rows.reshape(TOKENS, D), input_rows.reshape(TOKENS, D), gate_rows.reshape(TOKENS, TOP), grad_sum[0], grad_sum[1], grad_sum[2], grad_sum[3], grad_sum[4], grad_sum[5])
```

```python
import functools

import jax
import jax.numpy as jnp
from jax import lax
from jax.experimental import pallas as pl
from jax.experimental.pallas import tpu as pltpu
from jax.sharding import PartitionSpec as P

HD = 128
E = 16
EPSILON = 1e-05
ROPE_BASE = 10000.0
MASKED = -1e30
LANES = 128
CHUNKS = 2

f32 = jnp.float32
bf16 = jnp.bfloat16
NT = (((1,), (1,)), ((), ()))
TN = (((0,), (0,)), ((), ()))
ANY = pl.BlockSpec(memory_space=pl.ANY)
SMEM = pl.BlockSpec(memory_space=pltpu.SMEM)
VMEM = pl.BlockSpec(memory_space=pltpu.VMEM)


def dot(a, b):
    return jnp.dot(a, b, preferred_element_type=f32)


def dot_nt(a, b):
    return lax.dot_general(a, b, NT, preferred_element_type=f32)


def dot_tn(a, b):
    return lax.dot_general(a, b, TN, preferred_element_type=f32)


def shape(dims, dtype):
    return jax.ShapeDtypeStruct(dims, dtype)


def ring_of(groups):
    return list(range(0, groups, 2)) + list(range(groups - 1, 0, -2))


def ring_step(value, groups, sign):
    ring = ring_of(groups)
    pairs = [(ring[p], ring[(p + sign) % groups]) for p in range(groups)]
    return lax.ppermute(value, "tensor", pairs)


def ring_gather(own, groups):
    half = own.shape[0] // 2
    steps = groups // 2
    below, above = [own], [own]
    for _ in range(steps - 1):
        below.append(ring_step(below[-1], groups, 1))
        above.append(ring_step(above[-1], groups, -1))
    far_low = ring_step(below[-1][:half], groups, 1)
    far_high = ring_step(above[-1][half:], groups, -1)
    return [far_low, far_high, own] + above[1:] + below[:0:-1]


def ring_scatter(far_low, far_high, rest, groups):
    steps = groups // 2
    rows = rest.shape[0] // (groups - 1)

    def block(distance):
        at = (distance % groups if distance >= 0 else groups - 1 + distance) * rows
        return rest[at : at + rows].astype(f32)

    half = rows // 2
    rise = ring_step(far_low, groups, 1).astype(f32)
    fall = ring_step(far_high, groups, -1).astype(f32)
    rise = jnp.pad(rise, ((0, half), (0, 0)))
    fall = jnp.pad(fall, ((half, 0), (0, 0)))
    for distance in range(steps - 1, 0, -1):
        rise = ring_step((block(distance) + rise).astype(bf16), groups, 1).astype(f32)
        fall = ring_step((block(-distance) + fall).astype(bf16), groups, -1).astype(f32)
    return block(0) + rise + fall


def bits_of(count):
    return [1 << b for b in range(count.bit_length() - 1)]


def flip_step(value, axis, count, bit):
    return lax.ppermute(value, axis, [(s, s ^ bit) for s in range(count)])


def relative(parts, axis):
    count = len(parts)
    index = lax.axis_index(axis)
    for bit in bits_of(count):
        turned = (index & bit) != 0
        parts = [jnp.where(turned, parts[k ^ bit], parts[k]) for k in range(count)]
    return parts


def split_last(value, count):
    width = value.shape[-1] // count
    return [value[..., k * width : (k + 1) * width] for k in range(count)]


def relative_columns(value, axis, count):
    return jnp.concatenate(relative(split_last(value, count), axis), axis=-1)


def flip_gather(own, axis, count):
    parts = {0: own}
    for bit in reversed(bits_of(count)):
        for k in list(parts):
            parts[k ^ bit] = flip_step(parts[k], axis, count, bit)
    return [parts[k] for k in range(count)]


def flip_reduce(parts, axis, count):
    parts = list(parts)
    for bit in bits_of(count):
        for k in range(0, count, 2 * bit):
            sent = parts[k + bit]
            parts[k] = parts[k].astype(f32) + flip_step(sent, axis, count, bit).astype(f32)
            if k % (4 * bit) and 2 * bit < count:
                parts[k] = parts[k].astype(bf16)
    return parts[0]


def flip_reduce_rows(value, axis, count):
    for bit in bits_of(count):
        pairs = value.reshape((value.shape[0] // 2, 2) + value.shape[1:])
        value = pairs[:, 0] + flip_step(pairs[:, 1], axis, count, bit)
    return value[0]


def fetch(sources, target, sems, first, rows_at):
    copies = []
    for number, source in enumerate(sources):
        copy = pltpu.make_async_copy(
            source, target.at[pl.ds(rows_at[number], source.shape[0])], sems.at[first + number]
        )
        copy.start()
        copies.append(copy)
    return copies


def piece_rows(order, half, pieces):
    rows = 2 * half
    starts = [pl.multiple_of(order[0] * rows, rows)]
    starts.append(pl.multiple_of(order[0] * rows + half, half))
    for number in range(2, pieces):
        starts.append(pl.multiple_of(order[number - 1] * rows, rows))
    return starts


def send_out(staged, outs, sems, first, starts):
    low, high, rest = outs
    half = low.shape[0]
    copies = []
    targets = [low, high] + [
        rest.at[pl.ds(at, 2 * half)] for at in range(0, rest.shape[0], 2 * half)
    ]
    for number, target in enumerate(targets):
        copy = pltpu.make_async_copy(
            staged.at[pl.ds(starts[number], target.shape[0])], target, sems.at[first + number]
        )
        copy.start()
        copies.append(copy)
    return copies


def allowed_pairs(seg_col, seg_row, first, rows, width):
    row_pos = first + lax.broadcasted_iota(jnp.int32, (rows, width), 0)
    key_pos = lax.broadcasted_iota(jnp.int32, (rows, width), 1)
    return (seg_col[pl.ds(first, rows), :] == seg_row[:, pl.ds(0, width)]) & (key_pos <= row_pos)


def attn_fwd_body(n, count, block, *refs):
    it = iter(refs)
    order = next(it)
    pieces = [next(it) for _ in range(count)]
    wq = [next(it) for _ in range(n)]
    wo = [next(it) for _ in range(n)]
    gains, cosine, sine, seg_row, seg_col = (next(it) for _ in range(5))
    q_o, k_o, v_o, qr_o, kr_o, ctx_o, lse_o, x_o = (next(it) for _ in range(8))
    outs = [next(it) for _ in range(3)]
    xs, wqs, wos, stage, sems = (next(it) for _ in range(5))
    length, width = ctx_o.shape
    depth = wq[0].shape[1]
    heads = width // HD
    starts = piece_rows(order, pieces[0].shape[0], count)
    copies = []
    for k in range(n):
        for j in range(3):
            copies.append(
                pltpu.make_async_copy(
                    wq[k].at[j],
                    wqs.at[pl.ds(k * depth, depth), pl.ds(j * width, width)],
                    sems.at[2 * count + 4 * k + j],
                )
            )
        copies.append(
            pltpu.make_async_copy(
                wo[k], wos.at[:, pl.ds(k * depth, depth)], sems.at[2 * count + 4 * k + 3]
            )
        )
    for copy in copies:
        copy.start()
    for copy in copies + fetch(pieces, xs, sems, 0, starts):
        copy.wait()
    keep = pltpu.make_async_copy(xs, x_o, sems.at[0])
    keep.start()
    scale = HD ** (-0.5)

    def project(r, _):
        rows = pl.ds(pl.multiple_of(r * block, block), block)
        out = dot(xs[rows, :], wqs[...])
        v_o[rows, :] = out[:, 2 * width :].astype(bf16)
        for j, (raw_o, hat_o) in enumerate(((qr_o, q_o), (kr_o, k_o))):
            raw = out[:, j * width : (j + 1) * width]
            raw_o[rows, :] = raw
            for h in range(heads):
                cols = slice(h * HD, (h + 1) * HD)
                u = raw[:, cols]
                inv = lax.rsqrt(jnp.mean(u * u, axis=-1, keepdims=True) + EPSILON)
                u = u * inv * gains[j : j + 1, cols]
                u = u * cosine[rows, :] + pltpu.roll(u, HD // 2, 1) * sine[rows, :]
                hat_o[rows, cols] = u.astype(bf16)
        return 0

    lax.fori_loop(0, length // block, project, 0)
    for b in range(length // block):
        rows = pl.ds(b * block, block)
        hi = (b + 1) * block
        allowed = allowed_pairs(seg_col, seg_row, b * block, block, hi)
        for h in range(heads):
            cols = slice(h * HD, (h + 1) * HD)
            s = dot_nt(q_o[rows, cols], k_o[pl.ds(0, hi), cols]) * scale
            s = jnp.where(allowed, s, MASKED)
            top = jnp.max(s, axis=-1, keepdims=True)
            e = jnp.exp(s - top)
            total = jnp.sum(e, axis=-1, keepdims=True)
            probs = (e * (1.0 / total)).astype(bf16)
            ctx_o[rows, cols] = dot(probs, v_o[pl.ds(0, hi), cols]).astype(bf16)
            lse_o[h, rows, :] = top + jnp.log(total)
        stage[rows, :] = dot(ctx_o[rows, :], wos[...]).astype(bf16)
    for copy in send_out(stage, outs, sems, count, starts):
        copy.wait()
    keep.wait()


def attn_fwd(order, pieces, wq, wo, gains, cosine, sine, seg_row, seg_col):
    n, count = len(wq), len(pieces)
    half, d = pieces[0].shape
    length = cosine.shape[0]
    width = wo[0].shape[0]
    heads = width // HD
    block = min(256, length)
    scratch = [
        pltpu.VMEM((length, d), bf16),
        pltpu.VMEM((d, 3 * width), bf16),
        pltpu.VMEM((width, d), bf16),
        pltpu.VMEM((length, d), bf16),
        pltpu.SemaphoreType.DMA((2 * count + 4 * n,)),
    ]
    return pl.pallas_call(
        functools.partial(attn_fwd_body, n, count, block),
        in_specs=[SMEM] + [ANY] * (count + 2 * n) + [VMEM] * 5,
        out_specs=[VMEM] * 7 + [ANY] * 4,
        out_shape=[shape((length, width), bf16)] * 3
        + [shape((length, width), f32)] * 2
        + [shape((length, width), bf16), shape((heads, length, 1), f32), shape((length, d), bf16)]
        + [shape((half, d), bf16)] * 2
        + [shape((length - 2 * half, d), bf16)],
        scratch_shapes=scratch,
        compiler_params=pltpu.CompilerParams(vmem_limit_bytes=48 << 20),
        cost_estimate=pl.CostEstimate(
            flops=20 * length * d * width, bytes_accessed=40 << 20, transcendentals=0
        ),
        name="attn_fwd",
    )(order, *pieces, *wq, *wo, gains, cosine, sine, seg_row, seg_col)


def attn_bwd_body(n, count, block, *refs):
    it = iter(refs)
    order = next(it)
    pieces = [next(it) for _ in range(count)]
    wq = [next(it) for _ in range(n)]
    wo = [next(it) for _ in range(n)]
    q, k_, v, qr, kr, lse = (next(it) for _ in range(6))
    gains, cosine, sine, seg_row, seg_col, x = (next(it) for _ in range(6))
    outs = [next(it) for _ in range(3)]
    dp_o, hg_o, gs_o, db_o = (next(it) for _ in range(4))
    db, wqs, wos, stage, dctx, dq, dk, dv, sems = (next(it) for _ in range(9))
    length, width = q.shape
    depth = wq[0].shape[1]
    heads = width // HD
    starts = piece_rows(order, pieces[0].shape[0], count)
    copies = []
    for k in range(n):
        for j in range(3):
            copies.append(
                pltpu.make_async_copy(
                    wq[k].at[j],
                    wqs.at[pl.ds(k * depth, depth), pl.ds(j * width, width)],
                    sems.at[2 * count + 4 * k + j],
                )
            )
        copies.append(
            pltpu.make_async_copy(
                wo[k], wos.at[:, pl.ds(k * depth, depth)], sems.at[2 * count + 4 * k + 3]
            )
        )
    for copy in copies:
        copy.start()
    for copy in copies + fetch(pieces, db, sems, 0, starts):
        copy.wait()
    keep = pltpu.make_async_copy(db, db_o, sems.at[0])
    keep.start()
    scale = HD ** (-0.5)

    def branch(r, _):
        rows = pl.ds(pl.multiple_of(r * block, block), block)
        dctx[rows, :] = dot_nt(db[rows, :], wos[...]).astype(bf16)
        dk[rows, :] = jnp.zeros((block, width), f32)
        dv[rows, :] = jnp.zeros((block, width), f32)
        return 0

    lax.fori_loop(0, length // block, branch, 0)
    for b in range(length // block):
        rows = pl.ds(b * block, block)
        hi = (b + 1) * block
        low = pl.ds(0, hi)
        allowed = allowed_pairs(seg_col, seg_row, b * block, block, hi)
        for h in range(heads):
            cols = slice(h * HD, (h + 1) * HD)
            s = dot_nt(q[rows, cols], k_[low, cols]) * scale
            p = jnp.where(allowed, jnp.exp(s - lse[h, rows, :]), 0.0)
            g = dot_nt(dctx[rows, cols], v[low, cols])
            pg = p * g
            ds = (pg - p * jnp.sum(pg, axis=-1, keepdims=True)).astype(bf16)
            dq[rows, cols] = dot(ds, k_[low, cols]) * scale
            dk[low, cols] += dot_tn(ds, q[rows, cols]) * scale
            dv[low, cols] += dot_tn(p.astype(bf16), dctx[rows, cols])
    hg_o[...] = jnp.zeros_like(hg_o)
    gs_o[...] = jnp.zeros_like(gs_o)

    def finish(r, _):
        rows = pl.ds(pl.multiple_of(r * block, block), block)
        dp_o[rows, 2 * width :] = dv[rows, :].astype(bf16)
        for j, (raw, grad) in enumerate(((qr, dq), (kr, dk))):
            for h in range(heads):
                cols = slice(h * HD, (h + 1) * HD)
                u = raw[rows, cols]
                inv = lax.rsqrt(jnp.mean(u * u, axis=-1, keepdims=True) + EPSILON)
                hat = u * inv
                t = grad[rows, cols]
                t = t * cosine[rows, :] - pltpu.roll(t, HD // 2, 1) * sine[rows, :]
                hg_o[j : j + 1, cols] += jnp.sum(t * hat, axis=0, keepdims=True)
                w = t * gains[j : j + 1, cols]
                w = inv * (w - hat * jnp.mean(w * hat, axis=-1, keepdims=True))
                dp_o[rows, j * width + h * HD : j * width + (h + 1) * HD] = w.astype(bf16)
        out = dot_nt(dp_o[rows, :], wqs[...])
        gs_o[...] += jnp.sum(out * x[rows, :].astype(f32), axis=0, keepdims=True)
        stage[rows, :] = out.astype(bf16)
        return 0

    lax.fori_loop(0, length // block, finish, 0)
    for copy in send_out(stage, outs, sems, count, starts):
        copy.wait()
    keep.wait()


def attn_bwd(order, pieces, wq, wo, q, k, v, qr, kr, lse, gains, cosine, sine, seg_row, seg_col, x):
    n, count = len(wq), len(pieces)
    half, d = pieces[0].shape
    length, width = q.shape
    block = min(256, length)
    scratch = [
        pltpu.VMEM((length, d), bf16),
        pltpu.VMEM((d, 3 * width), bf16),
        pltpu.VMEM((width, d), bf16),
        pltpu.VMEM((length, d), bf16),
        pltpu.VMEM((length, width), bf16),
        pltpu.VMEM((length, width), f32),
        pltpu.VMEM((length, width), f32),
        pltpu.VMEM((length, width), f32),
        pltpu.SemaphoreType.DMA((2 * count + 4 * n,)),
    ]
    return pl.pallas_call(
        functools.partial(attn_bwd_body, n, count, block),
        in_specs=[SMEM] + [ANY] * (count + 2 * n) + [VMEM] * 12,
        out_specs=[ANY] * 3 + [VMEM] * 3 + [ANY],
        out_shape=[shape((half, d), bf16)] * 2
        + [shape((length - 2 * half, d), bf16)]
        + [
            shape((length, 3 * width), bf16),
            shape((2, width), f32),
            shape((1, d), f32),
            shape((length, d), bf16),
        ],
        scratch_shapes=scratch,
        compiler_params=pltpu.CompilerParams(vmem_limit_bytes=48 << 20),
        cost_estimate=pl.CostEstimate(
            flops=40 * length * d * width, bytes_accessed=40 << 20, transcendentals=0
        ),
        name="attn_bwd",
    )(order, *pieces, *wq, *wo, q, k, v, qr, kr, lse, gains, cosine, sine, seg_row, seg_col, x)


def attn_grad_body(x, dp, ctx, db, qkv_o, out_o):
    width = ctx.shape[1]
    grad = dot_tn(x[...], dp[...])
    for j in range(3):
        qkv_o[0, j] = grad[:, j * width : (j + 1) * width].astype(bf16)
    out_o[0] = dot_tn(ctx[...], db[...]).astype(bf16)


def attn_grad(x, dp, ctx, db, n):
    length, d = x.shape
    width = ctx.shape[1]
    depth = d // n
    return pl.pallas_call(
        attn_grad_body,
        grid=(n,),
        in_specs=[
            pl.BlockSpec((length, depth), lambda k: (0, k)),
            pl.BlockSpec((length, 3 * width), lambda k: (0, 0)),
            pl.BlockSpec((length, width), lambda k: (0, 0)),
            pl.BlockSpec((length, depth), lambda k: (0, k)),
        ],
        out_specs=[
            pl.BlockSpec((1, 3, depth, width), lambda k: (k, 0, 0, 0)),
            pl.BlockSpec((1, width, depth), lambda k: (k, 0, 0)),
        ],
        out_shape=[shape((n, 3, depth, width), bf16), shape((n, width, depth), bf16)],
        compiler_params=pltpu.CompilerParams(vmem_limit_bytes=32 << 20),
        cost_estimate=pl.CostEstimate(
            flops=8 * length * d * width, bytes_accessed=16 << 20, transcendentals=0
        ),
        name="attn_grad",
    )(x, dp, ctx, db)


def moe_body(n, group, block, steps, count, *refs):
    it = iter(refs)
    xp = [next(it) for _ in range(count)]
    cp = [next(it) for _ in range(count)]
    gu = [next(it) for _ in range(n)]
    dn = [next(it) for _ in range(n)]
    moe_o = [next(it) for _ in range(3)]
    dm_o = [next(it) for _ in range(3)]
    hw_o, dgu_o = next(it), next(it)
    xs, cs, wgu, wd, macc, dacc, gg, sems = (next(it) for _ in range(8))
    length, d = xs.shape
    fw, depth = dn[0].shape[1], dn[0].shape[2]
    step = pl.program_id(0)
    half = xp[0].shape[0]
    starts = [0, half] + [2 * half * (i - 1) for i in range(2, count)]

    @pl.when(step == 0)
    def _():
        copies = fetch(xp, xs, sems, 0, starts) + fetch(cp, cs, sems, count, starts)
        macc[...] = jnp.zeros_like(macc)
        dacc[...] = jnp.zeros_like(dacc)
        gg[...] = jnp.zeros_like(gg)
        for copy in copies:
            copy.wait()

    for k in range(n):
        for i in range(group):
            for g in range(2):
                wgu[pl.ds(k * depth, depth), pl.ds((2 * i + g) * fw, fw)] = gu[k][i, g]
            wd[pl.ds(i * fw, fw), pl.ds(k * depth, depth)] = dn[k][i]

    def rows_of(r, _):
        rows = pl.ds(pl.multiple_of(r * block, block), block)
        gate_up = dot(xs[rows, :], wgu[...])
        d_hid = dot_nt(cs[rows, pl.ds(0, d)], wd[...])
        gates = cs[rows, pl.ds(d, LANES)].astype(f32)
        lane = lax.broadcasted_iota(jnp.int32, gates.shape, 1)
        total = jnp.zeros(gates.shape, f32)
        hidden, grads = [], []
        for i in range(group):
            pick = lane == step * group + i
            w = jnp.sum(jnp.where(pick, gates, 0.0), axis=1, keepdims=True)
            g = gate_up[:, 2 * i * fw : (2 * i + 1) * fw]
            u = gate_up[:, (2 * i + 1) * fw : (2 * i + 2) * fw]
            dh = d_hid[:, i * fw : (i + 1) * fw]
            z = jax.nn.sigmoid(g)
            swish = g * z
            h = swish * u
            total = total + jnp.where(pick, jnp.sum(h * dh, axis=1, keepdims=True), 0.0)
            dw = dh * w
            hidden.append((h * w).astype(bf16))
            grads.append((dw * u * z * (1.0 + g * (1.0 - z))).astype(bf16))
            grads.append((dw * swish).astype(bf16))
        hid = jnp.concatenate(hidden, axis=1)
        grad = jnp.concatenate(grads, axis=1)
        hw_o[rows, :] = hid
        dgu_o[rows, :] = grad
        gg[rows, :] += total
        macc[rows, :] += dot(hid, wd[...])
        dacc[rows, :] += dot_nt(grad, wgu[...])
        return 0

    lax.fori_loop(0, length // block, rows_of, 0)

    @pl.when(step == steps - 1)
    def _():
        xs[...] = dacc[...].astype(bf16)
        copies = send_out(xs, dm_o, sems, 0, starts)
        cs[:, pl.ds(0, d)] = macc[...].astype(bf16)
        cs[:, pl.ds(d, LANES)] = gg[...].astype(bf16)
        copies = copies + send_out(cs, moe_o, sems, count, starts)
        for copy in copies:
            copy.wait()


def moe(xp, cp, gate_up, down, group=2):
    n, count = len(gate_up), len(xp)
    experts, _, depth, fw = gate_up[0].shape
    d = n * depth
    wide = d + LANES
    half = xp[0].shape[0]
    length = sum(p.shape[0] for p in xp)
    steps = experts // group

    def outs(columns):
        return [shape((half, columns), bf16)] * 2 + [shape((length - 2 * half, columns), bf16)]

    return pl.pallas_call(
        functools.partial(moe_body, n, group, min(512, length), steps, count),
        grid=(steps,),
        in_specs=[ANY] * (2 * count)
        + [pl.BlockSpec((group, 2, depth, fw), lambda s: (s, 0, 0, 0))] * n
        + [pl.BlockSpec((group, fw, depth), lambda s: (s, 0, 0))] * n,
        out_specs=[ANY] * 6
        + [
            pl.BlockSpec((length, group * fw), lambda s: (0, s)),
            pl.BlockSpec((length, 2 * group * fw), lambda s: (0, s)),
        ],
        out_shape=outs(wide)
        + outs(d)
        + [shape((length, experts * fw), bf16), shape((length, 2 * experts * fw), bf16)],
        scratch_shapes=[
            pltpu.VMEM((length, d), bf16),
            pltpu.VMEM((length, wide), bf16),
            pltpu.VMEM((d, 2 * group * fw), bf16),
            pltpu.VMEM((group * fw, d), bf16),
            pltpu.VMEM((length, d), f32),
            pltpu.VMEM((length, d), f32),
            pltpu.VMEM((length, LANES), f32),
            pltpu.SemaphoreType.DMA((2 * count,)),
        ],
        compiler_params=pltpu.CompilerParams(vmem_limit_bytes=60 << 20),
        cost_estimate=pl.CostEstimate(
            flops=18 * length * d * experts * fw, bytes_accessed=60 << 20, transcendentals=0
        ),
        name="moe",
    )(*xp, *cp, *gate_up, *down)


def turn_body(count, *refs):
    pieces, out, xs, sems = refs[:count], refs[count], refs[count + 1], refs[count + 2]
    half = pieces[0].shape[0]
    starts = [0, half] + [2 * half * (i - 1) for i in range(2, count)]
    for copy in fetch(pieces, xs, sems, 0, starts):
        copy.wait()
    length, d = xs.shape
    size = 256
    eye = (
        lax.broadcasted_iota(jnp.int32, (size, size), 0)
        == lax.broadcasted_iota(jnp.int32, (size, size), 1)
    ).astype(bf16)
    for at in range(0, d, size):
        out[pl.ds(at, size), :] = dot_nt(eye, xs[:, pl.ds(at, size)]).astype(bf16)


def turn_rows(pieces):
    count = len(pieces)
    length = sum(p.shape[0] for p in pieces)
    d = pieces[0].shape[1]
    return pl.pallas_call(
        functools.partial(turn_body, count),
        in_specs=[ANY] * count,
        out_specs=VMEM,
        out_shape=shape((d, length), bf16),
        scratch_shapes=[pltpu.VMEM((length, d), bf16), pltpu.SemaphoreType.DMA((count,))],
        compiler_params=pltpu.CompilerParams(vmem_limit_bytes=32 << 20),
        cost_estimate=pl.CostEstimate(
            flops=2 * length * d * 256, bytes_accessed=8 << 20, transcendentals=0
        ),
        name="turn_rows",
    )(*pieces)


def moe_grad_body(n, group, count, xt, dgu, hw, *refs):
    pieces = refs[:count]
    gu_o = refs[count : count + n]
    dn_o = refs[count + n : count + 2 * n]
    cs, sems = refs[count + 2 * n :]
    fw, depth = dn_o[0].shape[1], dn_o[0].shape[2]
    half = pieces[0].shape[0]
    d = n * depth
    starts = [0, half] + [2 * half * (i - 1) for i in range(2, count)]

    @pl.when(pl.program_id(0) == 0)
    def _():
        for copy in fetch([p.at[:, pl.ds(0, d)] for p in pieces], cs, sems, 0, starts):
            copy.wait()

    for k in range(n):
        grad = dot(xt[pl.ds(k * depth, depth), :], dgu[...])
        for i in range(group):
            for g in range(2):
                at = (2 * i + g) * fw
                gu_o[k][i, g] = grad[:, at : at + fw].astype(bf16)
    turned = hw[...].T
    for k in range(n):
        grad = dot(turned, cs[:, pl.ds(k * depth, depth)])
        for i in range(group):
            dn_o[k][i] = grad[i * fw : (i + 1) * fw].astype(bf16)


def moe_grad(xt, dgu, hw, cp, n, experts, first, number, group=2):
    d, length = xt.shape
    count = len(cp)
    depth = d // n
    fw = hw.shape[1] // experts
    start = first // group
    return pl.pallas_call(
        functools.partial(moe_grad_body, n, group, count),
        grid=(number // group,),
        in_specs=[
            pl.BlockSpec((d, length), lambda s: (0, 0)),
            pl.BlockSpec((length, 2 * group * fw), lambda s: (0, s + start)),
            pl.BlockSpec((length, group * fw), lambda s: (0, s + start)),
        ]
        + [ANY] * count,
        out_specs=[pl.BlockSpec((group, 2, depth, fw), lambda s: (s, 0, 0, 0))] * n
        + [pl.BlockSpec((group, fw, depth), lambda s: (s, 0, 0))] * n,
        out_shape=[shape((number, 2, depth, fw), bf16)] * n + [shape((number, fw, depth), bf16)] * n,
        scratch_shapes=[pltpu.VMEM((length, d), bf16), pltpu.SemaphoreType.DMA((count,))],
        compiler_params=pltpu.CompilerParams(vmem_limit_bytes=48 << 20),
        cost_estimate=pl.CostEstimate(
            flops=6 * length * d * number * fw, bytes_accessed=30 << 20, transcendentals=0
        ),
        name="moe_grad",
    )(xt, dgu, hw, *cp)


def rope_tables(length):
    positions = jnp.arange(length, dtype=f32)
    inverse_freq = ROPE_BASE ** (-jnp.arange(HD // 2, dtype=f32) * 2.0 / HD)
    phases = positions[:, None] * inverse_freq[None, :]
    cosine, sine = jnp.cos(phases), jnp.sin(phases)
    return jnp.concatenate([cosine, cosine], axis=-1), jnp.concatenate([-sine, sine], axis=-1)


def per_device(
    tokens,
    segments,
    routes,
    gate_values,
    cotangent,
    query_key_value,
    out_weight,
    head_gain,
    layer_gain,
    gate_up,
    down_weight,
):
    groups = lax.axis_size("tensor")
    n = lax.axis_size("dp")
    own_rows, d = tokens.shape
    seq_len = own_rows * groups
    heads = query_key_value.shape[2] // HD
    depth = d // n

    small = jnp.concatenate([layer_gain.reshape(-1), head_gain.reshape(-1)])
    small = flip_gather(small, "dp", n)
    cut = 2 * depth
    gain_rel = jnp.concatenate([s[:cut].reshape(2, depth) for s in small], axis=1).astype(f32)
    gain_in, gain_mid = gain_rel[0], gain_rel[1]
    head_parts = relative([s[cut:].reshape(2, heads, HD // n) for s in small], "dp")
    gain_head = jnp.concatenate(head_parts, axis=2).reshape(2, heads * HD).astype(f32)

    ring = jnp.array(ring_of(groups), jnp.int32)
    place = jnp.argmax(ring == lax.axis_index("tensor")).astype(jnp.int32)
    steps = groups // 2
    distances = [steps] + list(range(steps)) + list(range(1 - steps, 0))
    order = ring[(place + jnp.array(distances, jnp.int32)) % groups]
    cosine, sine = rope_tables(seq_len)
    seg_row = segments.reshape(1, seq_len)
    seg_col = segments.reshape(seq_len, 1)
    chosen = routes[:, :, None] == jnp.arange(E, dtype=jnp.int32)
    gates = jnp.sum(jnp.where(chosen, gate_values.astype(f32)[:, :, None], 0.0), axis=1)

    x = relative_columns(tokens, "dp", n).astype(f32)
    inv_in = lax.rsqrt(jnp.mean(x * x, axis=-1, keepdims=True) + EPSILON)
    x_hat = x * inv_in
    normed_in = ring_gather((x_hat * gain_in).astype(bf16), groups)
    wq = flip_gather(query_key_value, "dp", n)
    wo = flip_gather(out_weight, "dp", n)
    d_out = relative_columns(cotangent, "dp", n)
    q, k, v, q_raw, k_raw, context, lse, normed_all, *attn = attn_fwd(
        order, normed_in, wq, wo, gain_head, cosine, sine, seg_row, seg_col
    )
    with_gates = jnp.concatenate(
        [d_out, jnp.pad(gates, ((0, 0), (0, LANES - E))).astype(bf16)], axis=1
    )
    d_pieces = ring_gather(with_gates, groups)
    middle = x + ring_scatter(*attn, groups)
    inv_mid = lax.rsqrt(jnp.mean(middle * middle, axis=-1, keepdims=True) + EPSILON)
    mid_hat = middle * inv_mid
    normed_mid = ring_gather((mid_hat * gain_mid).astype(bf16), groups)

    gu = flip_gather(gate_up, "dp", n)
    dn = flip_gather(down_weight, "dp", n)
    *both, hidden, d_gate_up = moe(normed_mid, d_pieces, gu, dn)
    d_normed_mid = ring_scatter(*both[3:], groups)
    d_mid_hat = d_normed_mid * gain_mid
    d_middle = d_out.astype(f32) + inv_mid * (
        d_mid_hat - mid_hat * jnp.mean(d_mid_hat * mid_hat, axis=-1, keepdims=True)
    )
    d_branch = ring_gather(d_middle.astype(bf16), groups)
    mixed_rel = ring_scatter(*both[:3], groups)
    layer_out = relative_columns((middle + mixed_rel[:, :d]).astype(bf16), "dp", n)
    gate_grad = jnp.sum(jnp.where(chosen, mixed_rel[:, None, d : d + E], 0.0), axis=-1)

    mid_turned = turn_rows(normed_mid)
    number = E // CHUNKS
    gu_parts, dn_parts = [], []
    for c in range(CHUNKS):
        grads = moe_grad(mid_turned, d_gate_up, hidden, d_pieces, n, E, c * number, number)
        gu_parts.append(flip_reduce(grads[:n], "dp", n))
        dn_parts.append(flip_reduce(grads[n:], "dp", n))

    *to_rows, d_projected, head_part, in_part, d_branch_all = attn_bwd(
        order, d_branch, wq, wo, q, k, v, q_raw, k_raw, lse, gain_head, cosine, sine,
        seg_row, seg_col, normed_all,
    )
    d_normed_in = ring_scatter(*to_rows, groups)
    qkv_grad, out_grad = attn_grad(normed_all, d_projected, context, d_branch_all, n)
    qkv_grad = flip_reduce([qkv_grad[k] for k in range(n)], "dp", n)
    out_grad = flip_reduce([out_grad[k] for k in range(n)], "dp", n)

    d_x_hat = d_normed_in * gain_in
    input_grad = d_middle + inv_in * (
        d_x_hat - x_hat * jnp.mean(d_x_hat * x_hat, axis=-1, keepdims=True)
    )
    input_grad = relative_columns(input_grad, "dp", n)

    mid_part = jnp.sum(d_normed_mid * mid_hat, axis=0)
    layer_part = jnp.stack([in_part[0] / gain_in, mid_part])
    head_rel = relative(split_last(head_part.reshape(2, heads, HD), n), "dp")
    rows = [
        jnp.concatenate([a.reshape(-1), b.reshape(-1)])
        for a, b in zip(split_last(layer_part, n), head_rel)
    ]
    summed = flip_reduce_rows(jnp.stack(rows), "dp", n)
    head_grad = summed[cut:].reshape(2, heads, HD // n)
    layer_parts = relative(split_last(summed[:cut].reshape(2, depth), groups), "tensor")
    layer_grad = flip_reduce_rows(jnp.stack(layer_parts), "tensor", groups)

    return (
        layer_out,
        input_grad,
        gate_grad,
        qkv_grad,
        out_grad,
        head_grad,
        layer_grad,
        jnp.concatenate(gu_parts, axis=0),
        jnp.concatenate(dn_parts, axis=0),
    )


def solution(mesh):
    return jax.shard_map(
        per_device,
        mesh=mesh,
        in_specs=(
            P(("dp", "tensor"), None),
            P("dp", None),
            P(("dp", "tensor"), None),
            P(("dp", "tensor"), None),
            P(("dp", "tensor"), None),
            P(None, "dp", "tensor"),
            P("tensor", "dp"),
            P(None, "tensor", "dp"),
            P(None, "dp"),
            P(None, None, "dp", "tensor"),
            P(None, "tensor", "dp"),
        ),
        out_specs=(
            P(("dp", "tensor"), None),
            P(("dp", "tensor"), None),
            P(("dp", "tensor"), None),
            P(None, "dp", "tensor"),
            P("tensor", "dp"),
            P(None, "tensor", "dp"),
            P(None, ("dp", "tensor")),
            P(None, None, "dp", "tensor"),
            P(None, "tensor", "dp"),
        ),
        check_vma=False,
    )
```

```python
import functools

import jax
import jax.numpy as jnp
import numpy as np
from jax import lax
from jax.experimental import pallas as pl
from jax.experimental.pallas import tpu as pltpu
from jax.sharding import PartitionSpec as P

HD = 128
E = 16
EPSILON = 1e-05
ROPE_BASE = 10000.0
MASKED = -1e30
LANES = 128
CHUNKS = 4
VMEM_BYTES = 60 << 20

f32 = jnp.float32
bf16 = jnp.bfloat16
NT = (((1,), (1,)), ((), ()))
TN = (((0,), (0,)), ((), ()))
ANY = pl.BlockSpec(memory_space=pl.ANY)
SMEM = pl.BlockSpec(memory_space=pltpu.SMEM)
VMEM = pl.BlockSpec(memory_space=pltpu.VMEM)


def dot(a, b):
    return jnp.dot(a, b, preferred_element_type=f32)


def dot_nt(a, b):
    return lax.dot_general(a, b, NT, preferred_element_type=f32)


def dot_tn(a, b):
    return lax.dot_general(a, b, TN, preferred_element_type=f32)


def shape(dims, dtype):
    return jax.ShapeDtypeStruct(dims, dtype)


def ring_of(groups):
    return list(range(0, groups, 2)) + list(range(groups - 1, 0, -2))


def distances_of(groups):
    steps = groups // 2
    near = [s * k for k in range(steps - 1, 0, -1) for s in (1, -1)]
    return [steps] + near + [0]


def ring_step(value, groups, sign):
    ring = ring_of(groups)
    pairs = [(ring[p], ring[(p + sign) % groups]) for p in range(groups)]
    return lax.ppermute(value, "tensor", pairs)


def tie(values, after):
    values, after = tuple(values), tuple(after)
    return lax.optimization_barrier(values + after)[: len(values)]


class Gather:
    def __init__(self, own, groups):
        self.groups, self.steps = groups, groups // 2
        self.below, self.above = [own], [own]

    def step(self, after=()):
        low, high = self.below[-1], self.above[-1]
        if len(self.below) == self.steps:
            half = low.shape[0] // 2
            low, high = low[:half], high[half:]
        if after:
            low, high = tie((low, high), after)
        self.below.append(ring_step(low, self.groups, 1))
        self.above.append(ring_step(high, self.groups, -1))
        return [self.below[-1], self.above[-1]]

    def run(self):
        while len(self.below) <= self.steps:
            self.step()
        return self

    def at(self, distance):
        return self.above[distance] if distance >= 0 else self.below[-distance]

    def far(self):
        return [self.below[self.steps], self.above[self.steps]]

    def pieces(self):
        return self.far() + [self.at(k) for k in distances_of(self.groups)[1:]]


class Scatter:
    def __init__(self, pieces, groups):
        self.groups, self.steps, self.done = groups, groups // 2, 0
        self.far = pieces[:2]
        self.block = dict(zip(distances_of(groups)[1:], pieces[2:]))

    def step(self, after=(), riders=None):
        if self.done == 0:
            sent = self.far
        else:
            distance = self.steps - self.done
            low, high = (v.astype(f32) for v in self.moved)
            if self.done == 1:
                half = low.shape[0]
                low = jnp.pad(low, ((0, half), (0, 0)))
                high = jnp.pad(high, ((half, 0), (0, 0)))
            dtype = self.far[0].dtype
            low = (self.block[distance].astype(f32) + low).astype(dtype)
            high = (self.block[-distance].astype(f32) + high).astype(dtype)
            sent = [low, high]
        rows, columns = sent[0].shape
        if riders:
            riders = [jnp.pad(r, ((0, 0), (0, columns - r.shape[1]))) for r in riders]
            sent = [jnp.concatenate(pair, axis=0) for pair in zip(sent, riders)]
        if after:
            sent = tie(sent, after)
        self.moved = [ring_step(sent[0], self.groups, 1), ring_step(sent[1], self.groups, -1)]
        self.done += 1
        if riders:
            self.ridden = [m[rows:] for m in self.moved]
            self.moved = [m[:rows] for m in self.moved]
        return self.moved

    def run(self):
        while self.done < self.steps:
            self.step()
        return self

    def result(self):
        low, high = self.moved
        return self.block[0].astype(f32) + low.astype(f32) + high.astype(f32)


def bits_of(count):
    return [1 << b for b in range(count.bit_length() - 1)]


def flip_step(value, axis, count, bit):
    return lax.ppermute(value, axis, [(s, s ^ bit) for s in range(count)])


def relative(parts, axis):
    count = len(parts)
    index = lax.axis_index(axis)
    for bit in bits_of(count):
        turned = (index & bit) != 0
        parts = [jnp.where(turned, parts[k ^ bit], parts[k]) for k in range(count)]
    return parts


def split_last(value, count):
    width = value.shape[-1] // count
    return [value[..., k * width : (k + 1) * width] for k in range(count)]


def flip_reduce(keep, sent, axis, count):
    return flip_rest(keep, flip_step(sent, axis, count, 1), axis, count)


def flip_rest(keep, got, axis, count):
    for bit in bits_of(count)[1:]:
        odd = (keep[1::2].astype(f32) + got[1::2].astype(f32)).astype(bf16)
        more = flip_step(odd, axis, count, bit)
        if 2 * bit < count:
            keep = (keep[0::2].astype(f32) + got[0::2].astype(f32)).astype(bf16)
            got = more
    return [keep, got, more, odd]


def flip_reduce_rows(value, axis, count):
    for bit in bits_of(count):
        pairs = value.reshape((value.shape[0] // 2, 2) + value.shape[1:])
        value = pairs[:, 0] + flip_step(pairs[:, 1], axis, count, bit)
    return value[0]


def fetch(sources, target, sems, first, rows_at):
    copies = []
    for number, source in enumerate(sources):
        if source.shape[1] > target.shape[1]:
            source = source.at[:, pl.ds(0, target.shape[1])]
        copy = pltpu.make_async_copy(
            source, target.at[pl.ds(rows_at[number], source.shape[0])], sems.at[first + number]
        )
        copy.start()
        copies.append(copy)
    return copies


def load_projections(weights, wqs, sems, first):
    copies = []
    n, _, width = weights.shape
    depth = wqs.shape[0] // n
    for k in range(n):
        for j in range(3):
            source = weights.at[k, pl.ds(j * depth, depth)]
            target = wqs.at[pl.ds(k * depth, depth), pl.ds(j * width, width)]
            copies.append(pltpu.make_async_copy(source, target, sems.at[first + 3 * k + j]))
    return copies


def load_outputs(weights, wos, sems, first):
    copies = []
    n, _, width = weights.shape
    depth = wos.shape[1] // n
    cuts = max(1, depth // width)
    columns = depth // cuts
    for k in range(n):
        for c in range(cuts):
            source = weights.at[k, pl.ds(3 * depth + c * width, width), pl.ds(0, columns)]
            target = wos.at[:, pl.ds(k * depth + c * columns, columns)]
            copies.append(pltpu.make_async_copy(source, target, sems.at[first + cuts * k + c]))
    return copies


def output_copies(n, depth, width):
    return n * max(1, depth // width)


def piece_shapes(own_rows, columns, count):
    half = shape((own_rows // 2, columns), bf16)
    return [half, half] + [shape((own_rows, columns), bf16)] * (count - 2)


def cost(micros):
    return pl.CostEstimate(flops=int(micros * 6e8), bytes_accessed=1 << 20, transcendentals=0)


def piece_rows(order, half, pieces):
    rows = 2 * half
    starts = [pl.multiple_of(order[0] * rows, rows)]
    starts.append(pl.multiple_of(order[0] * rows + half, half))
    for number in range(2, pieces):
        starts.append(pl.multiple_of(order[number - 1] * rows, rows))
    return starts


def send_out(staged, targets, sems, first, starts):
    copies = []
    for number, target in enumerate(targets):
        copy = pltpu.make_async_copy(
            staged.at[pl.ds(starts[number], target.shape[0])], target, sems.at[first + number]
        )
        copy.start()
        copies.append(copy)
    return copies


def allowed_pairs(seg_col, seg_row, first, rows, width):
    row_pos = first + lax.broadcasted_iota(jnp.int32, (rows, width), 0)
    key_pos = lax.broadcasted_iota(jnp.int32, (rows, width), 1)
    return (seg_col[pl.ds(first, rows), :] == seg_row[:, pl.ds(0, width)]) & (key_pos <= row_pos)


def attn_proj_body(count, block, *refs):
    it = iter(refs)
    order = next(it)
    pieces = [next(it) for _ in range(count)]
    wq = next(it)
    gain, gains, cosine, sine = (next(it) for _ in range(4))
    q_o, k_o, v_o, qr_o, kr_o, x_o = (next(it) for _ in range(6))
    xs, xn, wqs, sems = (next(it) for _ in range(4))
    length, width = q_o.shape
    heads = width // HD
    starts = piece_rows(order, pieces[0].shape[0], count)
    copies = load_projections(wq, wqs, sems, count)
    for copy in copies:
        copy.start()
    for copy in fetch(pieces, xs, sems, 0, starts) + copies:
        copy.wait()

    def project(r, _):
        rows = pl.ds(pl.multiple_of(r * block, block), block)
        wide = xs[rows, :].astype(f32)
        inv = lax.rsqrt(jnp.mean(wide * wide, axis=-1, keepdims=True) + EPSILON)
        xn[rows, :] = (wide * inv * gain[...]).astype(bf16)
        out = dot(xn[rows, :], wqs[...])
        v_o[rows, :] = out[:, 2 * width :].astype(bf16)
        for j, (raw_o, hat_o) in enumerate(((qr_o, q_o), (kr_o, k_o))):
            raw = out[:, j * width : (j + 1) * width]
            raw_o[rows, :] = raw
            for h in range(heads):
                cols = slice(h * HD, (h + 1) * HD)
                u = raw[:, cols]
                inv = lax.rsqrt(jnp.mean(u * u, axis=-1, keepdims=True) + EPSILON)
                u = u * inv * gains[j : j + 1, cols]
                u = u * cosine[rows, :] + pltpu.roll(u, HD // 2, 1) * sine[rows, :]
                hat_o[rows, cols] = u.astype(bf16)
        return 0

    lax.fori_loop(0, length // block, project, 0)
    keep = pltpu.make_async_copy(xn, x_o, sems.at[0])
    keep.start()
    keep.wait()


def attn_proj(order, pieces, wq, gain, gains, cosine, sine):
    n, count = wq.shape[0], len(pieces)
    d = gain.shape[1]
    length = cosine.shape[0]
    width = wq.shape[2]
    return pl.pallas_call(
        functools.partial(attn_proj_body, count, min(256, length)),
        in_specs=[SMEM] + [ANY] * (count + 1) + [VMEM] * 4,
        out_specs=[VMEM] * 5 + [ANY],
        out_shape=[shape((length, width), bf16)] * 3
        + [shape((length, width), f32)] * 2
        + [shape((length, d), bf16)],
        scratch_shapes=[
            pltpu.VMEM((length, d), bf16),
            pltpu.VMEM((length, d), bf16),
            pltpu.VMEM((d, 3 * width), bf16),
            pltpu.SemaphoreType.DMA((count + 3 * n,)),
        ],
        compiler_params=pltpu.CompilerParams(vmem_limit_bytes=VMEM_BYTES),
        cost_estimate=cost(10),
        name="attn_proj",
    )(order, *pieces, wq, gain, gains, cosine, sine)


def attn_core_body(count, block, *refs):
    it = iter(refs)
    order = next(it)
    wo = next(it)
    q, k_, v, seg_row, seg_col = (next(it) for _ in range(5))
    ctx_o, lse_o = next(it), next(it)
    outs = [next(it) for _ in range(count)]
    wos, stage, sems = (next(it) for _ in range(3))
    length, width = ctx_o.shape
    heads = width // HD
    starts = piece_rows(order, outs[0].shape[0], count)
    copies = load_outputs(wo, wos, sems, count)
    for copy in copies:
        copy.start()
    scale = HD ** (-0.5)
    for b in range(length // block):
        rows = pl.ds(b * block, block)
        hi = (b + 1) * block
        allowed = allowed_pairs(seg_col, seg_row, b * block, block, hi)
        for h in range(heads):
            cols = slice(h * HD, (h + 1) * HD)
            s = dot_nt(q[rows, cols], k_[pl.ds(0, hi), cols]) * scale
            s = jnp.where(allowed, s, MASKED)
            top = jnp.max(s, axis=-1, keepdims=True)
            e = jnp.exp(s - top)
            total = jnp.sum(e, axis=-1, keepdims=True)
            probs = (e * (1.0 / total)).astype(bf16)
            ctx_o[rows, cols] = dot(probs, v[pl.ds(0, hi), cols]).astype(bf16)
            lse_o[h, rows, :] = top + jnp.log(total)
    for copy in copies:
        copy.wait()
    stage[...] = dot(ctx_o[...], wos[...]).astype(bf16)
    for copy in send_out(stage, outs, sems, 0, starts):
        copy.wait()


def attn_core(order, wo, q, k, v, seg_row, seg_col, own_rows, d):
    n = wo.shape[0]
    length, width = q.shape
    count = length // own_rows + 1
    return pl.pallas_call(
        functools.partial(attn_core_body, count, min(256, length)),
        in_specs=[SMEM] + [ANY] + [VMEM] * 5,
        out_specs=[VMEM] * 2 + [ANY] * count,
        out_shape=[shape((length, width), bf16), shape((width // HD, length, 1), f32)]
        + piece_shapes(own_rows, d, count),
        scratch_shapes=[
            pltpu.VMEM((width, d), bf16),
            pltpu.VMEM((length, d), bf16),
            pltpu.SemaphoreType.DMA((count + output_copies(n, d // n, width),)),
        ],
        compiler_params=pltpu.CompilerParams(vmem_limit_bytes=36 << 20),
        cost_estimate=cost(10),
        name="attn_core",
    )(order, wo, q, k, v, seg_row, seg_col)


def attn_back_body(count, block, *refs):
    it = iter(refs)
    order = next(it)
    pieces = [next(it) for _ in range(count)]
    wo = next(it)
    q, k_, v, lse, seg_row, seg_col = (next(it) for _ in range(6))
    dq_o, dk_o, dv_o, db_o = (next(it) for _ in range(4))
    db, wos, dctx, sems = (next(it) for _ in range(4))
    length, width = q.shape
    heads = width // HD
    starts = piece_rows(order, pieces[0].shape[0], count)
    copies = load_outputs(wo, wos, sems, count)
    for copy in copies:
        copy.start()
    for copy in copies + fetch(pieces, db, sems, 0, starts):
        copy.wait()
    keep = pltpu.make_async_copy(db, db_o, sems.at[0])
    keep.start()
    scale = HD ** (-0.5)
    dctx[...] = dot_nt(db[...], wos[...]).astype(bf16)
    dk_o[...] = jnp.zeros_like(dk_o)
    dv_o[...] = jnp.zeros_like(dv_o)
    for b in range(length // block):
        rows = pl.ds(b * block, block)
        hi = (b + 1) * block
        low = pl.ds(0, hi)
        allowed = allowed_pairs(seg_col, seg_row, b * block, block, hi)
        for h in range(heads):
            cols = slice(h * HD, (h + 1) * HD)
            s = dot_nt(q[rows, cols], k_[low, cols]) * scale
            p = jnp.where(allowed, jnp.exp(s - lse[h, rows, :]), 0.0)
            g = dot_nt(dctx[rows, cols], v[low, cols])
            pg = p * g
            ds = (pg - p * jnp.sum(pg, axis=-1, keepdims=True)).astype(bf16)
            dq_o[rows, cols] = dot(ds, k_[low, cols]) * scale
            dk_o[low, cols] += dot_tn(ds, q[rows, cols]) * scale
            dv_o[low, cols] += dot_tn(p.astype(bf16), dctx[rows, cols])
    keep.wait()


def attn_back(order, pieces, wo, q, k, v, lse, seg_row, seg_col):
    n, count = wo.shape[0], len(pieces)
    d = pieces[0].shape[1]
    length, width = q.shape
    return pl.pallas_call(
        functools.partial(attn_back_body, count, min(256, length)),
        in_specs=[SMEM] + [ANY] * (count + 1) + [VMEM] * 6,
        out_specs=[VMEM] * 3 + [ANY],
        out_shape=[shape((length, width), f32)] * 3 + [shape((length, d), bf16)],
        scratch_shapes=[
            pltpu.VMEM((length, d), bf16),
            pltpu.VMEM((width, d), bf16),
            pltpu.VMEM((length, width), bf16),
            pltpu.SemaphoreType.DMA((count + output_copies(n, d // n, width),)),
        ],
        compiler_params=pltpu.CompilerParams(vmem_limit_bytes=VMEM_BYTES),
        cost_estimate=cost(14),
        name="attn_back",
    )(order, *pieces, wo, q, k, v, lse, seg_row, seg_col)


def proj_back_body(count, block, *refs):
    it = iter(refs)
    order = next(it)
    wq = next(it)
    qr, kr, dq, dk, dv = (next(it) for _ in range(5))
    gains, cosine, sine, x = (next(it) for _ in range(4))
    dp_o, hg_o, gs_o = (next(it) for _ in range(3))
    outs = [next(it) for _ in range(count)]
    wqs, stage, sems = (next(it) for _ in range(3))
    length, width = qr.shape
    heads = width // HD
    starts = piece_rows(order, outs[0].shape[0], count)
    copies = load_projections(wq, wqs, sems, count)
    for copy in copies:
        copy.start()
    hg_o[...] = jnp.zeros_like(hg_o)
    gs_o[...] = jnp.zeros_like(gs_o)
    for copy in copies:
        copy.wait()

    def finish(r, _):
        rows = pl.ds(pl.multiple_of(r * block, block), block)
        dp_o[rows, 2 * width :] = dv[rows, :].astype(bf16)
        for j, (raw, grad) in enumerate(((qr, dq), (kr, dk))):
            for h in range(heads):
                cols = slice(h * HD, (h + 1) * HD)
                u = raw[rows, cols]
                inv = lax.rsqrt(jnp.mean(u * u, axis=-1, keepdims=True) + EPSILON)
                hat = u * inv
                t = grad[rows, cols]
                t = t * cosine[rows, :] - pltpu.roll(t, HD // 2, 1) * sine[rows, :]
                hg_o[j : j + 1, cols] += jnp.sum(t * hat, axis=0, keepdims=True)
                w = t * gains[j : j + 1, cols]
                w = inv * (w - hat * jnp.mean(w * hat, axis=-1, keepdims=True))
                dp_o[rows, j * width + h * HD : j * width + (h + 1) * HD] = w.astype(bf16)
        out = dot_nt(dp_o[rows, :], wqs[...])
        gs_o[...] += jnp.sum(out * x[rows, :].astype(f32), axis=0, keepdims=True)
        stage[rows, :] = out.astype(bf16)
        return 0

    lax.fori_loop(0, length // block, finish, 0)
    for copy in send_out(stage, outs, sems, 0, starts):
        copy.wait()


def proj_back(order, wq, qr, kr, dq, dk, dv, gains, cosine, sine, x, own_rows):
    n = wq.shape[0]
    length, width = qr.shape
    d = x.shape[1]
    count = length // own_rows + 1
    return pl.pallas_call(
        functools.partial(proj_back_body, count, min(256, length)),
        in_specs=[SMEM] + [ANY] + [VMEM] * 9,
        out_specs=[VMEM] * 3 + [ANY] * count,
        out_shape=[
            shape((length, 3 * width), bf16),
            shape((2, width), f32),
            shape((1, d), f32),
        ]
        + piece_shapes(own_rows, d, count),
        scratch_shapes=[
            pltpu.VMEM((d, 3 * width), bf16),
            pltpu.VMEM((length, d), bf16),
            pltpu.SemaphoreType.DMA((count + 3 * n,)),
        ],
        compiler_params=pltpu.CompilerParams(vmem_limit_bytes=36 << 20),
        cost_estimate=cost(12),
        name="proj_back",
    )(order, wq, qr, kr, dq, dk, dv, gains, cosine, sine, x)


def attn_grad_body(places, xa, xb, dp, ctx, da, db, qkv_keep, qkv_send, out_keep, out_send):
    width = ctx.shape[1]
    for x, d, qkv_o, out_o in ((xa, da, qkv_keep, out_keep), (xb, db, qkv_send, out_send)):
        grad = dot_tn(x[...], dp[...])
        for j in range(3):
            qkv_o[0, j] = grad[:, j * width : (j + 1) * width].astype(bf16)
        out_o[0] = dot_tn(ctx[...], d[...]).astype(bf16)


def attn_grad(places, x, dp, ctx, db, n):
    length, d = x.shape
    width = ctx.shape[1]
    depth = d // n
    even = pl.BlockSpec((length, depth), lambda m, at: (0, at[2 * m]))
    odd = pl.BlockSpec((length, depth), lambda m, at: (0, at[2 * m + 1]))
    return pl.pallas_call(
        attn_grad_body,
        grid_spec=pltpu.PrefetchScalarGridSpec(
            num_scalar_prefetch=1,
            grid=(n // 2,),
            in_specs=[
                even,
                odd,
                pl.BlockSpec((length, 3 * width), lambda m, at: (0, 0)),
                pl.BlockSpec((length, width), lambda m, at: (0, 0)),
                even,
                odd,
            ],
            out_specs=[pl.BlockSpec((1, 3, depth, width), lambda m, at: (m, 0, 0, 0))] * 2
            + [pl.BlockSpec((1, width, depth), lambda m, at: (m, 0, 0))] * 2,
        ),
        out_shape=[shape((n // 2, 3, depth, width), bf16)] * 2
        + [shape((n // 2, width, depth), bf16)] * 2,
        compiler_params=pltpu.CompilerParams(vmem_limit_bytes=VMEM_BYTES),
        cost_estimate=cost(6),
        name="attn_grad",
    )(places, x, x, dp, ctx, db, db)


def flat_rows(pieces):
    starts, at = [], 0
    for piece in pieces:
        starts.append(at)
        at += piece.shape[0]
    return starts


def moe_in_body(count, *refs):
    xp, gu, out, xs, sems = refs[:count], *refs[count:]

    @pl.when(pl.program_id(0) == 0)
    def _():
        for copy in fetch(xp, xs, sems, 0, flat_rows(xp)):
            copy.wait()

    out[...] = dot(xs[...], gu[...]).astype(bf16)


def moe_in(xp, gate_up, group=4):
    count = len(xp)
    d, columns = gate_up.shape
    rows = sum(p.shape[0] for p in xp)
    wide = 2 * group * LANES
    return pl.pallas_call(
        functools.partial(moe_in_body, count),
        grid=(columns // wide,),
        in_specs=[ANY] * count + [pl.BlockSpec((d, wide), lambda s: (0, s))],
        out_specs=pl.BlockSpec((rows, wide), lambda s: (0, s)),
        out_shape=shape((rows, columns), bf16),
        scratch_shapes=[pltpu.VMEM((rows, d), bf16), pltpu.SemaphoreType.DMA((count,))],
        compiler_params=pltpu.CompilerParams(vmem_limit_bytes=VMEM_BYTES),
        cost_estimate=cost(rows * 0.02 + 4),
        name="moe_in",
    )(*xp, gate_up)


def moe_mid_body(group, steps, sets, count, *refs):
    it = iter(refs)
    gates = next(it)
    cp = [next(it) for _ in range(count)]
    gus = [next(it) for _ in range(sets)]
    gu_w, dn_w = next(it), next(it)
    d_outs = [next(it) for _ in range(count)]
    m_outs = [next(it) for _ in range(count)]
    dgu_o, hw_o = next(it), next(it)
    cs, d_acc, m_acc, gg, stage, sems = (next(it) for _ in range(6))
    d = cs.shape[1]
    fw = LANES
    step = pl.program_id(0)

    @pl.when(step == 0)
    def _():
        copies = fetch(cp, cs, sems, 0, flat_rows(cp))
        d_acc[...] = jnp.zeros_like(d_acc)
        m_acc[...] = jnp.zeros_like(m_acc)
        gg[...] = jnp.zeros_like(gg)
        for copy in copies:
            copy.wait()

    d_hid = dot_nt(cs[...], dn_w[...])
    at = 0
    for gu in gus:
        rows = gu.shape[0]
        here = pl.ds(at, rows)
        table = gates[here, :].astype(f32)
        lane = lax.broadcasted_iota(jnp.int32, table.shape, 1)
        total = jnp.zeros(table.shape, f32)
        for i in range(group):
            g = gu[:, 2 * i * fw : (2 * i + 1) * fw].astype(f32)
            u = gu[:, (2 * i + 1) * fw : (2 * i + 2) * fw].astype(f32)
            dh = d_hid[at : at + rows, i * fw : (i + 1) * fw]
            z = jax.nn.sigmoid(g)
            swish = g * z
            h = swish * u
            expert = step * group + i
            own = jnp.sum(h * dh, axis=1, keepdims=True)
            total = total + jnp.where(lane == expert, own, 0.0)
            gate = jnp.sum(jnp.where(lane == expert, table, 0.0), axis=1, keepdims=True)
            dw = dh * gate
            d_g = dw * u * z * (1.0 + g * (1.0 - z))
            hw_o[here, i * fw : (i + 1) * fw] = (h * gate).astype(bf16)
            dgu_o[here, 2 * i * fw : (2 * i + 1) * fw] = d_g.astype(bf16)
            dgu_o[here, (2 * i + 1) * fw : (2 * i + 2) * fw] = (dw * swish).astype(bf16)
        gg[here, :] += total
        at += rows
    d_acc[...] += dot_nt(dgu_o[...], gu_w[...])
    m_acc[...] += dot(hw_o[...], dn_w[...])

    @pl.when(step == steps - 1)
    def _():
        stage[:, pl.ds(0, d)] = d_acc[...].astype(bf16)
        stage[:, pl.ds(d, LANES)] = gg[...].astype(bf16)
        copies = send_out(stage, d_outs, sems, 0, flat_rows(d_outs))
        cs[...] = m_acc[...].astype(bf16)
        copies = copies + send_out(cs, m_outs, sems, count, flat_rows(m_outs))
        for copy in copies:
            copy.wait()


def moe_mid(gates, cp, gus, gate_up, down, group=4):
    count = len(cp)
    hidden, d = down.shape
    rows = sum(p.shape[0] for p in cp)
    half = group * LANES
    steps = hidden // half
    return pl.pallas_call(
        functools.partial(moe_mid_body, group, steps, len(gus), count),
        grid=(steps,),
        in_specs=[pl.BlockSpec((rows, LANES), lambda s: (0, 0))]
        + [ANY] * count
        + [pl.BlockSpec((g.shape[0], 2 * half), lambda s: (0, s)) for g in gus]
        + [
            pl.BlockSpec((d, 2 * half), lambda s: (0, s)),
            pl.BlockSpec((half, d), lambda s: (s, 0)),
        ],
        out_specs=[ANY] * (2 * count)
        + [
            pl.BlockSpec((rows, 2 * half), lambda s: (0, s)),
            pl.BlockSpec((rows, half), lambda s: (0, s)),
        ],
        out_shape=[shape((p.shape[0], d + LANES), bf16) for p in cp]
        + [shape(p.shape, bf16) for p in cp]
        + [shape((rows, 2 * hidden), bf16), shape((rows, hidden), bf16)],
        scratch_shapes=[
            pltpu.VMEM((rows, d), bf16),
            pltpu.VMEM((rows, d), f32),
            pltpu.VMEM((rows, d), f32),
            pltpu.VMEM((rows, LANES), f32),
            pltpu.VMEM((rows, d + LANES), bf16),
            pltpu.SemaphoreType.DMA((2 * count,)),
        ],
        compiler_params=pltpu.CompilerParams(vmem_limit_bytes=VMEM_BYTES),
        cost_estimate=cost(rows * 0.04 + 6),
        name="moe_mid",
    )(gates, *cp, *gus, gate_up, down)


def turn_body(count, *refs):
    pieces, out, xs, sems = refs[:count], refs[count], refs[count + 1], refs[count + 2]
    for copy in fetch(pieces, xs, sems, 0, flat_rows(pieces)):
        copy.wait()
    d = xs.shape[1]
    size = 256
    eye = (
        lax.broadcasted_iota(jnp.int32, (size, size), 0)
        == lax.broadcasted_iota(jnp.int32, (size, size), 1)
    ).astype(bf16)
    for at in range(0, d, size):
        out[pl.ds(at, size), :] = dot_nt(eye, xs[:, pl.ds(at, size)]).astype(bf16)


def turn_rows(pieces):
    count = len(pieces)
    length = sum(p.shape[0] for p in pieces)
    d = pieces[0].shape[1]
    return pl.pallas_call(
        functools.partial(turn_body, count),
        in_specs=[ANY] * count,
        out_specs=VMEM,
        out_shape=shape((d, length), bf16),
        scratch_shapes=[pltpu.VMEM((length, d), bf16), pltpu.SemaphoreType.DMA((count,))],
        compiler_params=pltpu.CompilerParams(vmem_limit_bytes=VMEM_BYTES),
        cost_estimate=cost(4),
        name="turn_rows",
    )(*pieces)


def in_grad_body(n, group, sets, places, xt, *refs):
    dgus = refs[:sets]
    *outs, xs, sems = refs[-4:]
    depth, fw = outs[0].shape[3:]
    step = pl.program_id(0)

    def part(k):
        source = xt.at[pl.ds(pl.multiple_of(places[k] * depth, depth), depth)]
        return pltpu.make_async_copy(source, xs.at[pl.ds(k * depth, depth)], sems.at[k])

    @pl.when(step == 0)
    def _():
        for k in range(n):
            part(k).start()

    dgu = jnp.concatenate([ref[...] for ref in dgus], axis=0)
    for k in range(n):

        @pl.when(step == 0)
        def _(k=k):
            part(k).wait()

        grad = dot(xs[pl.ds(k * depth, depth), :], dgu)
        for i in range(group):
            for g in range(2):
                at = (2 * i + g) * fw
                outs[k % 2][k // 2, i, g] = grad[:, at : at + fw].astype(bf16)


def in_grad(places, xt, dgus, n, experts, first, number, held, whole=None, group=2):
    d, length = xt.shape
    depth = d // n
    fw = dgus[0].shape[1] // (2 * experts)
    start = first // group
    at = (first % held) // group
    before = [] if whole is None else list(whole)
    sets = len(dgus)
    return list(
        pl.pallas_call(
            functools.partial(in_grad_body, n, group, sets),
            grid=(number // group,),
            in_specs=[SMEM, ANY]
            + [pl.BlockSpec((a.shape[0], 2 * group * fw), lambda s: (0, s + start)) for a in dgus]
            + [ANY] * len(before),
            out_specs=[pl.BlockSpec((n // 2, group, 2, depth, fw), lambda s: (0, at + s, 0, 0, 0))]
            * 2,
            out_shape=[shape((n // 2, held, 2, depth, fw), bf16)] * 2,
            input_output_aliases={2 + sets: 0, 3 + sets: 1} if before else {},
            scratch_shapes=[pltpu.VMEM((d, length), bf16), pltpu.SemaphoreType.DMA((n,))],
            compiler_params=pltpu.CompilerParams(vmem_limit_bytes=VMEM_BYTES),
            cost_estimate=cost(1.5 * number + 3),
            name="in_grad",
        )(places, xt, *dgus, *before)
    )


def out_grad_body(group, count, sets, *refs):
    hws, pieces = refs[:sets], refs[sets : sets + count]
    out, cs, sems = refs[-3:]
    fw = out.shape[1]

    @pl.when(pl.program_id(0) == 0)
    def _():
        for copy in fetch(pieces, cs, sems, 0, flat_rows(pieces)):
            copy.wait()

    turned = jnp.concatenate([ref[...] for ref in hws], axis=0).T
    grad = dot(turned, cs[...])
    for i in range(group):
        out[i] = grad[i * fw : (i + 1) * fw].astype(bf16)


def out_grad(hws, cp, experts, part, whole=None, group=2):
    count = len(cp)
    length = sum(h.shape[0] for h in hws)
    d = cp[0].shape[1]
    fw = hws[0].shape[1] // experts
    steps = experts // (2 * group)
    at = part * steps
    before = [] if whole is None else [whole]
    return pl.pallas_call(
        functools.partial(out_grad_body, group, count, len(hws)),
        grid=(steps,),
        in_specs=[pl.BlockSpec((h.shape[0], group * fw), lambda s: (0, at + s)) for h in hws]
        + [ANY] * (count + len(before)),
        out_specs=pl.BlockSpec((group, fw, d), lambda s: (at + s, 0, 0)),
        out_shape=shape((experts, fw, d), bf16),
        input_output_aliases={len(hws) + count: 0} if before else {},
        scratch_shapes=[pltpu.VMEM((length, d), bf16), pltpu.SemaphoreType.DMA((count,))],
        compiler_params=pltpu.CompilerParams(vmem_limit_bytes=VMEM_BYTES),
        cost_estimate=cost(9),
        name="out_grad",
    )(*hws, *cp, *before)


def finish_body(*refs):
    keep, got, more, out = refs[-4:]
    out[...] = keep[0].astype(f32) + got[0].astype(f32) + more[0].astype(f32)


def finish(whole, terms, experts, first):
    number = terms[0].shape[1]
    rest = terms[0].shape[2:]
    zeros = (0,) * len(rest)
    before = [] if whole is None else [whole]
    each = 2
    at = first // each
    return pl.pallas_call(
        finish_body,
        grid=(number // each,),
        in_specs=[ANY] * len(before)
        + [pl.BlockSpec((1, each) + rest, lambda s: (0, s) + zeros)] * 3,
        out_specs=pl.BlockSpec((each,) + rest, lambda s: (at + s,) + zeros),
        out_shape=shape((experts,) + rest, f32),
        input_output_aliases={0: 0} if before else {},
        compiler_params=pltpu.CompilerParams(vmem_limit_bytes=VMEM_BYTES),
        cost_estimate=cost(2),
        name="finish",
    )(*before, *terms)


def place_body(*refs):
    part, out = refs[-2:]
    out[...] = part[...].astype(f32)


def place(part, experts, whole=None):
    rest = part.shape[1:]
    zeros = (0,) * len(rest)
    before = [] if whole is None else [whole]
    return pl.pallas_call(
        place_body,
        grid=(part.shape[0] // 2,),
        in_specs=[ANY] * len(before) + [pl.BlockSpec((2,) + rest, lambda s: (s,) + zeros)],
        out_specs=pl.BlockSpec((2,) + rest, lambda s: (s,) + zeros),
        out_shape=shape((experts,) + rest, f32),
        input_output_aliases={0: 0} if before else {},
        compiler_params=pltpu.CompilerParams(vmem_limit_bytes=VMEM_BYTES),
        cost_estimate=cost(3),
        name="place",
    )(*before, part)


def pack_body(w, out):
    fw = w.shape[3]
    for i in range(w.shape[0]):
        for g in range(2):
            at = (2 * i + g) * fw
            out[:, at : at + fw] = w[i, g]


def pack(gate_up, group=4):
    experts, _, depth, fw = gate_up.shape
    return pl.pallas_call(
        pack_body,
        grid=(experts // group,),
        in_specs=[pl.BlockSpec((group, 2, depth, fw), lambda s: (s, 0, 0, 0))],
        out_specs=pl.BlockSpec((depth, 2 * group * fw), lambda s: (0, s)),
        out_shape=shape((depth, 2 * experts * fw), bf16),
        compiler_params=pltpu.CompilerParams(vmem_limit_bytes=VMEM_BYTES),
        cost_estimate=cost(4),
        name="pack",
    )(gate_up)


def rope_tables(length):
    positions = np.arange(length, dtype=np.float32)
    power = -np.arange(HD // 2, dtype=np.float32) * np.float32(2.0) / np.float32(HD)
    inverse_freq = np.power(np.float32(ROPE_BASE), power)
    phases = positions[:, None] * inverse_freq[None, :]
    cosine, sine = np.cos(phases), np.sin(phases)
    tables = [cosine, cosine], [-sine, sine]
    return [np.concatenate(t, axis=-1).astype(np.float32) for t in tables]


def per_device(
    tokens,
    segments,
    routes,
    gate_values,
    cotangent,
    query_key_value,
    out_weight,
    head_gain,
    layer_gain,
    gate_up,
    down_weight,
):
    groups = lax.axis_size("tensor")
    n = lax.axis_size("dp")
    own_rows, d = tokens.shape
    seq_len = own_rows * groups
    heads = query_key_value.shape[2] // HD
    experts = gate_up.shape[0]
    depth = d // n
    steps = groups // 2
    top = routes.shape[1]

    x = tokens.astype(f32)
    routed = jnp.concatenate([routes.astype(bf16), gate_values], axis=1)
    routed = jnp.pad(routed, ((0, 0), (0, LANES - 2 * top)))
    normed = Gather(jnp.concatenate([tokens, routed], axis=1), groups)
    first = normed.step()

    width = query_key_value.shape[2]
    small = jnp.concatenate([layer_gain.reshape(-1), head_gain.reshape(-1)])
    size = small.shape[0]
    small = jnp.pad(small, (0, -size % (16 * width))).reshape(-1, width)
    outward = split_last(out_weight, max(1, depth // width))
    outward = [jnp.pad(a, ((0, 0), (0, width - a.shape[1]))) for a in outward]
    own = [query_key_value.reshape(-1, width)] + outward + [small]
    attn_weights = lax.all_gather(jnp.concatenate(own, axis=0), "dp", axis=0)

    ring = ring_of(groups)
    orders = [[ring[(ring.index(t) + k) % groups] for k in distances_of(groups)] for t in range(groups)]
    orders = jnp.array(orders, jnp.int32)
    order = lax.dynamic_slice(orders, (lax.axis_index("tensor"), 0), (1, groups)).reshape(groups)
    places = jnp.array([[i ^ k for k in range(n)] for i in range(n)], jnp.int32)
    places = lax.dynamic_slice(places, (lax.axis_index("dp"), 0), (1, n)).reshape(n)
    cosine, sine = rope_tables(seq_len)
    seg_row = segments.reshape(1, seq_len)
    seg_col = segments.reshape(seq_len, 1)
    expert_ids = jnp.arange(experts, dtype=jnp.int32)
    chosen = routes[:, :, None] == expert_ids
    (gate_up,) = tie((gate_up,), first)
    packed = pack(gate_up)

    done = normed.step()
    (packed,) = tie((packed,), done)
    gu = lax.all_gather(packed, "dp", axis=0, tiled=True)
    normed.step(after=[packed])
    normed.step()
    cut = 2 * depth
    small = [w[-small.shape[0] :].reshape(-1)[:size] for w in attn_weights]
    gain = jnp.concatenate([s[:cut].reshape(2, depth) for s in small], axis=1).astype(f32)
    gain_in, gain_mid = gain[0], gain[1]
    head_parts = [s[cut:].reshape(2, heads, HD // n) for s in small]
    gain_head = jnp.concatenate(head_parts, axis=2).reshape(2, heads * HD).astype(f32)
    pieces = normed.pieces()
    inv_in = lax.rsqrt(jnp.mean(x * x, axis=-1, keepdims=True) + EPSILON)
    x_hat = x * inv_in
    q, k, v, q_raw, k_raw, normed_all = attn_proj(
        order, pieces, attn_weights, gain_in[None, :], gain_head, cosine, sine
    )
    d_pieces = Gather(cotangent, groups)
    first = d_pieces.step(after=pieces)
    q, k, v = tie((q, k, v), first)
    context, lse, *attn = attn_core(
        order, attn_weights, q, k, v, seg_row, seg_col, own_rows, d
    )
    second = d_pieces.step(after=[q])
    routed = jnp.concatenate([p[:, d : d + 2 * top] for p in pieces], axis=0)
    named = routed[:, :top].astype(jnp.int32)[:, :, None] == expert_ids
    gate_table = jnp.sum(jnp.where(named, routed[:, top:].astype(f32)[:, :, None], 0.0), axis=1)
    gate_table = jnp.pad(gate_table.astype(bf16), ((0, 0), (0, LANES - experts)))
    attention = Scatter(attn, groups)
    done = attention.step(after=second)
    (down,) = tie((down_weight.reshape(-1, depth),), done)
    dn = lax.all_gather(down, "dp", axis=1, tiled=True)
    middle = x + attention.run().result()
    inv_mid = lax.rsqrt(jnp.mean(middle * middle, axis=-1, keepdims=True) + EPSILON)
    mid_hat = middle * inv_mid
    mid = Gather((mid_hat * gain_mid).astype(bf16), groups)

    hidden_in = []
    mid.step()
    for s in range(1, steps - 1):
        here = [mid.at(s), mid.at(-s)] + ([mid.at(0)] if s == 1 else [])
        mid.step(after=hidden_in[-1:])
        hidden_in.append(moe_in(here, gu))
    mid.step(after=hidden_in[-1:])
    normed_mid = mid.pieces()
    taken = normed_mid[:4]
    hidden_in.append(moe_in(taken, gu))
    d_pieces.step(after=taken)
    d_pieces.step(after=hidden_in[-1:])
    d_pieces = d_pieces.pieces()

    half_rows = hidden_in[-1].shape[0]
    d_far, d_near = d_pieces[:4], d_pieces[4:]
    far_out = list(moe_mid(gate_table[:half_rows], d_far, hidden_in[-1:], gu, dn))
    d_mid, moe, d_in, hidden = far_out[:4], far_out[4:8], far_out[8:9], far_out[9:]
    (mid_far,) = tie(normed_mid[:1], d_mid[:1])
    mid_turned = turn_rows([mid_far] + normed_mid[1:])
    d_normed = Scatter(d_mid, groups)
    done = d_normed.step()
    mixing = Scatter(moe, groups)
    second = d_normed.step(after=[mid_turned], riders=mixing.far)
    mixing.done, mixing.moved = 1, [m[:, :d] for m in d_normed.ridden]
    (table,) = tie((gate_table[half_rows:],), done + [mid_turned])
    near_out = list(moe_mid(table, d_near, hidden_in[:-1][::-1], gu, dn))
    count = len(d_near)
    d_mid, moe = d_mid + near_out[:count], moe + near_out[count : 2 * count]
    d_in, hidden = d_in + near_out[2 * count : -1], hidden + near_out[-1:]
    d_normed.block = dict(zip(distances_of(groups)[1:], d_mid[2:]))
    mixing.block = dict(zip(distances_of(groups)[1:], moe[2:]))
    third = d_normed.step(after=moe[-1:])

    (hidden_far,) = tie(hidden[:1], second + near_out[:1])
    dn_half = out_grad([hidden_far] + hidden[1:], d_pieces, experts, 0)
    dn_all = out_grad(hidden, d_pieces, experts, 1, dn_half)
    (ready,) = tie((dn_all,), third)
    dn_grad = lax.psum_scatter(ready, "dp", scatter_dimension=2, tiled=True)
    fourth = d_normed.step(after=[dn_all])

    def gradient(c, after, whole=None):
        (turned,) = tie((mid_turned,), after)
        return in_grad(places, turned, d_in, n, experts, c * each, each, 2 * each, whole)

    each = experts // CHUNKS
    low = gradient(0, third)
    d_normed_mid = d_normed.result()
    gate_sum = d_normed_mid[:, d:]
    d_normed_mid = d_normed_mid[:, :d]
    d_mid_hat = d_normed_mid * gain_mid
    d_middle = cotangent.astype(f32) + inv_mid * (
        d_mid_hat - mid_hat * jnp.mean(d_mid_hat * mid_hat, axis=-1, keepdims=True)
    )
    branch = Gather(d_middle.astype(bf16), groups)
    moved = branch.step(after=low)
    low = gradient(1, [d_middle], low)
    moved_on = branch.step(after=low)
    low_keep, low_send = low[0], tie(low[1:], moved)[0]
    low_terms = flip_reduce(low_keep, low_send, "dp", n)
    high = gradient(2, moved)
    moved = branch.step(after=high + low_terms[3:])
    high = gradient(3, moved_on, high)
    branch.step(after=high)
    high_keep, high_send = high[0], tie(high[1:], moved)[0]
    high_terms = flip_reduce(high_keep, high_send, "dp", n)
    d_branch = branch.pieces()

    moe_second = mixing.step(after=d_branch + high_terms[3:])
    dq, dk, dv, d_branch_all = attn_back(
        order, d_branch, attn_weights, q, k, v, lse, seg_row, seg_col
    )
    dq, dk, dv = tie((dq, dk, dv), moe_second)
    moe_third = mixing.step(after=low_terms[2:3])
    d_projected, head_part, in_part, *to_rows = proj_back(
        order, attn_weights, q_raw, k_raw, dq, dk, dv, gain_head, cosine, sine, normed_all, own_rows
    )
    d_normed = Scatter(to_rows, groups)
    late = [d_normed.step(after=moe_third)]
    (dn_grad,) = tie((dn_grad,), to_rows[:1])
    dn_grad = place(dn_grad, experts)
    late.append(d_normed.step(after=[dn_grad]))
    (projected,) = tie((d_projected,), late[0])
    qkv_keep, qkv_send, out_keep, out_send = attn_grad(
        places, normed_all, projected, context, d_branch_all, n
    )
    late.append(d_normed.step(after=[qkv_keep]))
    qkv_send, out_send = tie((qkv_send, out_send), late[1])
    qkv_terms = flip_reduce(qkv_keep, qkv_send, "dp", n)
    out_terms = flip_reduce(out_keep, out_send, "dp", n)

    (late_low,) = tie(low_terms[2:3], late[1])
    gu_grad = finish(None, low_terms[:2] + [late_low], experts, 0)
    late.append(
        d_normed.step(after=qkv_terms[3:] + out_terms[3:] + [gu_grad] + high_terms[2:3])
    )
    (late_high,) = tie(high_terms[2:3], late[2])
    gu_grad = finish(gu_grad, high_terms[:2] + [late_high], experts, 2 * each)
    late.append(mixing.step(after=late[3] + qkv_terms[2:3]))
    d_normed_in = d_normed.result()
    d_x_hat = d_normed_in * gain_in
    input_grad = d_middle + inv_in * (
        d_x_hat - x_hat * jnp.mean(d_x_hat * x_hat, axis=-1, keepdims=True)
    )
    mixed = (middle + mixing.result()).astype(bf16)
    gate_grad = jnp.sum(jnp.where(chosen, gate_sum[:, None, :experts], 0.0), axis=-1)
    out_terms = out_terms[:2] + list(tie(out_terms[2:3], late[4]))
    qkv_grad = sum(t[0].astype(f32) for t in qkv_terms[:3])
    out_weight_grad = sum(t[0].astype(f32) for t in out_terms[:3])

    mid_part = jnp.sum(d_normed_mid * mid_hat, axis=0)
    (in_part,) = tie((in_part,), late[3])
    layer_part = jnp.stack([in_part[0] / gain_in, mid_part]).reshape(2, n, groups, -1)
    layer_part = jnp.stack(relative([layer_part[:, :, t] for t in range(groups)], "tensor"))
    for bit in bits_of(groups):
        pairs = layer_part.reshape((layer_part.shape[0] // 2, 2) + layer_part.shape[1:])
        layer_part = pairs[:, 0] + flip_step(pairs[:, 1], "tensor", groups, bit)
    head_parts = split_last(head_part.reshape(2, heads, HD), n)
    rows = [
        jnp.concatenate([layer_part[0, :, k].reshape(-1), h.reshape(-1)])
        for k, h in enumerate(head_parts)
    ]
    rows = tie((jnp.stack(relative(rows, "dp")),), out_terms[2:])[0]
    summed = flip_reduce_rows(rows, "dp", n)
    cut = 2 * (depth // groups)
    layer_grad = summed[:cut].reshape(2, depth // groups)
    head_grad = summed[cut:].reshape(2, heads, HD // n)

    return (
        mixed,
        input_grad,
        gate_grad,
        qkv_grad,
        out_weight_grad,
        head_grad,
        layer_grad,
        gu_grad,
        dn_grad,
    )


def solution(mesh):
    return jax.shard_map(
        per_device,
        mesh=mesh,
        in_specs=(
            P(("dp", "tensor"), None),
            P("dp", None),
            P(("dp", "tensor"), None),
            P(("dp", "tensor"), None),
            P(("dp", "tensor"), None),
            P(None, "dp", "tensor"),
            P("tensor", "dp"),
            P(None, "tensor", "dp"),
            P(None, "dp"),
            P(None, None, "dp", "tensor"),
            P(None, "tensor", "dp"),
        ),
        out_specs=(
            P(("dp", "tensor"), None),
            P(("dp", "tensor"), None),
            P(("dp", "tensor"), None),
            P(None, "dp", "tensor"),
            P("tensor", "dp"),
            P(None, "tensor", "dp"),
            P(None, ("dp", "tensor")),
            P(None, None, "dp", "tensor"),
            P(None, "tensor", "dp"),
        ),
        check_vma=False,
    )
```

```python
import functools

import jax
import jax.numpy as jnp
import numpy as np
from jax import lax
from jax.experimental import pallas as pl
from jax.experimental.pallas import tpu as pltpu
from jax.sharding import PartitionSpec as P

HD = 128
E = 16
EPSILON = 1e-05
ROPE_BASE = 10000.0
MASKED = -1e30
LANES = 128
CHUNKS = 4
VMEM_BYTES = 60 << 20

f32 = jnp.float32
bf16 = jnp.bfloat16
NT = (((1,), (1,)), ((), ()))
TN = (((0,), (0,)), ((), ()))
ANY = pl.BlockSpec(memory_space=pl.ANY)
SMEM = pl.BlockSpec(memory_space=pltpu.SMEM)
VMEM = pl.BlockSpec(memory_space=pltpu.VMEM)


def dot(a, b):
    return jnp.dot(a, b, preferred_element_type=f32)


def dot_nt(a, b):
    return lax.dot_general(a, b, NT, preferred_element_type=f32)


def dot_tn(a, b):
    return lax.dot_general(a, b, TN, preferred_element_type=f32)


def shape(dims, dtype):
    return jax.ShapeDtypeStruct(dims, dtype)


def ring_of(groups):
    return list(range(0, groups, 2)) + list(range(groups - 1, 0, -2))


def distances_of(groups):
    steps = groups // 2
    near = [s * k for k in range(steps - 1, 0, -1) for s in (1, -1)]
    return [steps] + near + [0]


def ring_step(value, groups, sign):
    ring = ring_of(groups)
    pairs = [(ring[p], ring[(p + sign) % groups]) for p in range(groups)]
    return lax.ppermute(value, "tensor", pairs)


def tie(values, after):
    values, after = tuple(values), tuple(after)
    return lax.optimization_barrier(values + after)[: len(values)]


class Gather:
    def __init__(self, own, groups):
        self.groups, self.steps = groups, groups // 2
        self.below, self.above = [own], [own]

    def step(self, after=()):
        low, high = self.below[-1], self.above[-1]
        if len(self.below) == self.steps:
            half = low.shape[0] // 2
            low, high = low[:half], high[half:]
        if after:
            low, high = tie((low, high), after)
        self.below.append(ring_step(low, self.groups, 1))
        self.above.append(ring_step(high, self.groups, -1))
        return [self.below[-1], self.above[-1]]

    def run(self):
        while len(self.below) <= self.steps:
            self.step()
        return self

    def at(self, distance):
        return self.above[distance] if distance >= 0 else self.below[-distance]

    def far(self):
        return [self.below[self.steps], self.above[self.steps]]

    def pieces(self):
        return self.far() + [self.at(k) for k in distances_of(self.groups)[1:]]


class Scatter:
    def __init__(self, pieces, groups):
        self.groups, self.steps, self.done = groups, groups // 2, 0
        self.far = pieces[:2]
        self.block = dict(zip(distances_of(groups)[1:], pieces[2:]))

    def step(self, after=(), riders=None):
        if self.done == 0:
            sent = self.far
        else:
            distance = self.steps - self.done
            low, high = (v.astype(f32) for v in self.moved)
            if self.done == 1:
                half = low.shape[0]
                low = jnp.pad(low, ((0, half), (0, 0)))
                high = jnp.pad(high, ((half, 0), (0, 0)))
            dtype = self.far[0].dtype
            low = (self.block[distance].astype(f32) + low).astype(dtype)
            high = (self.block[-distance].astype(f32) + high).astype(dtype)
            sent = [low, high]
        rows, columns = sent[0].shape
        if riders:
            riders = [jnp.pad(r, ((0, 0), (0, columns - r.shape[1]))) for r in riders]
            sent = [jnp.concatenate(pair, axis=0) for pair in zip(sent, riders)]
        if after:
            sent = tie(sent, after)
        self.moved = [ring_step(sent[0], self.groups, 1), ring_step(sent[1], self.groups, -1)]
        self.done += 1
        if riders:
            self.ridden = [m[rows:] for m in self.moved]
            self.moved = [m[:rows] for m in self.moved]
        return self.moved

    def run(self):
        while self.done < self.steps:
            self.step()
        return self

    def result(self):
        low, high = self.moved
        return self.block[0].astype(f32) + low.astype(f32) + high.astype(f32)


def bits_of(count):
    return [1 << b for b in range(count.bit_length() - 1)]


def flip_step(value, axis, count, bit):
    return lax.ppermute(value, axis, [(s, s ^ bit) for s in range(count)])


def relative(parts, axis):
    count = len(parts)
    index = lax.axis_index(axis)
    for bit in bits_of(count):
        turned = (index & bit) != 0
        parts = [jnp.where(turned, parts[k ^ bit], parts[k]) for k in range(count)]
    return parts


def split_last(value, count):
    width = value.shape[-1] // count
    return [value[..., k * width : (k + 1) * width] for k in range(count)]


def flip_reduce(keep, sent, axis, count):
    return flip_rest(keep, flip_step(sent, axis, count, 1), axis, count)


def flip_rest(keep, got, axis, count):
    for bit in bits_of(count)[1:]:
        odd = (keep[1::2].astype(f32) + got[1::2].astype(f32)).astype(bf16)
        more = flip_step(odd, axis, count, bit)
        if 2 * bit < count:
            keep = (keep[0::2].astype(f32) + got[0::2].astype(f32)).astype(bf16)
            got = more
    return [keep, got, more, odd]


def flip_reduce_rows(value, axis, count):
    for bit in bits_of(count):
        pairs = value.reshape((value.shape[0] // 2, 2) + value.shape[1:])
        value = pairs[:, 0] + flip_step(pairs[:, 1], axis, count, bit)
    return value[0]


def fetch(sources, target, sems, first, rows_at):
    copies = []
    for number, source in enumerate(sources):
        if source.shape[1] > target.shape[1]:
            source = source.at[:, pl.ds(0, target.shape[1])]
        copy = pltpu.make_async_copy(
            source, target.at[pl.ds(rows_at[number], source.shape[0])], sems.at[first + number]
        )
        copy.start()
        copies.append(copy)
    return copies


def load_projections(weights, wqs, sems, first):
    copies = []
    n, _, width = weights.shape
    depth = wqs.shape[0] // n
    for k in range(n):
        for j in range(3):
            source = weights.at[k, pl.ds(j * depth, depth)]
            target = wqs.at[pl.ds(k * depth, depth), pl.ds(j * width, width)]
            copies.append(pltpu.make_async_copy(source, target, sems.at[first + 3 * k + j]))
    return copies


def load_outputs(weights, wos, sems, first):
    copies = []
    n, _, width = weights.shape
    depth = wos.shape[1] // n
    cuts = max(1, depth // width)
    columns = depth // cuts
    for k in range(n):
        for c in range(cuts):
            source = weights.at[k, pl.ds(3 * depth + c * width, width), pl.ds(0, columns)]
            target = wos.at[:, pl.ds(k * depth + c * columns, columns)]
            copies.append(pltpu.make_async_copy(source, target, sems.at[first + cuts * k + c]))
    return copies


def output_copies(n, depth, width):
    return n * max(1, depth // width)


def piece_shapes(own_rows, columns, count):
    half = shape((own_rows // 2, columns), bf16)
    return [half, half] + [shape((own_rows, columns), bf16)] * (count - 2)


def cost(micros):
    return pl.CostEstimate(flops=int(micros * 6e8), bytes_accessed=1 << 20, transcendentals=0)


def piece_rows(order, half, pieces):
    rows = 2 * half
    starts = [pl.multiple_of(order[0] * rows, rows)]
    starts.append(pl.multiple_of(order[0] * rows + half, half))
    for number in range(2, pieces):
        starts.append(pl.multiple_of(order[number - 1] * rows, rows))
    return starts


def send_out(staged, targets, sems, first, starts):
    copies = []
    for number, target in enumerate(targets):
        copy = pltpu.make_async_copy(
            staged.at[pl.ds(starts[number], target.shape[0])], target, sems.at[first + number]
        )
        copy.start()
        copies.append(copy)
    return copies


def allowed_pairs(seg_col, seg_row, first, rows, width):
    row_pos = first + lax.broadcasted_iota(jnp.int32, (rows, width), 0)
    key_pos = lax.broadcasted_iota(jnp.int32, (rows, width), 1)
    return (seg_col[pl.ds(first, rows), :] == seg_row[:, pl.ds(0, width)]) & (key_pos <= row_pos)


def attn_proj_body(count, block, *refs):
    it = iter(refs)
    order = next(it)
    pieces = [next(it) for _ in range(count)]
    wq = next(it)
    gain, gains, cosine, sine = (next(it) for _ in range(4))
    q_o, k_o, v_o, qr_o, kr_o, x_o = (next(it) for _ in range(6))
    xs, xn, wqs, sems = (next(it) for _ in range(4))
    length, width = q_o.shape
    heads = width // HD
    starts = piece_rows(order, pieces[0].shape[0], count)
    copies = load_projections(wq, wqs, sems, count)
    for copy in copies:
        copy.start()
    for copy in fetch(pieces, xs, sems, 0, starts) + copies:
        copy.wait()

    def project(r, _):
        rows = pl.ds(pl.multiple_of(r * block, block), block)
        wide = xs[rows, :].astype(f32)
        inv = lax.rsqrt(jnp.mean(wide * wide, axis=-1, keepdims=True) + EPSILON)
        xn[rows, :] = (wide * inv * gain[...]).astype(bf16)
        out = dot(xn[rows, :], wqs[...])
        v_o[rows, :] = out[:, 2 * width :].astype(bf16)
        for j, (raw_o, hat_o) in enumerate(((qr_o, q_o), (kr_o, k_o))):
            raw = out[:, j * width : (j + 1) * width]
            raw_o[rows, :] = raw
            for h in range(heads):
                cols = slice(h * HD, (h + 1) * HD)
                u = raw[:, cols]
                inv = lax.rsqrt(jnp.mean(u * u, axis=-1, keepdims=True) + EPSILON)
                u = u * inv * gains[j : j + 1, cols]
                u = u * cosine[rows, :] + pltpu.roll(u, HD // 2, 1) * sine[rows, :]
                hat_o[rows, cols] = u.astype(bf16)
        return 0

    lax.fori_loop(0, length // block, project, 0)
    keep = pltpu.make_async_copy(xn, x_o, sems.at[0])
    keep.start()
    keep.wait()


def attn_proj(order, pieces, wq, gain, gains, cosine, sine):
    n, count = wq.shape[0], len(pieces)
    d = gain.shape[1]
    length = cosine.shape[0]
    width = wq.shape[2]
    return pl.pallas_call(
        functools.partial(attn_proj_body, count, min(256, length)),
        in_specs=[SMEM] + [ANY] * (count + 1) + [VMEM] * 4,
        out_specs=[VMEM] * 5 + [ANY],
        out_shape=[shape((length, width), bf16)] * 3
        + [shape((length, width), f32)] * 2
        + [shape((length, d), bf16)],
        scratch_shapes=[
            pltpu.VMEM((length, d), bf16),
            pltpu.VMEM((length, d), bf16),
            pltpu.VMEM((d, 3 * width), bf16),
            pltpu.SemaphoreType.DMA((count + 3 * n,)),
        ],
        compiler_params=pltpu.CompilerParams(vmem_limit_bytes=VMEM_BYTES),
        cost_estimate=cost(10),
        name="attn_proj",
    )(order, *pieces, wq, gain, gains, cosine, sine)


def attn_core_body(count, block, *refs):
    it = iter(refs)
    order = next(it)
    wo = next(it)
    q, k_, v, seg_row, seg_col = (next(it) for _ in range(5))
    ctx_o, lse_o = next(it), next(it)
    outs = [next(it) for _ in range(count)]
    wos, stage, sems = (next(it) for _ in range(3))
    length, width = ctx_o.shape
    heads = width // HD
    starts = piece_rows(order, outs[0].shape[0], count)
    copies = load_outputs(wo, wos, sems, count)
    for copy in copies:
        copy.start()
    scale = HD ** (-0.5)
    for b in range(length // block):
        rows = pl.ds(b * block, block)
        hi = (b + 1) * block
        allowed = allowed_pairs(seg_col, seg_row, b * block, block, hi)
        for h in range(heads):
            cols = slice(h * HD, (h + 1) * HD)
            s = dot_nt(q[rows, cols], k_[pl.ds(0, hi), cols]) * scale
            s = jnp.where(allowed, s, MASKED)
            top = jnp.max(s, axis=-1, keepdims=True)
            e = jnp.exp(s - top)
            total = jnp.sum(e, axis=-1, keepdims=True)
            probs = (e * (1.0 / total)).astype(bf16)
            ctx_o[rows, cols] = dot(probs, v[pl.ds(0, hi), cols]).astype(bf16)
            lse_o[h, rows, :] = top + jnp.log(total)
    for copy in copies:
        copy.wait()
    stage[...] = dot(ctx_o[...], wos[...]).astype(bf16)
    for copy in send_out(stage, outs, sems, 0, starts):
        copy.wait()


def attn_core(order, wo, q, k, v, seg_row, seg_col, own_rows, d):
    n = wo.shape[0]
    length, width = q.shape
    count = length // own_rows + 1
    return pl.pallas_call(
        functools.partial(attn_core_body, count, min(256, length)),
        in_specs=[SMEM] + [ANY] + [VMEM] * 5,
        out_specs=[VMEM] * 2 + [ANY] * count,
        out_shape=[shape((length, width), bf16), shape((width // HD, length, 1), f32)]
        + piece_shapes(own_rows, d, count),
        scratch_shapes=[
            pltpu.VMEM((width, d), bf16),
            pltpu.VMEM((length, d), bf16),
            pltpu.SemaphoreType.DMA((count + output_copies(n, d // n, width),)),
        ],
        compiler_params=pltpu.CompilerParams(vmem_limit_bytes=VMEM_BYTES),
        cost_estimate=cost(10),
        name="attn_core",
    )(order, wo, q, k, v, seg_row, seg_col)


def attn_back_body(count, block, *refs):
    it = iter(refs)
    order = next(it)
    pieces = [next(it) for _ in range(count)]
    wo = next(it)
    q, k_, v, lse, seg_row, seg_col = (next(it) for _ in range(6))
    dq_o, dk_o, dv_o, db_o = (next(it) for _ in range(4))
    db, wos, dctx, sems = (next(it) for _ in range(4))
    length, width = q.shape
    heads = width // HD
    starts = piece_rows(order, pieces[0].shape[0], count)
    copies = load_outputs(wo, wos, sems, count)
    for copy in copies:
        copy.start()
    for copy in copies + fetch(pieces, db, sems, 0, starts):
        copy.wait()
    keep = pltpu.make_async_copy(db, db_o, sems.at[0])
    keep.start()
    scale = HD ** (-0.5)
    dctx[...] = dot_nt(db[...], wos[...]).astype(bf16)
    dk_o[...] = jnp.zeros_like(dk_o)
    dv_o[...] = jnp.zeros_like(dv_o)
    for b in range(length // block):
        rows = pl.ds(b * block, block)
        hi = (b + 1) * block
        low = pl.ds(0, hi)
        allowed = allowed_pairs(seg_col, seg_row, b * block, block, hi)
        for h in range(heads):
            cols = slice(h * HD, (h + 1) * HD)
            s = dot_nt(q[rows, cols], k_[low, cols]) * scale
            p = jnp.where(allowed, jnp.exp(s - lse[h, rows, :]), 0.0)
            g = dot_nt(dctx[rows, cols], v[low, cols])
            pg = p * g
            ds = (pg - p * jnp.sum(pg, axis=-1, keepdims=True)).astype(bf16)
            dq_o[rows, cols] = dot(ds, k_[low, cols]) * scale
            dk_o[low, cols] += dot_tn(ds, q[rows, cols]) * scale
            dv_o[low, cols] += dot_tn(p.astype(bf16), dctx[rows, cols])
    keep.wait()


def attn_back(order, pieces, wo, q, k, v, lse, seg_row, seg_col):
    n, count = wo.shape[0], len(pieces)
    d = pieces[0].shape[1]
    length, width = q.shape
    return pl.pallas_call(
        functools.partial(attn_back_body, count, min(256, length)),
        in_specs=[SMEM] + [ANY] * (count + 1) + [VMEM] * 6,
        out_specs=[VMEM] * 3 + [ANY],
        out_shape=[shape((length, width), f32)] * 3 + [shape((length, d), bf16)],
        scratch_shapes=[
            pltpu.VMEM((length, d), bf16),
            pltpu.VMEM((width, d), bf16),
            pltpu.VMEM((length, width), bf16),
            pltpu.SemaphoreType.DMA((count + output_copies(n, d // n, width),)),
        ],
        compiler_params=pltpu.CompilerParams(vmem_limit_bytes=VMEM_BYTES),
        cost_estimate=cost(14),
        name="attn_back",
    )(order, *pieces, wo, q, k, v, lse, seg_row, seg_col)


def proj_back_body(count, block, *refs):
    it = iter(refs)
    order = next(it)
    wq = next(it)
    qr, kr, dq, dk, dv = (next(it) for _ in range(5))
    gains, cosine, sine, x = (next(it) for _ in range(4))
    dp_o, hg_o, gs_o = (next(it) for _ in range(3))
    outs = [next(it) for _ in range(count)]
    wqs, stage, sems = (next(it) for _ in range(3))
    length, width = qr.shape
    heads = width // HD
    starts = piece_rows(order, outs[0].shape[0], count)
    copies = load_projections(wq, wqs, sems, count)
    for copy in copies:
        copy.start()
    hg_o[...] = jnp.zeros_like(hg_o)
    gs_o[...] = jnp.zeros_like(gs_o)
    for copy in copies:
        copy.wait()

    def finish(r, _):
        rows = pl.ds(pl.multiple_of(r * block, block), block)
        dp_o[rows, 2 * width :] = dv[rows, :].astype(bf16)
        for j, (raw, grad) in enumerate(((qr, dq), (kr, dk))):
            for h in range(heads):
                cols = slice(h * HD, (h + 1) * HD)
                u = raw[rows, cols]
                inv = lax.rsqrt(jnp.mean(u * u, axis=-1, keepdims=True) + EPSILON)
                hat = u * inv
                t = grad[rows, cols]
                t = t * cosine[rows, :] - pltpu.roll(t, HD // 2, 1) * sine[rows, :]
                hg_o[j : j + 1, cols] += jnp.sum(t * hat, axis=0, keepdims=True)
                w = t * gains[j : j + 1, cols]
                w = inv * (w - hat * jnp.mean(w * hat, axis=-1, keepdims=True))
                dp_o[rows, j * width + h * HD : j * width + (h + 1) * HD] = w.astype(bf16)
        out = dot_nt(dp_o[rows, :], wqs[...])
        gs_o[...] += jnp.sum(out * x[rows, :].astype(f32), axis=0, keepdims=True)
        stage[rows, :] = out.astype(bf16)
        return 0

    lax.fori_loop(0, length // block, finish, 0)
    for copy in send_out(stage, outs, sems, 0, starts):
        copy.wait()


def proj_back(order, wq, qr, kr, dq, dk, dv, gains, cosine, sine, x, own_rows):
    n = wq.shape[0]
    length, width = qr.shape
    d = x.shape[1]
    count = length // own_rows + 1
    return pl.pallas_call(
        functools.partial(proj_back_body, count, min(256, length)),
        in_specs=[SMEM] + [ANY] + [VMEM] * 9,
        out_specs=[VMEM] * 3 + [ANY] * count,
        out_shape=[
            shape((length, 3 * width), bf16),
            shape((2, width), f32),
            shape((1, d), f32),
        ]
        + piece_shapes(own_rows, d, count),
        scratch_shapes=[
            pltpu.VMEM((d, 3 * width), bf16),
            pltpu.VMEM((length, d), bf16),
            pltpu.SemaphoreType.DMA((count + 3 * n,)),
        ],
        compiler_params=pltpu.CompilerParams(vmem_limit_bytes=VMEM_BYTES),
        cost_estimate=cost(12),
        name="proj_back",
    )(order, wq, qr, kr, dq, dk, dv, gains, cosine, sine, x)


def attn_grad_body(places, xa, xb, dp, ctx, da, db, qkv_keep, qkv_send, out_keep, out_send):
    width = ctx.shape[1]
    for x, d, qkv_o, out_o in ((xa, da, qkv_keep, out_keep), (xb, db, qkv_send, out_send)):
        grad = dot_tn(x[...], dp[...])
        for j in range(3):
            qkv_o[0, j] = grad[:, j * width : (j + 1) * width].astype(bf16)
        out_o[0] = dot_tn(ctx[...], d[...]).astype(bf16)


def attn_grad(places, x, dp, ctx, db, n):
    length, d = x.shape
    width = ctx.shape[1]
    depth = d // n
    even = pl.BlockSpec((length, depth), lambda m, at: (0, at[2 * m]))
    odd = pl.BlockSpec((length, depth), lambda m, at: (0, at[2 * m + 1]))
    return pl.pallas_call(
        attn_grad_body,
        grid_spec=pltpu.PrefetchScalarGridSpec(
            num_scalar_prefetch=1,
            grid=(n // 2,),
            in_specs=[
                even,
                odd,
                pl.BlockSpec((length, 3 * width), lambda m, at: (0, 0)),
                pl.BlockSpec((length, width), lambda m, at: (0, 0)),
                even,
                odd,
            ],
            out_specs=[pl.BlockSpec((1, 3, depth, width), lambda m, at: (m, 0, 0, 0))] * 2
            + [pl.BlockSpec((1, width, depth), lambda m, at: (m, 0, 0))] * 2,
        ),
        out_shape=[shape((n // 2, 3, depth, width), bf16)] * 2
        + [shape((n // 2, width, depth), bf16)] * 2,
        compiler_params=pltpu.CompilerParams(vmem_limit_bytes=VMEM_BYTES),
        cost_estimate=cost(6),
        name="attn_grad",
    )(places, x, x, dp, ctx, db, db)


def flat_rows(pieces):
    starts, at = [], 0
    for piece in pieces:
        starts.append(at)
        at += piece.shape[0]
    return starts


def moe_in_body(count, *refs):
    xp, gu, out, xs, sems = refs[:count], *refs[count:]

    @pl.when(pl.program_id(0) == 0)
    def _():
        for copy in fetch(xp, xs, sems, 0, flat_rows(xp)):
            copy.wait()

    out[...] = dot(xs[...], gu[...]).astype(bf16)


def moe_in(xp, gate_up, group=4):
    count = len(xp)
    d, columns = gate_up.shape
    rows = sum(p.shape[0] for p in xp)
    wide = 2 * group * LANES
    return pl.pallas_call(
        functools.partial(moe_in_body, count),
        grid=(columns // wide,),
        in_specs=[ANY] * count + [pl.BlockSpec((d, wide), lambda s: (0, s))],
        out_specs=pl.BlockSpec((rows, wide), lambda s: (0, s)),
        out_shape=shape((rows, columns), bf16),
        scratch_shapes=[pltpu.VMEM((rows, d), bf16), pltpu.SemaphoreType.DMA((count,))],
        compiler_params=pltpu.CompilerParams(vmem_limit_bytes=VMEM_BYTES),
        cost_estimate=cost(rows * 0.02 + 4),
        name="moe_in",
    )(*xp, gate_up)


def moe_mid_body(group, steps, sets, count, *refs):
    it = iter(refs)
    gates = next(it)
    cp = [next(it) for _ in range(count)]
    gus = [next(it) for _ in range(sets)]
    gu_w, dn_w = next(it), next(it)
    d_outs = [next(it) for _ in range(count)]
    m_outs = [next(it) for _ in range(count)]
    dgu_o, hw_o = next(it), next(it)
    cs, d_acc, m_acc, gg, stage, sems = (next(it) for _ in range(6))
    d = cs.shape[1]
    fw = LANES
    step = pl.program_id(0)

    @pl.when(step == 0)
    def _():
        copies = fetch(cp, cs, sems, 0, flat_rows(cp))
        d_acc[...] = jnp.zeros_like(d_acc)
        m_acc[...] = jnp.zeros_like(m_acc)
        gg[...] = jnp.zeros_like(gg)
        for copy in copies:
            copy.wait()

    d_hid = dot_nt(cs[...], dn_w[...])
    at = 0
    for gu in gus:
        rows = gu.shape[0]
        here = pl.ds(at, rows)
        table = gates[here, :].astype(f32)
        lane = lax.broadcasted_iota(jnp.int32, table.shape, 1)
        total = jnp.zeros(table.shape, f32)
        for i in range(group):
            g = gu[:, 2 * i * fw : (2 * i + 1) * fw].astype(f32)
            u = gu[:, (2 * i + 1) * fw : (2 * i + 2) * fw].astype(f32)
            dh = d_hid[at : at + rows, i * fw : (i + 1) * fw]
            z = jax.nn.sigmoid(g)
            swish = g * z
            h = swish * u
            expert = step * group + i
            own = jnp.sum(h * dh, axis=1, keepdims=True)
            total = total + jnp.where(lane == expert, own, 0.0)
            gate = jnp.sum(jnp.where(lane == expert, table, 0.0), axis=1, keepdims=True)
            dw = dh * gate
            d_g = dw * u * z * (1.0 + g * (1.0 - z))
            hw_o[here, i * fw : (i + 1) * fw] = (h * gate).astype(bf16)
            dgu_o[here, 2 * i * fw : (2 * i + 1) * fw] = d_g.astype(bf16)
            dgu_o[here, (2 * i + 1) * fw : (2 * i + 2) * fw] = (dw * swish).astype(bf16)
        gg[here, :] += total
        at += rows
    d_acc[...] += dot_nt(dgu_o[...], gu_w[...])
    m_acc[...] += dot(hw_o[...], dn_w[...])

    @pl.when(step == steps - 1)
    def _():
        stage[:, pl.ds(0, d)] = d_acc[...].astype(bf16)
        stage[:, pl.ds(d, LANES)] = gg[...].astype(bf16)
        copies = send_out(stage, d_outs, sems, 0, flat_rows(d_outs))
        cs[...] = m_acc[...].astype(bf16)
        copies = copies + send_out(cs, m_outs, sems, count, flat_rows(m_outs))
        for copy in copies:
            copy.wait()


def moe_mid(gates, cp, gus, gate_up, down, group=4):
    count = len(cp)
    hidden, d = down.shape
    rows = sum(p.shape[0] for p in cp)
    half = group * LANES
    steps = hidden // half
    return pl.pallas_call(
        functools.partial(moe_mid_body, group, steps, len(gus), count),
        grid=(steps,),
        in_specs=[pl.BlockSpec((rows, LANES), lambda s: (0, 0))]
        + [ANY] * count
        + [pl.BlockSpec((g.shape[0], 2 * half), lambda s: (0, s)) for g in gus]
        + [
            pl.BlockSpec((d, 2 * half), lambda s: (0, s)),
            pl.BlockSpec((half, d), lambda s: (s, 0)),
        ],
        out_specs=[ANY] * (2 * count)
        + [
            pl.BlockSpec((rows, 2 * half), lambda s: (0, s)),
            pl.BlockSpec((rows, half), lambda s: (0, s)),
        ],
        out_shape=[shape((p.shape[0], d + LANES), bf16) for p in cp]
        + [shape(p.shape, bf16) for p in cp]
        + [shape((rows, 2 * hidden), bf16), shape((rows, hidden), bf16)],
        scratch_shapes=[
            pltpu.VMEM((rows, d), bf16),
            pltpu.VMEM((rows, d), f32),
            pltpu.VMEM((rows, d), f32),
            pltpu.VMEM((rows, LANES), f32),
            pltpu.VMEM((rows, d + LANES), bf16),
            pltpu.SemaphoreType.DMA((2 * count,)),
        ],
        compiler_params=pltpu.CompilerParams(vmem_limit_bytes=VMEM_BYTES),
        cost_estimate=cost(rows * 0.04 + 6),
        name="moe_mid",
    )(gates, *cp, *gus, gate_up, down)


def turn_body(count, *refs):
    pieces, out, xs, sems = refs[:count], refs[count], refs[count + 1], refs[count + 2]
    for copy in fetch(pieces, xs, sems, 0, flat_rows(pieces)):
        copy.wait()
    d = xs.shape[1]
    size = 256
    eye = (
        lax.broadcasted_iota(jnp.int32, (size, size), 0)
        == lax.broadcasted_iota(jnp.int32, (size, size), 1)
    ).astype(bf16)
    for at in range(0, d, size):
        out[pl.ds(at, size), :] = dot_nt(eye, xs[:, pl.ds(at, size)]).astype(bf16)


def turn_rows(pieces):
    count = len(pieces)
    length = sum(p.shape[0] for p in pieces)
    d = pieces[0].shape[1]
    return pl.pallas_call(
        functools.partial(turn_body, count),
        in_specs=[ANY] * count,
        out_specs=VMEM,
        out_shape=shape((d, length), bf16),
        scratch_shapes=[pltpu.VMEM((length, d), bf16), pltpu.SemaphoreType.DMA((count,))],
        compiler_params=pltpu.CompilerParams(vmem_limit_bytes=VMEM_BYTES),
        cost_estimate=cost(4),
        name="turn_rows",
    )(*pieces)


def in_grad_body(n, group, sets, places, xt, *refs):
    dgus = refs[:sets]
    *outs, xs, sems = refs[-4:]
    depth, fw = outs[0].shape[3:]
    step = pl.program_id(0)

    def part(k):
        source = xt.at[pl.ds(pl.multiple_of(places[k] * depth, depth), depth)]
        return pltpu.make_async_copy(source, xs.at[pl.ds(k * depth, depth)], sems.at[k])

    @pl.when(step == 0)
    def _():
        for k in range(n):
            part(k).start()

    dgu = jnp.concatenate([ref[...] for ref in dgus], axis=0)
    for k in range(n):

        @pl.when(step == 0)
        def _(k=k):
            part(k).wait()

        grad = dot(xs[pl.ds(k * depth, depth), :], dgu)
        for i in range(group):
            for g in range(2):
                at = (2 * i + g) * fw
                outs[k % 2][k // 2, i, g] = grad[:, at : at + fw].astype(bf16)


def in_grad(places, xt, dgus, n, experts, first, number, held, whole=None, group=2):
    d, length = xt.shape
    depth = d // n
    fw = dgus[0].shape[1] // (2 * experts)
    start = first // group
    at = (first % held) // group
    before = [] if whole is None else list(whole)
    sets = len(dgus)
    return list(
        pl.pallas_call(
            functools.partial(in_grad_body, n, group, sets),
            grid=(number // group,),
            in_specs=[SMEM, ANY]
            + [pl.BlockSpec((a.shape[0], 2 * group * fw), lambda s: (0, s + start)) for a in dgus]
            + [ANY] * len(before),
            out_specs=[pl.BlockSpec((n // 2, group, 2, depth, fw), lambda s: (0, at + s, 0, 0, 0))]
            * 2,
            out_shape=[shape((n // 2, held, 2, depth, fw), bf16)] * 2,
            input_output_aliases={2 + sets: 0, 3 + sets: 1} if before else {},
            scratch_shapes=[pltpu.VMEM((d, length), bf16), pltpu.SemaphoreType.DMA((n,))],
            compiler_params=pltpu.CompilerParams(vmem_limit_bytes=VMEM_BYTES),
            cost_estimate=cost(1.5 * number + 3),
            name="in_grad",
        )(places, xt, *dgus, *before)
    )


def out_grad_body(group, count, sets, *refs):
    hws, pieces = refs[:sets], refs[sets : sets + count]
    out, cs, sems = refs[-3:]
    fw = out.shape[1]

    @pl.when(pl.program_id(0) == 0)
    def _():
        for copy in fetch(pieces, cs, sems, 0, flat_rows(pieces)):
            copy.wait()

    turned = jnp.concatenate([ref[...] for ref in hws], axis=0).T
    grad = dot(turned, cs[...])
    for i in range(group):
        out[i] = grad[i * fw : (i + 1) * fw].astype(bf16)


def out_grad(hws, cp, experts, group=2):
    count = len(cp)
    length = sum(h.shape[0] for h in hws)
    d = cp[0].shape[1]
    fw = hws[0].shape[1] // experts
    return pl.pallas_call(
        functools.partial(out_grad_body, group, count, len(hws)),
        grid=(experts // group,),
        in_specs=[pl.BlockSpec((h.shape[0], group * fw), lambda s: (0, s)) for h in hws]
        + [ANY] * count,
        out_specs=pl.BlockSpec((group, fw, d), lambda s: (s, 0, 0)),
        out_shape=shape((experts, fw, d), bf16),
        scratch_shapes=[pltpu.VMEM((length, d), bf16), pltpu.SemaphoreType.DMA((count,))],
        compiler_params=pltpu.CompilerParams(vmem_limit_bytes=VMEM_BYTES),
        cost_estimate=cost(12),
        name="out_grad",
    )(*hws, *cp)


def finish_body(*refs):
    keep, got, more, out = refs[-4:]
    out[...] = keep[0].astype(f32) + got[0].astype(f32) + more[0].astype(f32)


def finish(whole, terms, experts, first):
    number = terms[0].shape[1]
    rest = terms[0].shape[2:]
    zeros = (0,) * len(rest)
    before = [] if whole is None else [whole]
    each = 2
    at = first // each
    return pl.pallas_call(
        finish_body,
        grid=(number // each,),
        in_specs=[ANY] * len(before)
        + [pl.BlockSpec((1, each) + rest, lambda s: (0, s) + zeros)] * 3,
        out_specs=pl.BlockSpec((each,) + rest, lambda s: (at + s,) + zeros),
        out_shape=shape((experts,) + rest, f32),
        input_output_aliases={0: 0} if before else {},
        compiler_params=pltpu.CompilerParams(vmem_limit_bytes=VMEM_BYTES),
        cost_estimate=cost(2),
        name="finish",
    )(*before, *terms)


def place_body(*refs):
    part, out = refs[-2:]
    out[...] = part[...].astype(f32)


def place(part, experts, whole=None):
    rest = part.shape[1:]
    zeros = (0,) * len(rest)
    before = [] if whole is None else [whole]
    return pl.pallas_call(
        place_body,
        grid=(part.shape[0] // 2,),
        in_specs=[ANY] * len(before) + [pl.BlockSpec((2,) + rest, lambda s: (s,) + zeros)],
        out_specs=pl.BlockSpec((2,) + rest, lambda s: (s,) + zeros),
        out_shape=shape((experts,) + rest, f32),
        input_output_aliases={0: 0} if before else {},
        compiler_params=pltpu.CompilerParams(vmem_limit_bytes=VMEM_BYTES),
        cost_estimate=cost(3),
        name="place",
    )(*before, part)


def pack_body(w, out):
    fw = w.shape[3]
    for i in range(w.shape[0]):
        for g in range(2):
            at = (2 * i + g) * fw
            out[:, at : at + fw] = w[i, g]


def pack(gate_up, group=4):
    experts, _, depth, fw = gate_up.shape
    return pl.pallas_call(
        pack_body,
        grid=(experts // group,),
        in_specs=[pl.BlockSpec((group, 2, depth, fw), lambda s: (s, 0, 0, 0))],
        out_specs=pl.BlockSpec((depth, 2 * group * fw), lambda s: (0, s)),
        out_shape=shape((depth, 2 * experts * fw), bf16),
        compiler_params=pltpu.CompilerParams(vmem_limit_bytes=VMEM_BYTES),
        cost_estimate=cost(4),
        name="pack",
    )(gate_up)


def rope_tables(length):
    positions = np.arange(length, dtype=np.float32)
    power = -np.arange(HD // 2, dtype=np.float32) * np.float32(2.0) / np.float32(HD)
    inverse_freq = np.power(np.float32(ROPE_BASE), power)
    phases = positions[:, None] * inverse_freq[None, :]
    cosine, sine = np.cos(phases), np.sin(phases)
    tables = [cosine, cosine], [-sine, sine]
    return [np.concatenate(t, axis=-1).astype(np.float32) for t in tables]


def per_device(
    tokens,
    segments,
    routes,
    gate_values,
    cotangent,
    query_key_value,
    out_weight,
    head_gain,
    layer_gain,
    gate_up,
    down_weight,
):
    groups = lax.axis_size("tensor")
    n = lax.axis_size("dp")
    own_rows, d = tokens.shape
    seq_len = own_rows * groups
    heads = query_key_value.shape[2] // HD
    experts = gate_up.shape[0]
    depth = d // n
    steps = groups // 2
    top = routes.shape[1]

    x = tokens.astype(f32)
    routed = jnp.concatenate([routes.astype(bf16), gate_values], axis=1)
    routed = jnp.pad(routed, ((0, 0), (0, LANES - 2 * top)))
    normed = Gather(jnp.concatenate([tokens, routed], axis=1), groups)
    first = normed.step()

    width = query_key_value.shape[2]
    small = jnp.concatenate([layer_gain.reshape(-1), head_gain.reshape(-1)])
    size = small.shape[0]
    small = jnp.pad(small, (0, -size % (16 * width))).reshape(-1, width)
    outward = split_last(out_weight, max(1, depth // width))
    outward = [jnp.pad(a, ((0, 0), (0, width - a.shape[1]))) for a in outward]
    own = [query_key_value.reshape(-1, width)] + outward + [small]
    attn_weights = lax.all_gather(jnp.concatenate(own, axis=0), "dp", axis=0)

    ring = ring_of(groups)
    orders = [[ring[(ring.index(t) + k) % groups] for k in distances_of(groups)] for t in range(groups)]
    orders = jnp.array(orders, jnp.int32)
    order = lax.dynamic_slice(orders, (lax.axis_index("tensor"), 0), (1, groups)).reshape(groups)
    places = jnp.array([[i ^ k for k in range(n)] for i in range(n)], jnp.int32)
    places = lax.dynamic_slice(places, (lax.axis_index("dp"), 0), (1, n)).reshape(n)
    cosine, sine = rope_tables(seq_len)
    seg_row = segments.reshape(1, seq_len)
    seg_col = segments.reshape(seq_len, 1)
    expert_ids = jnp.arange(experts, dtype=jnp.int32)
    chosen = routes[:, :, None] == expert_ids
    (gate_up,) = tie((gate_up,), first)
    packed = pack(gate_up)

    done = normed.step()
    (packed,) = tie((packed,), done)
    gu = lax.all_gather(packed, "dp", axis=0, tiled=True)
    normed.step(after=[packed])
    normed.step()
    cut = 2 * depth
    small = [w[-small.shape[0] :].reshape(-1)[:size] for w in attn_weights]
    gain = jnp.concatenate([s[:cut].reshape(2, depth) for s in small], axis=1).astype(f32)
    gain_in, gain_mid = gain[0], gain[1]
    head_parts = [s[cut:].reshape(2, heads, HD // n) for s in small]
    gain_head = jnp.concatenate(head_parts, axis=2).reshape(2, heads * HD).astype(f32)
    pieces = normed.pieces()
    inv_in = lax.rsqrt(jnp.mean(x * x, axis=-1, keepdims=True) + EPSILON)
    x_hat = x * inv_in
    q, k, v, q_raw, k_raw, normed_all = attn_proj(
        order, pieces, attn_weights, gain_in[None, :], gain_head, cosine, sine
    )
    d_pieces = Gather(cotangent, groups)
    first = d_pieces.step(after=pieces)
    q, k, v = tie((q, k, v), first)
    context, lse, *attn = attn_core(
        order, attn_weights, q, k, v, seg_row, seg_col, own_rows, d
    )
    second = d_pieces.step(after=[q])
    routed = jnp.concatenate([p[:, d : d + 2 * top] for p in pieces], axis=0)
    named = routed[:, :top].astype(jnp.int32)[:, :, None] == expert_ids
    gate_table = jnp.sum(jnp.where(named, routed[:, top:].astype(f32)[:, :, None], 0.0), axis=1)
    gate_table = jnp.pad(gate_table.astype(bf16), ((0, 0), (0, LANES - experts)))
    attention = Scatter(attn, groups)
    done = attention.step(after=second)
    (down,) = tie((down_weight.reshape(-1, depth),), done)
    dn = lax.all_gather(down, "dp", axis=1, tiled=True)
    middle = x + attention.run().result()
    inv_mid = lax.rsqrt(jnp.mean(middle * middle, axis=-1, keepdims=True) + EPSILON)
    mid_hat = middle * inv_mid
    mid = Gather((mid_hat * gain_mid).astype(bf16), groups)

    hidden_in = []
    mid.step()
    for s in range(1, steps - 1):
        here = [mid.at(s), mid.at(-s)] + ([mid.at(0)] if s == 1 else [])
        mid.step(after=hidden_in[-1:])
        hidden_in.append(moe_in(here, gu))
    mid.step(after=hidden_in[-1:])
    normed_mid = mid.pieces()
    taken = normed_mid[:4]
    hidden_in.append(moe_in(taken, gu))
    d_pieces.step(after=taken)
    d_pieces.step(after=hidden_in[-1:])
    d_pieces = d_pieces.pieces()

    half_rows = hidden_in[-1].shape[0]
    d_far, d_near = d_pieces[:4], d_pieces[4:]
    far_out = list(moe_mid(gate_table[:half_rows], d_far, hidden_in[-1:], gu, dn))
    d_mid, moe, d_in, hidden = far_out[:4], far_out[4:8], far_out[8:9], far_out[9:]
    (mid_far,) = tie(normed_mid[:1], d_mid[:1])
    mid_turned = turn_rows([mid_far] + normed_mid[1:])
    d_normed = Scatter(d_mid, groups)
    done = d_normed.step()
    mixing = Scatter(moe, groups)
    second = d_normed.step(after=[mid_turned], riders=mixing.far)
    mixing.done, mixing.moved = 1, [m[:, :d] for m in d_normed.ridden]
    (table,) = tie((gate_table[half_rows:],), done + [mid_turned])
    near_out = list(moe_mid(table, d_near, hidden_in[:-1][::-1], gu, dn))
    count = len(d_near)
    d_mid, moe = d_mid + near_out[:count], moe + near_out[count : 2 * count]
    d_in, hidden = d_in + near_out[2 * count : -1], hidden + near_out[-1:]
    d_normed.block = dict(zip(distances_of(groups)[1:], d_mid[2:]))
    mixing.block = dict(zip(distances_of(groups)[1:], moe[2:]))
    third = d_normed.step(after=moe[-1:])

    (hidden_far,) = tie(hidden[:1], second + near_out[:1])
    dn_all = out_grad([hidden_far] + hidden[1:], d_pieces, experts)
    (ready,) = tie((dn_all,), third)
    dn_grad = lax.psum_scatter(ready, "dp", scatter_dimension=2, tiled=True)
    fourth = d_normed.step(after=[dn_all])

    def gradient(c, after, whole=None):
        (turned,) = tie((mid_turned,), after)
        return in_grad(places, turned, d_in, n, experts, c * each, each, 2 * each, whole)

    each = experts // CHUNKS
    low = gradient(0, third)
    d_normed_mid = d_normed.result()
    gate_sum = d_normed_mid[:, d:]
    d_normed_mid = d_normed_mid[:, :d]
    d_mid_hat = d_normed_mid * gain_mid
    d_middle = cotangent.astype(f32) + inv_mid * (
        d_mid_hat - mid_hat * jnp.mean(d_mid_hat * mid_hat, axis=-1, keepdims=True)
    )
    branch = Gather(d_middle.astype(bf16), groups)
    moved = branch.step(after=low)
    low = gradient(1, [d_middle], low)
    moved_on = branch.step(after=low)
    low_keep, low_send = low[0], tie(low[1:], moved)[0]
    low_terms = flip_reduce(low_keep, low_send, "dp", n)
    high = gradient(2, moved)
    moved = branch.step(after=high + low_terms[3:])
    high = gradient(3, moved_on, high)
    branch.step(after=high)
    high_keep, high_send = high[0], tie(high[1:], moved)[0]
    high_terms = flip_reduce(high_keep, high_send, "dp", n)
    d_branch = branch.pieces()

    moe_second = mixing.step(after=d_branch + high_terms[3:])
    dq, dk, dv, d_branch_all = attn_back(
        order, d_branch, attn_weights, q, k, v, lse, seg_row, seg_col
    )
    dq, dk, dv = tie((dq, dk, dv), moe_second)
    moe_third = mixing.step()
    d_projected, head_part, in_part, *to_rows = proj_back(
        order, attn_weights, q_raw, k_raw, dq, dk, dv, gain_head, cosine, sine, normed_all, own_rows
    )
    d_normed = Scatter(to_rows, groups)
    late = [d_normed.step(after=moe_third + low_terms[2:3])]
    (projected,) = tie((d_projected,), late[0])
    qkv_keep, qkv_send, out_keep, out_send = attn_grad(
        places, normed_all, projected, context, d_branch_all, n
    )
    late.append(d_normed.step())
    qkv_send, out_send = tie((qkv_send, out_send), late[1])
    qkv_terms = flip_reduce(qkv_keep, qkv_send, "dp", n)
    out_terms = flip_reduce(out_keep, out_send, "dp", n)
    (dn_grad,) = tie((dn_grad,), late[0])
    dn_grad = place(dn_grad, experts)
    late.append(
        d_normed.step(after=[qkv_keep, dn_grad])
    )

    (late_low,) = tie(low_terms[2:3], late[1])
    gu_grad = finish(None, low_terms[:2] + [late_low], experts, 0)
    late.append(d_normed.step(after=[gu_grad] + qkv_terms[3:] + out_terms[3:] + high_terms[2:3]))
    (late_high,) = tie(high_terms[2:3], late[3])
    gu_grad = finish(gu_grad, high_terms[:2] + [late_high], experts, 2 * each)
    late.append(mixing.step(after=late[3]))
    qkv_terms = qkv_terms[:2] + list(tie(qkv_terms[2:3], late[4]))
    d_normed_in = d_normed.result()
    d_x_hat = d_normed_in * gain_in
    input_grad = d_middle + inv_in * (
        d_x_hat - x_hat * jnp.mean(d_x_hat * x_hat, axis=-1, keepdims=True)
    )
    mixed = (middle + mixing.result()).astype(bf16)
    gate_grad = jnp.sum(jnp.where(chosen, gate_sum[:, None, :experts], 0.0), axis=-1)
    out_terms = out_terms[:2] + list(tie(out_terms[2:3], late[4]))
    qkv_grad = sum(t[0].astype(f32) for t in qkv_terms[:3])
    out_weight_grad = sum(t[0].astype(f32) for t in out_terms[:3])

    mid_part = jnp.sum(d_normed_mid * mid_hat, axis=0)
    (in_part,) = tie((in_part,), late[2])
    layer_part = jnp.stack([in_part[0] / gain_in, mid_part]).reshape(2, n, groups, -1)
    layer_part = jnp.stack(relative([layer_part[:, :, t] for t in range(groups)], "tensor"))
    for bit in bits_of(groups):
        pairs = layer_part.reshape((layer_part.shape[0] // 2, 2) + layer_part.shape[1:])
        layer_part = pairs[:, 0] + flip_step(pairs[:, 1], "tensor", groups, bit)
    head_parts = split_last(head_part.reshape(2, heads, HD), n)
    rows = [
        jnp.concatenate([layer_part[0, :, k].reshape(-1), h.reshape(-1)])
        for k, h in enumerate(head_parts)
    ]
    rows = jnp.stack(relative(rows, "dp"))
    summed = flip_reduce_rows(rows, "dp", n)
    cut = 2 * (depth // groups)
    layer_grad = summed[:cut].reshape(2, depth // groups)
    head_grad = summed[cut:].reshape(2, heads, HD // n)

    return (
        mixed,
        input_grad,
        gate_grad,
        qkv_grad,
        out_weight_grad,
        head_grad,
        layer_grad,
        gu_grad,
        dn_grad,
    )


def solution(mesh):
    return jax.shard_map(
        per_device,
        mesh=mesh,
        in_specs=(
            P(("dp", "tensor"), None),
            P("dp", None),
            P(("dp", "tensor"), None),
            P(("dp", "tensor"), None),
            P(("dp", "tensor"), None),
            P(None, "dp", "tensor"),
            P("tensor", "dp"),
            P(None, "tensor", "dp"),
            P(None, "dp"),
            P(None, None, "dp", "tensor"),
            P(None, "tensor", "dp"),
        ),
        out_specs=(
            P(("dp", "tensor"), None),
            P(("dp", "tensor"), None),
            P(("dp", "tensor"), None),
            P(None, "dp", "tensor"),
            P("tensor", "dp"),
            P(None, "tensor", "dp"),
            P(None, ("dp", "tensor")),
            P(None, None, "dp", "tensor"),
            P(None, "tensor", "dp"),
        ),
        check_vma=False,
    )
```

```python
import functools

import jax
import jax.numpy as jnp
import numpy as np
from jax import lax
from jax.experimental import pallas as pl
from jax.experimental.pallas import tpu as pltpu
from jax.sharding import PartitionSpec as P

HD = 128
E = 16
EPSILON = 1e-05
ROPE_BASE = 10000.0
MASKED = -1e30
LANES = 128
CHUNKS = 4
VMEM_BYTES = 60 << 20

f32 = jnp.float32
bf16 = jnp.bfloat16
NT = (((1,), (1,)), ((), ()))
TN = (((0,), (0,)), ((), ()))
ANY = pl.BlockSpec(memory_space=pl.ANY)
SMEM = pl.BlockSpec(memory_space=pltpu.SMEM)
VMEM = pl.BlockSpec(memory_space=pltpu.VMEM)


def dot(a, b):
    return jnp.dot(a, b, preferred_element_type=f32)


def dot_nt(a, b):
    return lax.dot_general(a, b, NT, preferred_element_type=f32)


def dot_tn(a, b):
    return lax.dot_general(a, b, TN, preferred_element_type=f32)


def shape(dims, dtype):
    return jax.ShapeDtypeStruct(dims, dtype)


def ring_of(groups):
    return list(range(0, groups, 2)) + list(range(groups - 1, 0, -2))


def distances_of(groups):
    steps = groups // 2
    near = [s * k for k in range(steps - 1, 0, -1) for s in (1, -1)]
    return [steps] + near + [0]


def ring_step(value, groups, sign):
    ring = ring_of(groups)
    pairs = [(ring[p], ring[(p + sign) % groups]) for p in range(groups)]
    return lax.ppermute(value, "tensor", pairs)


def tie(values, after):
    values, after = tuple(values), tuple(after)
    return lax.optimization_barrier(values + after)[: len(values)]


class Gather:
    def __init__(self, own, groups):
        self.groups, self.steps = groups, groups // 2
        self.below, self.above = [own], [own]

    def step(self, after=()):
        low, high = self.below[-1], self.above[-1]
        if len(self.below) == self.steps:
            half = low.shape[0] // 2
            low, high = low[:half], high[half:]
        if after:
            low, high = tie((low, high), after)
        self.below.append(ring_step(low, self.groups, 1))
        self.above.append(ring_step(high, self.groups, -1))
        return [self.below[-1], self.above[-1]]

    def run(self):
        while len(self.below) <= self.steps:
            self.step()
        return self

    def at(self, distance):
        return self.above[distance] if distance >= 0 else self.below[-distance]

    def far(self):
        return [self.below[self.steps], self.above[self.steps]]

    def pieces(self):
        return self.far() + [self.at(k) for k in distances_of(self.groups)[1:]]


class Scatter:
    def __init__(self, pieces, groups):
        self.groups, self.steps, self.done = groups, groups // 2, 0
        self.far = pieces[:2]
        self.block = dict(zip(distances_of(groups)[1:], pieces[2:]))

    def step(self, after=(), riders=None):
        if self.done == 0:
            sent = self.far
        else:
            distance = self.steps - self.done
            low, high = (v.astype(f32) for v in self.moved)
            if self.done == 1:
                half = low.shape[0]
                low = jnp.pad(low, ((0, half), (0, 0)))
                high = jnp.pad(high, ((half, 0), (0, 0)))
            dtype = self.far[0].dtype
            low = (self.block[distance].astype(f32) + low).astype(dtype)
            high = (self.block[-distance].astype(f32) + high).astype(dtype)
            sent = [low, high]
        rows, columns = sent[0].shape
        if riders:
            riders = [jnp.pad(r, ((0, 0), (0, columns - r.shape[1]))) for r in riders]
            sent = [jnp.concatenate(pair, axis=0) for pair in zip(sent, riders)]
        if after:
            sent = tie(sent, after)
        self.moved = [ring_step(sent[0], self.groups, 1), ring_step(sent[1], self.groups, -1)]
        self.done += 1
        if riders:
            self.ridden = [m[rows:] for m in self.moved]
            self.moved = [m[:rows] for m in self.moved]
        return self.moved

    def run(self):
        while self.done < self.steps:
            self.step()
        return self

    def result(self):
        low, high = self.moved
        return self.block[0].astype(f32) + low.astype(f32) + high.astype(f32)


def bits_of(count):
    return [1 << b for b in range(count.bit_length() - 1)]


def flip_step(value, axis, count, bit):
    return lax.ppermute(value, axis, [(s, s ^ bit) for s in range(count)])


def relative(parts, axis):
    count = len(parts)
    index = lax.axis_index(axis)
    for bit in bits_of(count):
        turned = (index & bit) != 0
        parts = [jnp.where(turned, parts[k ^ bit], parts[k]) for k in range(count)]
    return parts


def split_last(value, count):
    width = value.shape[-1] // count
    return [value[..., k * width : (k + 1) * width] for k in range(count)]


def flip_reduce(keep, sent, axis, count):
    return flip_rest(keep, flip_step(sent, axis, count, 1), axis, count)


def flip_rest(keep, got, axis, count):
    for bit in bits_of(count)[1:]:
        odd = (keep[1::2].astype(f32) + got[1::2].astype(f32)).astype(bf16)
        more = flip_step(odd, axis, count, bit)
        if 2 * bit < count:
            keep = (keep[0::2].astype(f32) + got[0::2].astype(f32)).astype(bf16)
            got = more
    return [keep, got, more, odd]


def flip_reduce_rows(value, axis, count):
    for bit in bits_of(count):
        pairs = value.reshape((value.shape[0] // 2, 2) + value.shape[1:])
        value = pairs[:, 0] + flip_step(pairs[:, 1], axis, count, bit)
    return value[0]


def fetch(sources, target, sems, first, rows_at):
    copies = []
    for number, source in enumerate(sources):
        if source.shape[1] > target.shape[1]:
            source = source.at[:, pl.ds(0, target.shape[1])]
        copy = pltpu.make_async_copy(
            source, target.at[pl.ds(rows_at[number], source.shape[0])], sems.at[first + number]
        )
        copy.start()
        copies.append(copy)
    return copies


def load_projections(weights, wqs, sems, first):
    copies = []
    n, _, width = weights.shape
    depth = wqs.shape[0] // n
    for k in range(n):
        for j in range(3):
            source = weights.at[k, pl.ds(j * depth, depth)]
            target = wqs.at[pl.ds(k * depth, depth), pl.ds(j * width, width)]
            copies.append(pltpu.make_async_copy(source, target, sems.at[first + 3 * k + j]))
    return copies


def load_outputs(weights, wos, sems, first):
    copies = []
    n, _, width = weights.shape
    depth = wos.shape[1] // n
    cuts = max(1, depth // width)
    columns = depth // cuts
    for k in range(n):
        for c in range(cuts):
            source = weights.at[k, pl.ds(3 * depth + c * width, width), pl.ds(0, columns)]
            target = wos.at[:, pl.ds(k * depth + c * columns, columns)]
            copies.append(pltpu.make_async_copy(source, target, sems.at[first + cuts * k + c]))
    return copies


def output_copies(n, depth, width):
    return n * max(1, depth // width)


def piece_shapes(own_rows, columns, count):
    half = shape((own_rows // 2, columns), bf16)
    return [half, half] + [shape((own_rows, columns), bf16)] * (count - 2)


def cost(micros):
    return pl.CostEstimate(flops=int(micros * 6e8), bytes_accessed=1 << 20, transcendentals=0)


def piece_rows(order, half, pieces):
    rows = 2 * half
    starts = [pl.multiple_of(order[0] * rows, rows)]
    starts.append(pl.multiple_of(order[0] * rows + half, half))
    for number in range(2, pieces):
        starts.append(pl.multiple_of(order[number - 1] * rows, rows))
    return starts


def send_out(staged, targets, sems, first, starts):
    copies = []
    for number, target in enumerate(targets):
        copy = pltpu.make_async_copy(
            staged.at[pl.ds(starts[number], target.shape[0])], target, sems.at[first + number]
        )
        copy.start()
        copies.append(copy)
    return copies


def allowed_pairs(seg_col, seg_row, first, rows, width):
    row_pos = first + lax.broadcasted_iota(jnp.int32, (rows, width), 0)
    key_pos = lax.broadcasted_iota(jnp.int32, (rows, width), 1)
    return (seg_col[pl.ds(first, rows), :] == seg_row[:, pl.ds(0, width)]) & (key_pos <= row_pos)


def attn_proj_body(count, *refs):
    it = iter(refs)
    order = next(it)
    pieces = [next(it) for _ in range(count)]
    wq = next(it)
    gain, gains, cosine, sine = (next(it) for _ in range(4))
    q_o, k_o, v_o, qr_o, kr_o, x_o = (next(it) for _ in range(6))
    xs, wqs, sems = (next(it) for _ in range(3))
    block, width = q_o.shape
    heads = width // HD
    step = pl.program_id(0)

    @pl.when(step == 0)
    def _():
        starts = piece_rows(order, pieces[0].shape[0], count)
        copies = load_projections(wq, wqs, sems, count)
        for copy in copies:
            copy.start()
        for copy in fetch(pieces, xs, sems, 0, starts) + copies:
            copy.wait()

    wide = xs[pl.ds(pl.multiple_of(step * block, block), block), :].astype(f32)
    inv = lax.rsqrt(jnp.mean(wide * wide, axis=-1, keepdims=True) + EPSILON)
    x_o[...] = (wide * inv * gain[...]).astype(bf16)
    out = dot(x_o[...], wqs[...])
    v_o[...] = out[:, 2 * width :].astype(bf16)
    for j, (raw_o, hat_o) in enumerate(((qr_o, q_o), (kr_o, k_o))):
        raw = out[:, j * width : (j + 1) * width]
        raw_o[...] = raw
        for h in range(heads):
            cols = slice(h * HD, (h + 1) * HD)
            u = raw[:, cols]
            inv = lax.rsqrt(jnp.mean(u * u, axis=-1, keepdims=True) + EPSILON)
            u = u * inv * gains[j : j + 1, cols]
            u = u * cosine[...] + pltpu.roll(u, HD // 2, 1) * sine[...]
            hat_o[:, cols] = u.astype(bf16)


def attn_proj(order, pieces, wq, gain, gains, cosine, sine):
    n, count = wq.shape[0], len(pieces)
    d = gain.shape[1]
    length = cosine.shape[0]
    width = wq.shape[2]
    block = min(256, length)

    def rows(columns):
        return pl.BlockSpec((block, columns), lambda r: (r, 0))

    def whole(a):
        return pl.BlockSpec(a.shape, lambda r: (0, 0))

    return pl.pallas_call(
        functools.partial(attn_proj_body, count),
        grid=(length // block,),
        in_specs=[SMEM] + [ANY] * (count + 1) + [whole(gain), whole(gains), rows(HD), rows(HD)],
        out_specs=[rows(width)] * 5 + [rows(d)],
        out_shape=[shape((length, width), bf16)] * 3
        + [shape((length, width), f32)] * 2
        + [shape((length, d), bf16)],
        scratch_shapes=[
            pltpu.VMEM((length, d), bf16),
            pltpu.VMEM((d, 3 * width), bf16),
            pltpu.SemaphoreType.DMA((count + 3 * n,)),
        ],
        compiler_params=pltpu.CompilerParams(vmem_limit_bytes=VMEM_BYTES),
        cost_estimate=cost(10),
        name="attn_proj",
    )(order, *pieces, wq, gain, gains, cosine, sine)


def attn_core_body(count, block, *refs):
    it = iter(refs)
    order = next(it)
    wo = next(it)
    q, k_, v, seg_row, seg_col = (next(it) for _ in range(5))
    ctx_o, lse_o = next(it), next(it)
    outs = [next(it) for _ in range(count)]
    wos, stage, sems = (next(it) for _ in range(3))
    length, width = ctx_o.shape
    heads = width // HD
    starts = piece_rows(order, outs[0].shape[0], count)
    copies = load_outputs(wo, wos, sems, count)
    for copy in copies:
        copy.start()
    scale = HD ** (-0.5)
    for b in range(length // block):
        rows = pl.ds(b * block, block)
        hi = (b + 1) * block
        allowed = allowed_pairs(seg_col, seg_row, b * block, block, hi)
        for h in range(heads):
            cols = slice(h * HD, (h + 1) * HD)
            s = dot_nt(q[rows, cols], k_[pl.ds(0, hi), cols]) * scale
            s = jnp.where(allowed, s, MASKED)
            top = jnp.max(s, axis=-1, keepdims=True)
            e = jnp.exp(s - top)
            total = jnp.sum(e, axis=-1, keepdims=True)
            probs = (e * (1.0 / total)).astype(bf16)
            ctx_o[rows, cols] = dot(probs, v[pl.ds(0, hi), cols]).astype(bf16)
            lse_o[h, rows, :] = top + jnp.log(total)
    for copy in copies:
        copy.wait()
    stage[...] = dot(ctx_o[...], wos[...]).astype(bf16)
    for copy in send_out(stage, outs, sems, 0, starts):
        copy.wait()


def attn_core(order, wo, q, k, v, seg_row, seg_col, own_rows, d):
    n = wo.shape[0]
    length, width = q.shape
    count = length // own_rows + 1
    return pl.pallas_call(
        functools.partial(attn_core_body, count, min(256, length)),
        in_specs=[SMEM] + [ANY] + [VMEM] * 5,
        out_specs=[VMEM] * 2 + [ANY] * count,
        out_shape=[shape((length, width), bf16), shape((width // HD, length, 1), f32)]
        + piece_shapes(own_rows, d, count),
        scratch_shapes=[
            pltpu.VMEM((width, d), bf16),
            pltpu.VMEM((length, d), bf16),
            pltpu.SemaphoreType.DMA((count + output_copies(n, d // n, width),)),
        ],
        compiler_params=pltpu.CompilerParams(vmem_limit_bytes=VMEM_BYTES),
        cost_estimate=cost(10),
        name="attn_core",
    )(order, wo, q, k, v, seg_row, seg_col)


def attn_back_body(count, block, *refs):
    it = iter(refs)
    order = next(it)
    pieces = [next(it) for _ in range(count)]
    wo = next(it)
    q, k_, v, lse, seg_row, seg_col = (next(it) for _ in range(6))
    dq_o, dk_o, dv_o, db_o = (next(it) for _ in range(4))
    db, wos, dctx, sems = (next(it) for _ in range(4))
    length, width = q.shape
    heads = width // HD
    starts = piece_rows(order, pieces[0].shape[0], count)
    copies = load_outputs(wo, wos, sems, count)
    for copy in copies:
        copy.start()
    for copy in copies + fetch(pieces, db, sems, 0, starts):
        copy.wait()
    keep = pltpu.make_async_copy(db, db_o, sems.at[0])
    keep.start()
    scale = HD ** (-0.5)
    dctx[...] = dot_nt(db[...], wos[...]).astype(bf16)
    dk_o[...] = jnp.zeros_like(dk_o)
    dv_o[...] = jnp.zeros_like(dv_o)
    for b in range(length // block):
        rows = pl.ds(b * block, block)
        hi = (b + 1) * block
        low = pl.ds(0, hi)
        allowed = allowed_pairs(seg_col, seg_row, b * block, block, hi)
        for h in range(heads):
            cols = slice(h * HD, (h + 1) * HD)
            s = dot_nt(q[rows, cols], k_[low, cols]) * scale
            p = jnp.where(allowed, jnp.exp(s - lse[h, rows, :]), 0.0)
            g = dot_nt(dctx[rows, cols], v[low, cols])
            pg = p * g
            ds = (pg - p * jnp.sum(pg, axis=-1, keepdims=True)).astype(bf16)
            dq_o[rows, cols] = dot(ds, k_[low, cols]) * scale
            dk_o[low, cols] += dot_tn(ds, q[rows, cols]) * scale
            dv_o[low, cols] += dot_tn(p.astype(bf16), dctx[rows, cols])
    keep.wait()


def attn_back(order, pieces, wo, q, k, v, lse, seg_row, seg_col):
    n, count = wo.shape[0], len(pieces)
    d = pieces[0].shape[1]
    length, width = q.shape
    return pl.pallas_call(
        functools.partial(attn_back_body, count, min(256, length)),
        in_specs=[SMEM] + [ANY] * (count + 1) + [VMEM] * 6,
        out_specs=[VMEM] * 3 + [ANY],
        out_shape=[shape((length, width), f32)] * 3 + [shape((length, d), bf16)],
        scratch_shapes=[
            pltpu.VMEM((length, d), bf16),
            pltpu.VMEM((width, d), bf16),
            pltpu.VMEM((length, width), bf16),
            pltpu.SemaphoreType.DMA((count + output_copies(n, d // n, width),)),
        ],
        compiler_params=pltpu.CompilerParams(vmem_limit_bytes=VMEM_BYTES),
        cost_estimate=cost(14),
        name="attn_back",
    )(order, *pieces, wo, q, k, v, lse, seg_row, seg_col)


def proj_back_body(count, steps, *refs):
    it = iter(refs)
    order = next(it)
    wq = next(it)
    qr, kr, dq, dk, dv = (next(it) for _ in range(5))
    gains, cosine, sine, x = (next(it) for _ in range(4))
    dp_o, hg_o, gs_o = (next(it) for _ in range(3))
    outs = [next(it) for _ in range(count)]
    wqs, stage, sems = (next(it) for _ in range(3))
    block, width = qr.shape
    heads = width // HD
    step = pl.program_id(0)

    @pl.when(step == 0)
    def _():
        copies = load_projections(wq, wqs, sems, count)
        for copy in copies:
            copy.start()
        hg_o[...] = jnp.zeros_like(hg_o)
        gs_o[...] = jnp.zeros_like(gs_o)
        for copy in copies:
            copy.wait()

    dp_o[:, 2 * width :] = dv[...].astype(bf16)
    for j, (raw, grad) in enumerate(((qr, dq), (kr, dk))):
        for h in range(heads):
            cols = slice(h * HD, (h + 1) * HD)
            u = raw[:, cols]
            inv = lax.rsqrt(jnp.mean(u * u, axis=-1, keepdims=True) + EPSILON)
            hat = u * inv
            t = grad[:, cols]
            t = t * cosine[...] - pltpu.roll(t, HD // 2, 1) * sine[...]
            hg_o[j : j + 1, cols] += jnp.sum(t * hat, axis=0, keepdims=True)
            w = t * gains[j : j + 1, cols]
            w = inv * (w - hat * jnp.mean(w * hat, axis=-1, keepdims=True))
            dp_o[:, j * width + h * HD : j * width + (h + 1) * HD] = w.astype(bf16)
    out = dot_nt(dp_o[...], wqs[...])
    gs_o[...] += jnp.sum(out * x[...].astype(f32), axis=0, keepdims=True)
    stage[pl.ds(pl.multiple_of(step * block, block), block), :] = out.astype(bf16)

    @pl.when(step == steps - 1)
    def _():
        starts = piece_rows(order, outs[0].shape[0], count)
        for copy in send_out(stage, outs, sems, 0, starts):
            copy.wait()


def proj_back(order, wq, qr, kr, dq, dk, dv, gains, cosine, sine, x, own_rows):
    n = wq.shape[0]
    length, width = qr.shape
    d = x.shape[1]
    count = length // own_rows + 1
    block = min(256, length)
    steps = length // block

    def rows(columns):
        return pl.BlockSpec((block, columns), lambda r: (r, 0))

    def whole(dims):
        return pl.BlockSpec(dims, lambda r: (0, 0))

    return pl.pallas_call(
        functools.partial(proj_back_body, count, steps),
        grid=(steps,),
        in_specs=[SMEM, ANY]
        + [rows(width)] * 5
        + [whole(gains.shape), rows(HD), rows(HD), rows(d)],
        out_specs=[rows(3 * width), whole((2, width)), whole((1, d))] + [ANY] * count,
        out_shape=[
            shape((length, 3 * width), bf16),
            shape((2, width), f32),
            shape((1, d), f32),
        ]
        + piece_shapes(own_rows, d, count),
        scratch_shapes=[
            pltpu.VMEM((d, 3 * width), bf16),
            pltpu.VMEM((length, d), bf16),
            pltpu.SemaphoreType.DMA((count + 3 * n,)),
        ],
        compiler_params=pltpu.CompilerParams(vmem_limit_bytes=VMEM_BYTES),
        cost_estimate=cost(12),
        name="proj_back",
    )(order, wq, qr, kr, dq, dk, dv, gains, cosine, sine, x)


def attn_grad_body(places, xa, xb, dp, ctx, da, db, qkv_keep, qkv_send, out_keep, out_send):
    width = ctx.shape[1]
    for x, d, qkv_o, out_o in ((xa, da, qkv_keep, out_keep), (xb, db, qkv_send, out_send)):
        grad = dot_tn(x[...], dp[...])
        for j in range(3):
            qkv_o[0, j] = grad[:, j * width : (j + 1) * width].astype(bf16)
        out_o[0] = dot_tn(ctx[...], d[...]).astype(bf16)


def attn_grad(places, x, dp, ctx, db, n):
    length, d = x.shape
    width = ctx.shape[1]
    depth = d // n
    even = pl.BlockSpec((length, depth), lambda m, at: (0, at[2 * m]))
    odd = pl.BlockSpec((length, depth), lambda m, at: (0, at[2 * m + 1]))
    return pl.pallas_call(
        attn_grad_body,
        grid_spec=pltpu.PrefetchScalarGridSpec(
            num_scalar_prefetch=1,
            grid=(n // 2,),
            in_specs=[
                even,
                odd,
                pl.BlockSpec((length, 3 * width), lambda m, at: (0, 0)),
                pl.BlockSpec((length, width), lambda m, at: (0, 0)),
                even,
                odd,
            ],
            out_specs=[pl.BlockSpec((1, 3, depth, width), lambda m, at: (m, 0, 0, 0))] * 2
            + [pl.BlockSpec((1, width, depth), lambda m, at: (m, 0, 0))] * 2,
        ),
        out_shape=[shape((n // 2, 3, depth, width), bf16)] * 2
        + [shape((n // 2, width, depth), bf16)] * 2,
        compiler_params=pltpu.CompilerParams(vmem_limit_bytes=VMEM_BYTES),
        cost_estimate=cost(6),
        name="attn_grad",
    )(places, x, x, dp, ctx, db, db)


def flat_rows(pieces):
    starts, at = [], 0
    for piece in pieces:
        starts.append(at)
        at += piece.shape[0]
    return starts


def moe_in_body(count, *refs):
    xp, gu, out, xs, sems = refs[:count], *refs[count:]

    @pl.when(pl.program_id(0) == 0)
    def _():
        for copy in fetch(xp, xs, sems, 0, flat_rows(xp)):
            copy.wait()

    out[...] = dot(xs[...], gu[...]).astype(bf16)


def moe_in(xp, gate_up, group=4):
    count = len(xp)
    d, columns = gate_up.shape
    rows = sum(p.shape[0] for p in xp)
    wide = 2 * group * LANES
    return pl.pallas_call(
        functools.partial(moe_in_body, count),
        grid=(columns // wide,),
        in_specs=[ANY] * count + [pl.BlockSpec((d, wide), lambda s: (0, s))],
        out_specs=pl.BlockSpec((rows, wide), lambda s: (0, s)),
        out_shape=shape((rows, columns), bf16),
        scratch_shapes=[pltpu.VMEM((rows, d), bf16), pltpu.SemaphoreType.DMA((count,))],
        compiler_params=pltpu.CompilerParams(vmem_limit_bytes=VMEM_BYTES),
        cost_estimate=cost(rows * 0.02 + 4),
        name="moe_in",
    )(*xp, gate_up)


def moe_mid_body(group, steps, sets, count, *refs):
    it = iter(refs)
    gates = next(it)
    cp = [next(it) for _ in range(count)]
    gus = [next(it) for _ in range(sets)]
    gu_w, dn_w = next(it), next(it)
    d_outs = [next(it) for _ in range(count)]
    m_outs = [next(it) for _ in range(count)]
    dgu_o, hw_o = next(it), next(it)
    cs, d_acc, m_acc, gg, stage, sems = (next(it) for _ in range(6))
    d = cs.shape[1]
    fw = LANES
    step = pl.program_id(0)

    @pl.when(step == 0)
    def _():
        copies = fetch(cp, cs, sems, 0, flat_rows(cp))
        d_acc[...] = jnp.zeros_like(d_acc)
        m_acc[...] = jnp.zeros_like(m_acc)
        gg[...] = jnp.zeros_like(gg)
        for copy in copies:
            copy.wait()

    d_hid = dot_nt(cs[...], dn_w[...])
    at = 0
    for gu in gus:
        rows = gu.shape[0]
        here = pl.ds(at, rows)
        table = gates[here, :].astype(f32)
        lane = lax.broadcasted_iota(jnp.int32, table.shape, 1)
        total = jnp.zeros(table.shape, f32)
        for i in range(group):
            g = gu[:, 2 * i * fw : (2 * i + 1) * fw].astype(f32)
            u = gu[:, (2 * i + 1) * fw : (2 * i + 2) * fw].astype(f32)
            dh = d_hid[at : at + rows, i * fw : (i + 1) * fw]
            z = jax.nn.sigmoid(g)
            swish = g * z
            h = swish * u
            expert = step * group + i
            own = jnp.sum(h * dh, axis=1, keepdims=True)
            total = total + jnp.where(lane == expert, own, 0.0)
            gate = jnp.sum(jnp.where(lane == expert, table, 0.0), axis=1, keepdims=True)
            dw = dh * gate
            d_g = dw * u * z * (1.0 + g * (1.0 - z))
            hw_o[here, i * fw : (i + 1) * fw] = (h * gate).astype(bf16)
            dgu_o[here, 2 * i * fw : (2 * i + 1) * fw] = d_g.astype(bf16)
            dgu_o[here, (2 * i + 1) * fw : (2 * i + 2) * fw] = (dw * swish).astype(bf16)
        gg[here, :] += total
        at += rows
    d_acc[...] += dot_nt(dgu_o[...], gu_w[...])
    m_acc[...] += dot(hw_o[...], dn_w[...])

    @pl.when(step == steps - 1)
    def _():
        stage[:, pl.ds(0, d)] = d_acc[...].astype(bf16)
        stage[:, pl.ds(d, LANES)] = gg[...].astype(bf16)
        copies = send_out(stage, d_outs, sems, 0, flat_rows(d_outs))
        cs[...] = m_acc[...].astype(bf16)
        copies = copies + send_out(cs, m_outs, sems, count, flat_rows(m_outs))
        for copy in copies:
            copy.wait()


def moe_mid(gates, cp, gus, gate_up, down, group=4):
    count = len(cp)
    hidden, d = down.shape
    rows = sum(p.shape[0] for p in cp)
    half = group * LANES
    steps = hidden // half
    return pl.pallas_call(
        functools.partial(moe_mid_body, group, steps, len(gus), count),
        grid=(steps,),
        in_specs=[pl.BlockSpec((rows, LANES), lambda s: (0, 0))]
        + [ANY] * count
        + [pl.BlockSpec((g.shape[0], 2 * half), lambda s: (0, s)) for g in gus]
        + [
            pl.BlockSpec((d, 2 * half), lambda s: (0, s)),
            pl.BlockSpec((half, d), lambda s: (s, 0)),
        ],
        out_specs=[ANY] * (2 * count)
        + [
            pl.BlockSpec((rows, 2 * half), lambda s: (0, s)),
            pl.BlockSpec((rows, half), lambda s: (0, s)),
        ],
        out_shape=[shape((p.shape[0], d + LANES), bf16) for p in cp]
        + [shape(p.shape, bf16) for p in cp]
        + [shape((rows, 2 * hidden), bf16), shape((rows, hidden), bf16)],
        scratch_shapes=[
            pltpu.VMEM((rows, d), bf16),
            pltpu.VMEM((rows, d), f32),
            pltpu.VMEM((rows, d), f32),
            pltpu.VMEM((rows, LANES), f32),
            pltpu.VMEM((rows, d + LANES), bf16),
            pltpu.SemaphoreType.DMA((2 * count,)),
        ],
        compiler_params=pltpu.CompilerParams(vmem_limit_bytes=VMEM_BYTES),
        cost_estimate=cost(rows * 0.04 + 6),
        name="moe_mid",
    )(gates, *cp, *gus, gate_up, down)


def turn_body(count, *refs):
    pieces, out, xs, sems = refs[:count], refs[count], refs[count + 1], refs[count + 2]
    for copy in fetch(pieces, xs, sems, 0, flat_rows(pieces)):
        copy.wait()
    d = xs.shape[1]
    size = 256
    eye = (
        lax.broadcasted_iota(jnp.int32, (size, size), 0)
        == lax.broadcasted_iota(jnp.int32, (size, size), 1)
    ).astype(bf16)
    for at in range(0, d, size):
        out[pl.ds(at, size), :] = dot_nt(eye, xs[:, pl.ds(at, size)]).astype(bf16)


def turn_rows(pieces):
    count = len(pieces)
    length = sum(p.shape[0] for p in pieces)
    d = pieces[0].shape[1]
    return pl.pallas_call(
        functools.partial(turn_body, count),
        in_specs=[ANY] * count,
        out_specs=VMEM,
        out_shape=shape((d, length), bf16),
        scratch_shapes=[pltpu.VMEM((length, d), bf16), pltpu.SemaphoreType.DMA((count,))],
        compiler_params=pltpu.CompilerParams(vmem_limit_bytes=VMEM_BYTES),
        cost_estimate=cost(4),
        name="turn_rows",
    )(*pieces)


def in_grad_body(n, group, sets, places, xt, *refs):
    dgus = refs[:sets]
    *outs, xs, sems = refs[-4:]
    depth, fw = outs[0].shape[3:]
    step = pl.program_id(0)

    def part(k):
        source = xt.at[pl.ds(pl.multiple_of(places[k] * depth, depth), depth)]
        return pltpu.make_async_copy(source, xs.at[pl.ds(k * depth, depth)], sems.at[k])

    @pl.when(step == 0)
    def _():
        for k in range(n):
            part(k).start()

    dgu = jnp.concatenate([ref[...] for ref in dgus], axis=0)
    for k in range(n):

        @pl.when(step == 0)
        def _(k=k):
            part(k).wait()

        grad = dot(xs[pl.ds(k * depth, depth), :], dgu)
        for i in range(group):
            for g in range(2):
                at = (2 * i + g) * fw
                outs[k % 2][k // 2, i, g] = grad[:, at : at + fw].astype(bf16)


def in_grad(places, xt, dgus, n, experts, first, number, held, whole=None, group=2):
    d, length = xt.shape
    depth = d // n
    fw = dgus[0].shape[1] // (2 * experts)
    start = first // group
    at = (first % held) // group
    before = [] if whole is None else list(whole)
    sets = len(dgus)
    return list(
        pl.pallas_call(
            functools.partial(in_grad_body, n, group, sets),
            grid=(number // group,),
            in_specs=[SMEM, ANY]
            + [pl.BlockSpec((a.shape[0], 2 * group * fw), lambda s: (0, s + start)) for a in dgus]
            + [ANY] * len(before),
            out_specs=[pl.BlockSpec((n // 2, group, 2, depth, fw), lambda s: (0, at + s, 0, 0, 0))]
            * 2,
            out_shape=[shape((n // 2, held, 2, depth, fw), bf16)] * 2,
            input_output_aliases={2 + sets: 0, 3 + sets: 1} if before else {},
            scratch_shapes=[pltpu.VMEM((d, length), bf16), pltpu.SemaphoreType.DMA((n,))],
            compiler_params=pltpu.CompilerParams(vmem_limit_bytes=VMEM_BYTES),
            cost_estimate=cost(1.5 * number + 3),
            name="in_grad",
        )(places, xt, *dgus, *before)
    )


def out_grad_body(group, count, sets, *refs):
    hws, pieces = refs[:sets], refs[sets : sets + count]
    out, cs, sems = refs[-3:]
    fw = out.shape[1]

    @pl.when(pl.program_id(0) == 0)
    def _():
        for copy in fetch(pieces, cs, sems, 0, flat_rows(pieces)):
            copy.wait()

    turned = jnp.concatenate([ref[...] for ref in hws], axis=0).T
    grad = dot(turned, cs[...])
    for i in range(group):
        out[i] = grad[i * fw : (i + 1) * fw].astype(bf16)


def out_grad(hws, cp, experts, group=2):
    count = len(cp)
    length = sum(h.shape[0] for h in hws)
    d = cp[0].shape[1]
    fw = hws[0].shape[1] // experts
    return pl.pallas_call(
        functools.partial(out_grad_body, group, count, len(hws)),
        grid=(experts // group,),
        in_specs=[pl.BlockSpec((h.shape[0], group * fw), lambda s: (0, s)) for h in hws]
        + [ANY] * count,
        out_specs=pl.BlockSpec((group, fw, d), lambda s: (s, 0, 0)),
        out_shape=shape((experts, fw, d), bf16),
        scratch_shapes=[pltpu.VMEM((length, d), bf16), pltpu.SemaphoreType.DMA((count,))],
        compiler_params=pltpu.CompilerParams(vmem_limit_bytes=VMEM_BYTES),
        cost_estimate=cost(12),
        name="out_grad",
    )(*hws, *cp)


def finish_body(*refs):
    keep, got, more, out = refs[-4:]
    out[...] = keep[0].astype(f32) + got[0].astype(f32) + more[0].astype(f32)


def finish(whole, terms, experts, first):
    number = terms[0].shape[1]
    rest = terms[0].shape[2:]
    zeros = (0,) * len(rest)
    before = [] if whole is None else [whole]
    each = 2
    at = first // each
    return pl.pallas_call(
        finish_body,
        grid=(number // each,),
        in_specs=[ANY] * len(before)
        + [pl.BlockSpec((1, each) + rest, lambda s: (0, s) + zeros)] * 3,
        out_specs=pl.BlockSpec((each,) + rest, lambda s: (at + s,) + zeros),
        out_shape=shape((experts,) + rest, f32),
        input_output_aliases={0: 0} if before else {},
        compiler_params=pltpu.CompilerParams(vmem_limit_bytes=VMEM_BYTES),
        cost_estimate=cost(2),
        name="finish",
    )(*before, *terms)


def place_body(*refs):
    part, out = refs[-2:]
    out[...] = part[...].astype(f32)


def place(part, experts, whole=None):
    rest = part.shape[1:]
    zeros = (0,) * len(rest)
    before = [] if whole is None else [whole]
    return pl.pallas_call(
        place_body,
        grid=(part.shape[0] // 4,),
        in_specs=[ANY] * len(before) + [pl.BlockSpec((4,) + rest, lambda s: (s,) + zeros)],
        out_specs=pl.BlockSpec((4,) + rest, lambda s: (s,) + zeros),
        out_shape=shape((experts,) + rest, f32),
        input_output_aliases={0: 0} if before else {},
        compiler_params=pltpu.CompilerParams(vmem_limit_bytes=VMEM_BYTES),
        cost_estimate=cost(3),
        name="place",
    )(*before, part)


def pack_body(w, out):
    fw = w.shape[3]
    for i in range(w.shape[0]):
        for g in range(2):
            at = (2 * i + g) * fw
            out[:, at : at + fw] = w[i, g]


def pack(gate_up, group=2):
    experts, _, depth, fw = gate_up.shape
    return pl.pallas_call(
        pack_body,
        grid=(experts // group,),
        in_specs=[pl.BlockSpec((group, 2, depth, fw), lambda s: (s, 0, 0, 0))],
        out_specs=pl.BlockSpec((depth, 2 * group * fw), lambda s: (0, s)),
        out_shape=shape((depth, 2 * experts * fw), bf16),
        compiler_params=pltpu.CompilerParams(vmem_limit_bytes=VMEM_BYTES),
        cost_estimate=cost(4),
        name="pack",
    )(gate_up)


def rope_tables(length):
    positions = np.arange(length, dtype=np.float32)
    power = -np.arange(HD // 2, dtype=np.float32) * np.float32(2.0) / np.float32(HD)
    inverse_freq = np.power(np.float32(ROPE_BASE), power)
    phases = positions[:, None] * inverse_freq[None, :]
    cosine, sine = np.cos(phases), np.sin(phases)
    tables = [cosine, cosine], [-sine, sine]
    return [np.concatenate(t, axis=-1).astype(np.float32) for t in tables]


def per_device(
    tokens,
    segments,
    routes,
    gate_values,
    cotangent,
    query_key_value,
    out_weight,
    head_gain,
    layer_gain,
    gate_up,
    down_weight,
):
    groups = lax.axis_size("tensor")
    n = lax.axis_size("dp")
    own_rows, d = tokens.shape
    seq_len = own_rows * groups
    heads = query_key_value.shape[2] // HD
    experts = gate_up.shape[0]
    depth = d // n
    steps = groups // 2
    top = routes.shape[1]

    x = tokens.astype(f32)
    routed = jnp.concatenate([routes.astype(bf16), gate_values], axis=1)
    routed = jnp.pad(routed, ((0, 0), (0, LANES - 2 * top)))
    normed = Gather(jnp.concatenate([tokens, routed], axis=1), groups)
    first = normed.step()

    width = query_key_value.shape[2]
    small = jnp.concatenate([layer_gain.reshape(-1), head_gain.reshape(-1)])
    size = small.shape[0]
    small = jnp.pad(small, (0, -size % (16 * width))).reshape(-1, width)
    outward = split_last(out_weight, max(1, depth // width))
    outward = [jnp.pad(a, ((0, 0), (0, width - a.shape[1]))) for a in outward]
    own = [query_key_value.reshape(-1, width)] + outward + [small]
    attn_weights = lax.all_gather(jnp.concatenate(own, axis=0), "dp", axis=0)

    ring = ring_of(groups)
    orders = [[ring[(ring.index(t) + k) % groups] for k in distances_of(groups)] for t in range(groups)]
    orders = jnp.array(orders, jnp.int32)
    order = lax.dynamic_slice(orders, (lax.axis_index("tensor"), 0), (1, groups)).reshape(groups)
    places = jnp.array([[i ^ k for k in range(n)] for i in range(n)], jnp.int32)
    places = lax.dynamic_slice(places, (lax.axis_index("dp"), 0), (1, n)).reshape(n)
    cosine, sine = rope_tables(seq_len)
    seg_row = segments.reshape(1, seq_len)
    seg_col = segments.reshape(seq_len, 1)
    expert_ids = jnp.arange(experts, dtype=jnp.int32)
    chosen = routes[:, :, None] == expert_ids
    (gate_up,) = tie((gate_up,), first)
    packed = pack(gate_up)

    done = normed.step()
    (packed,) = tie((packed,), done)
    gu = lax.all_gather(packed, "dp", axis=0, tiled=True)
    normed.step(after=[packed])
    normed.step()
    cut = 2 * depth
    small = [w[-small.shape[0] :].reshape(-1)[:size] for w in attn_weights]
    gain = jnp.concatenate([s[:cut].reshape(2, depth) for s in small], axis=1).astype(f32)
    gain_in, gain_mid = gain[0], gain[1]
    head_parts = [s[cut:].reshape(2, heads, HD // n) for s in small]
    gain_head = jnp.concatenate(head_parts, axis=2).reshape(2, heads * HD).astype(f32)
    pieces = normed.pieces()
    inv_in = lax.rsqrt(jnp.mean(x * x, axis=-1, keepdims=True) + EPSILON)
    x_hat = x * inv_in
    q, k, v, q_raw, k_raw, normed_all = attn_proj(
        order, pieces, attn_weights, gain_in[None, :], gain_head, cosine, sine
    )
    d_pieces = Gather(cotangent, groups)
    first = d_pieces.step(after=pieces)
    q, k, v = tie((q, k, v), first)
    context, lse, *attn = attn_core(
        order, attn_weights, q, k, v, seg_row, seg_col, own_rows, d
    )
    second = d_pieces.step(after=[q])
    routed = jnp.concatenate([p[:, d : d + 2 * top] for p in pieces], axis=0)
    named = routed[:, :top].astype(jnp.int32)[:, :, None] == expert_ids
    gate_table = jnp.sum(jnp.where(named, routed[:, top:].astype(f32)[:, :, None], 0.0), axis=1)
    gate_table = jnp.pad(gate_table.astype(bf16), ((0, 0), (0, LANES - experts)))
    attention = Scatter(attn, groups)
    done = attention.step(after=second)
    (down,) = tie((down_weight.reshape(-1, depth),), done)
    dn = lax.all_gather(down, "dp", axis=1, tiled=True)
    middle = x + attention.run().result()
    inv_mid = lax.rsqrt(jnp.mean(middle * middle, axis=-1, keepdims=True) + EPSILON)
    mid_hat = middle * inv_mid
    mid = Gather((mid_hat * gain_mid).astype(bf16), groups)

    hidden_in = []
    mid.step()
    for s in range(1, steps - 1):
        here = [mid.at(s), mid.at(-s)] + ([mid.at(0)] if s == 1 else [])
        mid.step(after=hidden_in[-1:])
        hidden_in.append(moe_in(here, gu))
    mid.step(after=hidden_in[-1:])
    normed_mid = mid.pieces()
    taken = normed_mid[:4]
    hidden_in.append(moe_in(taken, gu))
    d_pieces.step(after=taken)
    d_pieces.step(after=hidden_in[-1:])
    d_pieces = d_pieces.pieces()

    half_rows = hidden_in[-1].shape[0]
    d_far, d_near = d_pieces[:4], d_pieces[4:]
    far_out = list(moe_mid(gate_table[:half_rows], d_far, hidden_in[-1:], gu, dn))
    d_mid, moe, d_in, hidden = far_out[:4], far_out[4:8], far_out[8:9], far_out[9:]
    (mid_far,) = tie(normed_mid[:1], d_mid[:1])
    mid_turned = turn_rows([mid_far] + normed_mid[1:])
    d_normed = Scatter(d_mid, groups)
    done = d_normed.step()
    mixing = Scatter(moe, groups)
    second = d_normed.step(after=[mid_turned], riders=mixing.far)
    mixing.done, mixing.moved = 1, [m[:, :d] for m in d_normed.ridden]
    (table,) = tie((gate_table[half_rows:],), done + [mid_turned])
    near_out = list(moe_mid(table, d_near, hidden_in[:-1][::-1], gu, dn))
    count = len(d_near)
    d_mid, moe = d_mid + near_out[:count], moe + near_out[count : 2 * count]
    d_in, hidden = d_in + near_out[2 * count : -1], hidden + near_out[-1:]
    d_normed.block = dict(zip(distances_of(groups)[1:], d_mid[2:]))
    mixing.block = dict(zip(distances_of(groups)[1:], moe[2:]))
    third = d_normed.step(after=moe[-1:])

    (hidden_far,) = tie(hidden[:1], second + near_out[:1])
    dn_all = out_grad([hidden_far] + hidden[1:], d_pieces, experts)
    (ready,) = tie((dn_all,), third)
    dn_grad = lax.psum_scatter(ready, "dp", scatter_dimension=2, tiled=True)
    fourth = d_normed.step(after=[dn_all])

    def gradient(c, after, whole=None):
        (turned,) = tie((mid_turned,), after)
        return in_grad(places, turned, d_in, n, experts, c * each, each, 2 * each, whole)

    each = experts // CHUNKS
    low = gradient(0, third)
    d_normed_mid = d_normed.result()
    gate_sum = d_normed_mid[:, d:]
    d_normed_mid = d_normed_mid[:, :d]
    d_mid_hat = d_normed_mid * gain_mid
    d_middle = cotangent.astype(f32) + inv_mid * (
        d_mid_hat - mid_hat * jnp.mean(d_mid_hat * mid_hat, axis=-1, keepdims=True)
    )
    branch = Gather(d_middle.astype(bf16), groups)
    moved = branch.step(after=low)
    low = gradient(1, [d_middle], low)
    moved_on = branch.step(after=low)
    low_keep, low_send = low[0], tie(low[1:], moved)[0]
    low_terms = flip_reduce(low_keep, low_send, "dp", n)
    high = gradient(2, moved)
    moved = branch.step(after=high + low_terms[3:])
    high = gradient(3, moved_on, high)
    branch.step(after=high)
    high_keep, high_send = high[0], tie(high[1:], moved)[0]
    high_terms = flip_reduce(high_keep, high_send, "dp", n)
    d_branch = branch.pieces()

    moe_second = mixing.step(after=d_branch + high_terms[3:])
    dq, dk, dv, d_branch_all = attn_back(
        order, d_branch, attn_weights, q, k, v, lse, seg_row, seg_col
    )
    dq, dk, dv = tie((dq, dk, dv), moe_second)
    moe_third = mixing.step()
    d_projected, head_part, in_part, *to_rows = proj_back(
        order, attn_weights, q_raw, k_raw, dq, dk, dv, gain_head, cosine, sine, normed_all, own_rows
    )
    d_normed = Scatter(to_rows, groups)
    late = [d_normed.step(after=moe_third + low_terms[2:3])]
    (projected,) = tie((d_projected,), late[0])
    qkv_keep, qkv_send, out_keep, out_send = attn_grad(
        places, normed_all, projected, context, d_branch_all, n
    )
    late.append(d_normed.step())
    qkv_send, out_send = tie((qkv_send, out_send), late[1])
    qkv_terms = flip_reduce(qkv_keep, qkv_send, "dp", n)
    out_terms = flip_reduce(out_keep, out_send, "dp", n)
    (dn_grad,) = tie((dn_grad,), late[0])
    dn_grad = place(dn_grad, experts)
    late.append(
        d_normed.step(after=[qkv_keep, dn_grad])
    )

    (late_low,) = tie(low_terms[2:3], late[1])
    gu_grad = finish(None, low_terms[:2] + [late_low], experts, 0)
    late.append(d_normed.step(after=[gu_grad] + qkv_terms[3:] + out_terms[3:] + high_terms[2:3]))
    (late_high,) = tie(high_terms[2:3], late[3])
    gu_grad = finish(gu_grad, high_terms[:2] + [late_high], experts, 2 * each)
    late.append(mixing.step(after=late[3]))
    qkv_terms = qkv_terms[:2] + list(tie(qkv_terms[2:3], late[4]))
    d_normed_in = d_normed.result()
    d_x_hat = d_normed_in * gain_in
    input_grad = d_middle + inv_in * (
        d_x_hat - x_hat * jnp.mean(d_x_hat * x_hat, axis=-1, keepdims=True)
    )
    mixed = (middle + mixing.result()).astype(bf16)
    gate_grad = jnp.sum(jnp.where(chosen, gate_sum[:, None, :experts], 0.0), axis=-1)
    out_terms = out_terms[:2] + list(tie(out_terms[2:3], late[4]))
    qkv_grad = sum(t[0].astype(f32) for t in qkv_terms[:3])
    out_weight_grad = sum(t[0].astype(f32) for t in out_terms[:3])

    mid_part = jnp.sum(d_normed_mid * mid_hat, axis=0)
    (in_part,) = tie((in_part,), late[2])
    layer_part = jnp.stack([in_part[0] / gain_in, mid_part]).reshape(2, n, groups, -1)
    layer_part = jnp.stack(relative([layer_part[:, :, t] for t in range(groups)], "tensor"))
    for bit in bits_of(groups):
        pairs = layer_part.reshape((layer_part.shape[0] // 2, 2) + layer_part.shape[1:])
        layer_part = pairs[:, 0] + flip_step(pairs[:, 1], "tensor", groups, bit)
    head_parts = split_last(head_part.reshape(2, heads, HD), n)
    rows = [
        jnp.concatenate([layer_part[0, :, k].reshape(-1), h.reshape(-1)])
        for k, h in enumerate(head_parts)
    ]
    rows = jnp.stack(relative(rows, "dp"))
    summed = flip_reduce_rows(rows, "dp", n)
    cut = 2 * (depth // groups)
    layer_grad = summed[:cut].reshape(2, depth // groups)
    head_grad = summed[cut:].reshape(2, heads, HD // n)

    return (
        mixed,
        input_grad,
        gate_grad,
        qkv_grad,
        out_weight_grad,
        head_grad,
        layer_grad,
        gu_grad,
        dn_grad,
    )


def solution(mesh):
    return jax.shard_map(
        per_device,
        mesh=mesh,
        in_specs=(
            P(("dp", "tensor"), None),
            P("dp", None),
            P(("dp", "tensor"), None),
            P(("dp", "tensor"), None),
            P(("dp", "tensor"), None),
            P(None, "dp", "tensor"),
            P("tensor", "dp"),
            P(None, "tensor", "dp"),
            P(None, "dp"),
            P(None, None, "dp", "tensor"),
            P(None, "tensor", "dp"),
        ),
        out_specs=(
            P(("dp", "tensor"), None),
            P(("dp", "tensor"), None),
            P(("dp", "tensor"), None),
            P(None, "dp", "tensor"),
            P("tensor", "dp"),
            P(None, "tensor", "dp"),
            P(None, ("dp", "tensor")),
            P(None, None, "dp", "tensor"),
            P(None, "tensor", "dp"),
        ),
        check_vma=False,
    )
```

```python
import functools

import jax
import jax.numpy as jnp
import numpy as np
from jax import lax
from jax.experimental import pallas as pl
from jax.experimental.pallas import tpu as pltpu
from jax.sharding import PartitionSpec as P

HD = 128
E = 16
EPSILON = 1e-05
ROPE_BASE = 10000.0
MASKED = -1e30
LANES = 128
CHUNKS = 4
VMEM_BYTES = 60 << 20

f32 = jnp.float32
bf16 = jnp.bfloat16
NT = (((1,), (1,)), ((), ()))
TN = (((0,), (0,)), ((), ()))
ANY = pl.BlockSpec(memory_space=pl.ANY)
SMEM = pl.BlockSpec(memory_space=pltpu.SMEM)
VMEM = pl.BlockSpec(memory_space=pltpu.VMEM)


def dot(a, b):
    return jnp.dot(a, b, preferred_element_type=f32)


def dot_nt(a, b):
    return lax.dot_general(a, b, NT, preferred_element_type=f32)


def dot_tn(a, b):
    return lax.dot_general(a, b, TN, preferred_element_type=f32)


def shape(dims, dtype):
    return jax.ShapeDtypeStruct(dims, dtype)


def ring_of(groups):
    return list(range(0, groups, 2)) + list(range(groups - 1, 0, -2))


def distances_of(groups):
    steps = groups // 2
    near = [s * k for k in range(steps - 1, 0, -1) for s in (1, -1)]
    return [steps] + near + [0]


def ring_step(value, groups, sign):
    ring = ring_of(groups)
    pairs = [(ring[p], ring[(p + sign) % groups]) for p in range(groups)]
    return lax.ppermute(value, "tensor", pairs)


def tie(values, after):
    values, after = tuple(values), tuple(after)
    return lax.optimization_barrier(values + after)[: len(values)]


class Gather:
    def __init__(self, own, groups):
        self.groups, self.steps = groups, groups // 2
        self.below, self.above = [own], [own]

    def step(self, after=()):
        low, high = self.below[-1], self.above[-1]
        if len(self.below) == self.steps:
            half = low.shape[0] // 2
            low, high = low[:half], high[half:]
        if after:
            low, high = tie((low, high), after)
        self.below.append(ring_step(low, self.groups, 1))
        self.above.append(ring_step(high, self.groups, -1))
        return [self.below[-1], self.above[-1]]

    def run(self):
        while len(self.below) <= self.steps:
            self.step()
        return self

    def at(self, distance):
        return self.above[distance] if distance >= 0 else self.below[-distance]

    def far(self):
        return [self.below[self.steps], self.above[self.steps]]

    def pieces(self):
        return self.far() + [self.at(k) for k in distances_of(self.groups)[1:]]


class Scatter:
    def __init__(self, pieces, groups):
        self.groups, self.steps, self.done = groups, groups // 2, 0
        self.far = pieces[:2]
        self.block = dict(zip(distances_of(groups)[1:], pieces[2:]))

    def step(self, after=(), riders=None):
        if self.done == 0:
            sent = self.far
        else:
            distance = self.steps - self.done
            low, high = (v.astype(f32) for v in self.moved)
            if self.done == 1:
                half = low.shape[0]
                low = jnp.pad(low, ((0, half), (0, 0)))
                high = jnp.pad(high, ((half, 0), (0, 0)))
            dtype = self.far[0].dtype
            low = (self.block[distance].astype(f32) + low).astype(dtype)
            high = (self.block[-distance].astype(f32) + high).astype(dtype)
            sent = [low, high]
        rows, columns = sent[0].shape
        if riders:
            riders = [jnp.pad(r, ((0, 0), (0, columns - r.shape[1]))) for r in riders]
            sent = [jnp.concatenate(pair, axis=0) for pair in zip(sent, riders)]
        if after:
            sent = tie(sent, after)
        self.moved = [ring_step(sent[0], self.groups, 1), ring_step(sent[1], self.groups, -1)]
        self.done += 1
        if riders:
            self.ridden = [m[rows:] for m in self.moved]
            self.moved = [m[:rows] for m in self.moved]
        return self.moved

    def run(self):
        while self.done < self.steps:
            self.step()
        return self

    def result(self):
        low, high = self.moved
        return self.block[0].astype(f32) + low.astype(f32) + high.astype(f32)


def bits_of(count):
    return [1 << b for b in range(count.bit_length() - 1)]


def flip_step(value, axis, count, bit):
    return lax.ppermute(value, axis, [(s, s ^ bit) for s in range(count)])


def relative(parts, axis):
    count = len(parts)
    index = lax.axis_index(axis)
    for bit in bits_of(count):
        turned = (index & bit) != 0
        parts = [jnp.where(turned, parts[k ^ bit], parts[k]) for k in range(count)]
    return parts


def split_last(value, count):
    width = value.shape[-1] // count
    return [value[..., k * width : (k + 1) * width] for k in range(count)]


def flip_reduce(keep, sent, axis, count):
    return flip_rest(keep, flip_step(sent, axis, count, 1), axis, count)


def flip_rest(keep, got, axis, count):
    for bit in bits_of(count)[1:]:
        odd = (keep[1::2].astype(f32) + got[1::2].astype(f32)).astype(bf16)
        more = flip_step(odd, axis, count, bit)
        if 2 * bit < count:
            keep = (keep[0::2].astype(f32) + got[0::2].astype(f32)).astype(bf16)
            got = more
    return [keep, got, more, odd]


def flip_reduce_rows(value, axis, count):
    for bit in bits_of(count):
        pairs = value.reshape((value.shape[0] // 2, 2) + value.shape[1:])
        value = pairs[:, 0] + flip_step(pairs[:, 1], axis, count, bit)
    return value[0]


def fetch(sources, target, sems, first, rows_at):
    copies = []
    for number, source in enumerate(sources):
        if source.shape[1] > target.shape[1]:
            source = source.at[:, pl.ds(0, target.shape[1])]
        copy = pltpu.make_async_copy(
            source, target.at[pl.ds(rows_at[number], source.shape[0])], sems.at[first + number]
        )
        copy.start()
        copies.append(copy)
    return copies


def load_projections(weights, wqs, sems, first):
    copies = []
    n, _, width = weights.shape
    depth = wqs.shape[0] // n
    for k in range(n):
        for j in range(3):
            source = weights.at[k, pl.ds(j * depth, depth)]
            target = wqs.at[pl.ds(k * depth, depth), pl.ds(j * width, width)]
            copies.append(pltpu.make_async_copy(source, target, sems.at[first + 3 * k + j]))
    return copies


def load_outputs(weights, wos, sems, first):
    copies = []
    n, _, width = weights.shape
    depth = wos.shape[1] // n
    cuts = max(1, depth // width)
    columns = depth // cuts
    for k in range(n):
        for c in range(cuts):
            source = weights.at[k, pl.ds(3 * depth + c * width, width), pl.ds(0, columns)]
            target = wos.at[:, pl.ds(k * depth + c * columns, columns)]
            copies.append(pltpu.make_async_copy(source, target, sems.at[first + cuts * k + c]))
    return copies


def output_copies(n, depth, width):
    return n * max(1, depth // width)


def piece_shapes(own_rows, columns, count):
    half = shape((own_rows // 2, columns), bf16)
    return [half, half] + [shape((own_rows, columns), bf16)] * (count - 2)


def cost(micros):
    return pl.CostEstimate(flops=int(micros * 6e8), bytes_accessed=1 << 20, transcendentals=0)


def piece_rows(order, half, pieces):
    rows = 2 * half
    starts = [pl.multiple_of(order[0] * rows, rows)]
    starts.append(pl.multiple_of(order[0] * rows + half, half))
    for number in range(2, pieces):
        starts.append(pl.multiple_of(order[number - 1] * rows, rows))
    return starts


def send_out(staged, targets, sems, first, starts):
    copies = []
    for number, target in enumerate(targets):
        copy = pltpu.make_async_copy(
            staged.at[pl.ds(starts[number], target.shape[0])], target, sems.at[first + number]
        )
        copy.start()
        copies.append(copy)
    return copies


def allowed_pairs(seg_col, seg_row, first, rows, width):
    row_pos = first + lax.broadcasted_iota(jnp.int32, (rows, width), 0)
    key_pos = lax.broadcasted_iota(jnp.int32, (rows, width), 1)
    return (seg_col[pl.ds(first, rows), :] == seg_row[:, pl.ds(0, width)]) & (key_pos <= row_pos)


def attn_proj_body(count, *refs):
    it = iter(refs)
    order = next(it)
    pieces = [next(it) for _ in range(count)]
    wq = next(it)
    gain, gains, cosine, sine = (next(it) for _ in range(4))
    q_o, k_o, v_o, qr_o, kr_o, x_o = (next(it) for _ in range(6))
    xs, wqs, sems = (next(it) for _ in range(3))
    block, width = q_o.shape
    heads = width // HD
    step = pl.program_id(0)

    @pl.when(step == 0)
    def _():
        starts = piece_rows(order, pieces[0].shape[0], count)
        copies = load_projections(wq, wqs, sems, count)
        for copy in copies:
            copy.start()
        for copy in fetch(pieces, xs, sems, 0, starts) + copies:
            copy.wait()

    wide = xs[pl.ds(pl.multiple_of(step * block, block), block), :].astype(f32)
    inv = lax.rsqrt(jnp.mean(wide * wide, axis=-1, keepdims=True) + EPSILON)
    x_o[...] = (wide * inv * gain[...]).astype(bf16)
    out = dot(x_o[...], wqs[...])
    v_o[...] = out[:, 2 * width :].astype(bf16)
    for j, (raw_o, hat_o) in enumerate(((qr_o, q_o), (kr_o, k_o))):
        raw = out[:, j * width : (j + 1) * width]
        raw_o[...] = raw
        for h in range(heads):
            cols = slice(h * HD, (h + 1) * HD)
            u = raw[:, cols]
            inv = lax.rsqrt(jnp.mean(u * u, axis=-1, keepdims=True) + EPSILON)
            u = u * inv * gains[j : j + 1, cols]
            u = u * cosine[...] + pltpu.roll(u, HD // 2, 1) * sine[...]
            hat_o[:, cols] = u.astype(bf16)


def attn_proj(order, pieces, wq, gain, gains, cosine, sine):
    n, count = wq.shape[0], len(pieces)
    d = gain.shape[1]
    length = cosine.shape[0]
    width = wq.shape[2]
    block = min(256, length)

    def rows(columns):
        return pl.BlockSpec((block, columns), lambda r: (r, 0))

    def whole(a):
        return pl.BlockSpec(a.shape, lambda r: (0, 0))

    return pl.pallas_call(
        functools.partial(attn_proj_body, count),
        grid=(length // block,),
        in_specs=[SMEM] + [ANY] * (count + 1) + [whole(gain), whole(gains), rows(HD), rows(HD)],
        out_specs=[rows(width)] * 5 + [rows(d)],
        out_shape=[shape((length, width), bf16)] * 3
        + [shape((length, width), f32)] * 2
        + [shape((length, d), bf16)],
        scratch_shapes=[
            pltpu.VMEM((length, d), bf16),
            pltpu.VMEM((d, 3 * width), bf16),
            pltpu.SemaphoreType.DMA((count + 3 * n,)),
        ],
        compiler_params=pltpu.CompilerParams(vmem_limit_bytes=VMEM_BYTES),
        cost_estimate=cost(10),
        name="attn_proj",
    )(order, *pieces, wq, gain, gains, cosine, sine)


def attn_core_body(count, block, *refs):
    it = iter(refs)
    order = next(it)
    wo = next(it)
    q, k_, v, seg_row, seg_col = (next(it) for _ in range(5))
    ctx_o, lse_o = next(it), next(it)
    outs = [next(it) for _ in range(count)]
    wos, stage, sems = (next(it) for _ in range(3))
    length, width = ctx_o.shape
    heads = width // HD
    starts = piece_rows(order, outs[0].shape[0], count)
    copies = load_outputs(wo, wos, sems, count)
    for copy in copies:
        copy.start()
    scale = HD ** (-0.5)
    for b in range(length // block):
        rows = pl.ds(b * block, block)
        hi = (b + 1) * block
        allowed = allowed_pairs(seg_col, seg_row, b * block, block, hi)
        for h in range(heads):
            cols = slice(h * HD, (h + 1) * HD)
            s = dot_nt(q[rows, cols], k_[pl.ds(0, hi), cols]) * scale
            s = jnp.where(allowed, s, MASKED)
            top = jnp.max(s, axis=-1, keepdims=True)
            e = jnp.exp(s - top)
            total = jnp.sum(e, axis=-1, keepdims=True)
            probs = (e * (1.0 / total)).astype(bf16)
            ctx_o[rows, cols] = dot(probs, v[pl.ds(0, hi), cols]).astype(bf16)
            lse_o[h, rows, :] = top + jnp.log(total)
    for copy in copies:
        copy.wait()
    stage[...] = dot(ctx_o[...], wos[...]).astype(bf16)
    for copy in send_out(stage, outs, sems, 0, starts):
        copy.wait()


def attn_core(order, wo, q, k, v, seg_row, seg_col, own_rows, d):
    n = wo.shape[0]
    length, width = q.shape
    count = length // own_rows + 1
    return pl.pallas_call(
        functools.partial(attn_core_body, count, min(256, length)),
        in_specs=[SMEM] + [ANY] + [VMEM] * 5,
        out_specs=[VMEM] * 2 + [ANY] * count,
        out_shape=[shape((length, width), bf16), shape((width // HD, length, 1), f32)]
        + piece_shapes(own_rows, d, count),
        scratch_shapes=[
            pltpu.VMEM((width, d), bf16),
            pltpu.VMEM((length, d), bf16),
            pltpu.SemaphoreType.DMA((count + output_copies(n, d // n, width),)),
        ],
        compiler_params=pltpu.CompilerParams(vmem_limit_bytes=VMEM_BYTES),
        cost_estimate=cost(10),
        name="attn_core",
    )(order, wo, q, k, v, seg_row, seg_col)


def attn_back_body(count, block, *refs):
    it = iter(refs)
    order = next(it)
    pieces = [next(it) for _ in range(count)]
    wo = next(it)
    q, k_, v, lse, seg_row, seg_col = (next(it) for _ in range(6))
    dq_o, dk_o, dv_o, db_o = (next(it) for _ in range(4))
    db, wos, dctx, sems = (next(it) for _ in range(4))
    length, width = q.shape
    heads = width // HD
    starts = piece_rows(order, pieces[0].shape[0], count)
    copies = load_outputs(wo, wos, sems, count)
    for copy in copies:
        copy.start()
    for copy in copies + fetch(pieces, db, sems, 0, starts):
        copy.wait()
    keep = pltpu.make_async_copy(db, db_o, sems.at[0])
    keep.start()
    scale = HD ** (-0.5)
    dctx[...] = dot_nt(db[...], wos[...]).astype(bf16)
    dk_o[...] = jnp.zeros_like(dk_o)
    dv_o[...] = jnp.zeros_like(dv_o)
    for b in range(length // block):
        rows = pl.ds(b * block, block)
        hi = (b + 1) * block
        low = pl.ds(0, hi)
        allowed = allowed_pairs(seg_col, seg_row, b * block, block, hi)
        for h in range(heads):
            cols = slice(h * HD, (h + 1) * HD)
            s = dot_nt(q[rows, cols], k_[low, cols]) * scale
            p = jnp.where(allowed, jnp.exp(s - lse[h, rows, :]), 0.0)
            g = dot_nt(dctx[rows, cols], v[low, cols])
            pg = p * g
            ds = (pg - p * jnp.sum(pg, axis=-1, keepdims=True)).astype(bf16)
            dq_o[rows, cols] = dot(ds, k_[low, cols]) * scale
            dk_o[low, cols] += dot_tn(ds, q[rows, cols]) * scale
            dv_o[low, cols] += dot_tn(p.astype(bf16), dctx[rows, cols])
    keep.wait()


def attn_back(order, pieces, wo, q, k, v, lse, seg_row, seg_col):
    n, count = wo.shape[0], len(pieces)
    d = pieces[0].shape[1]
    length, width = q.shape
    return pl.pallas_call(
        functools.partial(attn_back_body, count, min(256, length)),
        in_specs=[SMEM] + [ANY] * (count + 1) + [VMEM] * 6,
        out_specs=[VMEM] * 3 + [ANY],
        out_shape=[shape((length, width), f32)] * 3 + [shape((length, d), bf16)],
        scratch_shapes=[
            pltpu.VMEM((length, d), bf16),
            pltpu.VMEM((width, d), bf16),
            pltpu.VMEM((length, width), bf16),
            pltpu.SemaphoreType.DMA((count + output_copies(n, d // n, width),)),
        ],
        compiler_params=pltpu.CompilerParams(vmem_limit_bytes=VMEM_BYTES),
        cost_estimate=cost(14),
        name="attn_back",
    )(order, *pieces, wo, q, k, v, lse, seg_row, seg_col)


def proj_back_body(count, steps, *refs):
    it = iter(refs)
    order = next(it)
    wq = next(it)
    qr, kr, dq, dk, dv = (next(it) for _ in range(5))
    gains, cosine, sine, x = (next(it) for _ in range(4))
    dp_o, hg_o, gs_o = (next(it) for _ in range(3))
    outs = [next(it) for _ in range(count)]
    wqs, stage, sems = (next(it) for _ in range(3))
    block, width = qr.shape
    heads = width // HD
    step = pl.program_id(0)

    @pl.when(step == 0)
    def _():
        copies = load_projections(wq, wqs, sems, count)
        for copy in copies:
            copy.start()
        hg_o[...] = jnp.zeros_like(hg_o)
        gs_o[...] = jnp.zeros_like(gs_o)
        for copy in copies:
            copy.wait()

    dp_o[:, 2 * width :] = dv[...].astype(bf16)
    for j, (raw, grad) in enumerate(((qr, dq), (kr, dk))):
        for h in range(heads):
            cols = slice(h * HD, (h + 1) * HD)
            u = raw[:, cols]
            inv = lax.rsqrt(jnp.mean(u * u, axis=-1, keepdims=True) + EPSILON)
            hat = u * inv
            t = grad[:, cols]
            t = t * cosine[...] - pltpu.roll(t, HD // 2, 1) * sine[...]
            hg_o[j : j + 1, cols] += jnp.sum(t * hat, axis=0, keepdims=True)
            w = t * gains[j : j + 1, cols]
            w = inv * (w - hat * jnp.mean(w * hat, axis=-1, keepdims=True))
            dp_o[:, j * width + h * HD : j * width + (h + 1) * HD] = w.astype(bf16)
    out = dot_nt(dp_o[...], wqs[...])
    gs_o[...] += jnp.sum(out * x[...].astype(f32), axis=0, keepdims=True)
    stage[pl.ds(pl.multiple_of(step * block, block), block), :] = out.astype(bf16)

    @pl.when(step == steps - 1)
    def _():
        starts = piece_rows(order, outs[0].shape[0], count)
        for copy in send_out(stage, outs, sems, 0, starts):
            copy.wait()


def proj_back(order, wq, qr, kr, dq, dk, dv, gains, cosine, sine, x, own_rows):
    n = wq.shape[0]
    length, width = qr.shape
    d = x.shape[1]
    count = length // own_rows + 1
    block = min(256, length)
    steps = length // block

    def rows(columns):
        return pl.BlockSpec((block, columns), lambda r: (r, 0))

    def whole(dims):
        return pl.BlockSpec(dims, lambda r: (0, 0))

    return pl.pallas_call(
        functools.partial(proj_back_body, count, steps),
        grid=(steps,),
        in_specs=[SMEM, ANY]
        + [rows(width)] * 5
        + [whole(gains.shape), rows(HD), rows(HD), rows(d)],
        out_specs=[rows(3 * width), whole((2, width)), whole((1, d))] + [ANY] * count,
        out_shape=[
            shape((length, 3 * width), bf16),
            shape((2, width), f32),
            shape((1, d), f32),
        ]
        + piece_shapes(own_rows, d, count),
        scratch_shapes=[
            pltpu.VMEM((d, 3 * width), bf16),
            pltpu.VMEM((length, d), bf16),
            pltpu.SemaphoreType.DMA((count + 3 * n,)),
        ],
        compiler_params=pltpu.CompilerParams(vmem_limit_bytes=VMEM_BYTES),
        cost_estimate=cost(12),
        name="proj_back",
    )(order, wq, qr, kr, dq, dk, dv, gains, cosine, sine, x)


def attn_grad_body(places, xa, xb, dp, ctx, da, db, qkv_keep, qkv_send, out_keep, out_send):
    width = ctx.shape[1]
    for x, d, qkv_o, out_o in ((xa, da, qkv_keep, out_keep), (xb, db, qkv_send, out_send)):
        grad = dot_tn(x[...], dp[...])
        for j in range(3):
            qkv_o[0, j] = grad[:, j * width : (j + 1) * width].astype(bf16)
        out_o[0] = dot_tn(ctx[...], d[...]).astype(bf16)


def attn_grad(places, x, dp, ctx, db, n):
    length, d = x.shape
    width = ctx.shape[1]
    depth = d // n
    even = pl.BlockSpec((length, depth), lambda m, at: (0, at[2 * m]))
    odd = pl.BlockSpec((length, depth), lambda m, at: (0, at[2 * m + 1]))
    return pl.pallas_call(
        attn_grad_body,
        grid_spec=pltpu.PrefetchScalarGridSpec(
            num_scalar_prefetch=1,
            grid=(n // 2,),
            in_specs=[
                even,
                odd,
                pl.BlockSpec((length, 3 * width), lambda m, at: (0, 0)),
                pl.BlockSpec((length, width), lambda m, at: (0, 0)),
                even,
                odd,
            ],
            out_specs=[pl.BlockSpec((1, 3, depth, width), lambda m, at: (m, 0, 0, 0))] * 2
            + [pl.BlockSpec((1, width, depth), lambda m, at: (m, 0, 0))] * 2,
        ),
        out_shape=[shape((n // 2, 3, depth, width), bf16)] * 2
        + [shape((n // 2, width, depth), bf16)] * 2,
        compiler_params=pltpu.CompilerParams(vmem_limit_bytes=VMEM_BYTES),
        cost_estimate=cost(6),
        name="attn_grad",
    )(places, x, x, dp, ctx, db, db)


def flat_rows(pieces):
    starts, at = [], 0
    for piece in pieces:
        starts.append(at)
        at += piece.shape[0]
    return starts


def held(piece):
    return pl.BlockSpec(piece.shape, lambda s: (0, 0))


def stacked(pieces):
    return jnp.concatenate([piece[...] for piece in pieces], axis=0)


def moe_in_body(count, *refs):
    xp, gu, out = refs[:count], *refs[count:]
    out[...] = dot(stacked(xp), gu[...]).astype(bf16)


def moe_in(xp, gate_up, group=4):
    count = len(xp)
    d, columns = gate_up.shape
    rows = sum(p.shape[0] for p in xp)
    wide = 2 * group * LANES
    return pl.pallas_call(
        functools.partial(moe_in_body, count),
        grid=(columns // wide,),
        in_specs=[held(p) for p in xp] + [pl.BlockSpec((d, wide), lambda s: (0, s))],
        out_specs=pl.BlockSpec((rows, wide), lambda s: (0, s)),
        out_shape=shape((rows, columns), bf16),
        compiler_params=pltpu.CompilerParams(vmem_limit_bytes=VMEM_BYTES),
        cost_estimate=cost(rows * 0.02 + 4),
        name="moe_in",
    )(*xp, gate_up)


def moe_mid_body(group, steps, sets, count, *refs):
    it = iter(refs)
    gates = next(it)
    cp = [next(it) for _ in range(count)]
    gus = [next(it) for _ in range(sets)]
    gu_w, dn_w = next(it), next(it)
    d_outs = [next(it) for _ in range(count)]
    m_outs = [next(it) for _ in range(count)]
    dgu_o, hw_o = next(it), next(it)
    cs, d_acc, m_acc, gg, stage, sems = (next(it) for _ in range(6))
    d = cs.shape[1]
    fw = LANES
    step = pl.program_id(0)

    @pl.when(step == 0)
    def _():
        d_acc[...] = jnp.zeros_like(d_acc)
        m_acc[...] = jnp.zeros_like(m_acc)
        gg[...] = jnp.zeros_like(gg)

    d_hid = dot_nt(stacked(cp), dn_w[...])
    at = 0
    for gu in gus:
        rows = gu.shape[0]
        here = pl.ds(at, rows)
        table = gates[here, :].astype(f32)
        lane = lax.broadcasted_iota(jnp.int32, table.shape, 1)
        total = jnp.zeros(table.shape, f32)
        for i in range(group):
            g = gu[:, 2 * i * fw : (2 * i + 1) * fw].astype(f32)
            u = gu[:, (2 * i + 1) * fw : (2 * i + 2) * fw].astype(f32)
            dh = d_hid[at : at + rows, i * fw : (i + 1) * fw]
            z = jax.nn.sigmoid(g)
            swish = g * z
            h = swish * u
            expert = step * group + i
            own = jnp.sum(h * dh, axis=1, keepdims=True)
            total = total + jnp.where(lane == expert, own, 0.0)
            gate = jnp.sum(jnp.where(lane == expert, table, 0.0), axis=1, keepdims=True)
            dw = dh * gate
            d_g = dw * u * z * (1.0 + g * (1.0 - z))
            hw_o[here, i * fw : (i + 1) * fw] = (h * gate).astype(bf16)
            dgu_o[here, 2 * i * fw : (2 * i + 1) * fw] = d_g.astype(bf16)
            dgu_o[here, (2 * i + 1) * fw : (2 * i + 2) * fw] = (dw * swish).astype(bf16)
        gg[here, :] += total
        at += rows
    d_acc[...] += dot_nt(dgu_o[...], gu_w[...])
    m_acc[...] += dot(hw_o[...], dn_w[...])

    @pl.when(step == steps - 1)
    def _():
        stage[:, pl.ds(0, d)] = d_acc[...].astype(bf16)
        stage[:, pl.ds(d, LANES)] = gg[...].astype(bf16)
        copies = send_out(stage, d_outs, sems, 0, flat_rows(d_outs))
        cs[...] = m_acc[...].astype(bf16)
        copies = copies + send_out(cs, m_outs, sems, count, flat_rows(m_outs))
        for copy in copies:
            copy.wait()


def moe_mid(gates, cp, gus, gate_up, down, group=4):
    count = len(cp)
    hidden, d = down.shape
    rows = sum(p.shape[0] for p in cp)
    half = group * LANES
    steps = hidden // half
    return pl.pallas_call(
        functools.partial(moe_mid_body, group, steps, len(gus), count),
        grid=(steps,),
        in_specs=[pl.BlockSpec((rows, LANES), lambda s: (0, 0))]
        + [held(p) for p in cp]
        + [pl.BlockSpec((g.shape[0], 2 * half), lambda s: (0, s)) for g in gus]
        + [
            pl.BlockSpec((d, 2 * half), lambda s: (0, s)),
            pl.BlockSpec((half, d), lambda s: (s, 0)),
        ],
        out_specs=[ANY] * (2 * count)
        + [
            pl.BlockSpec((rows, 2 * half), lambda s: (0, s)),
            pl.BlockSpec((rows, half), lambda s: (0, s)),
        ],
        out_shape=[shape((p.shape[0], d + LANES), bf16) for p in cp]
        + [shape(p.shape, bf16) for p in cp]
        + [shape((rows, 2 * hidden), bf16), shape((rows, hidden), bf16)],
        scratch_shapes=[
            pltpu.VMEM((rows, d), bf16),
            pltpu.VMEM((rows, d), f32),
            pltpu.VMEM((rows, d), f32),
            pltpu.VMEM((rows, LANES), f32),
            pltpu.VMEM((rows, d + LANES), bf16),
            pltpu.SemaphoreType.DMA((2 * count,)),
        ],
        compiler_params=pltpu.CompilerParams(vmem_limit_bytes=VMEM_BYTES),
        cost_estimate=cost(rows * 0.04 + 6),
        name="moe_mid",
    )(gates, *cp, *gus, gate_up, down)


def turn_body(count, *refs):
    pieces, out, xs, sems = refs[:count], refs[count], refs[count + 1], refs[count + 2]
    for copy in fetch(pieces, xs, sems, 0, flat_rows(pieces)):
        copy.wait()
    d = xs.shape[1]
    size = 256
    eye = (
        lax.broadcasted_iota(jnp.int32, (size, size), 0)
        == lax.broadcasted_iota(jnp.int32, (size, size), 1)
    ).astype(bf16)
    for at in range(0, d, size):
        out[pl.ds(at, size), :] = dot_nt(eye, xs[:, pl.ds(at, size)]).astype(bf16)


def turn_rows(pieces):
    count = len(pieces)
    length = sum(p.shape[0] for p in pieces)
    d = pieces[0].shape[1]
    return pl.pallas_call(
        functools.partial(turn_body, count),
        in_specs=[ANY] * count,
        out_specs=VMEM,
        out_shape=shape((d, length), bf16),
        scratch_shapes=[pltpu.VMEM((length, d), bf16), pltpu.SemaphoreType.DMA((count,))],
        compiler_params=pltpu.CompilerParams(vmem_limit_bytes=VMEM_BYTES),
        cost_estimate=cost(4),
        name="turn_rows",
    )(*pieces)


def in_grad_body(n, group, sets, places, xt, *refs):
    dgus = refs[:sets]
    *outs, xs, sems = refs[-4:]
    depth, fw = outs[0].shape[3:]
    step = pl.program_id(0)

    def part(k):
        source = xt.at[pl.ds(pl.multiple_of(places[k] * depth, depth), depth)]
        return pltpu.make_async_copy(source, xs.at[pl.ds(k * depth, depth)], sems.at[k])

    @pl.when(step == 0)
    def _():
        for k in range(n):
            part(k).start()

    dgu = jnp.concatenate([ref[...] for ref in dgus], axis=0)
    for k in range(n):

        @pl.when(step == 0)
        def _(k=k):
            part(k).wait()

        grad = dot(xs[pl.ds(k * depth, depth), :], dgu)
        for i in range(group):
            for g in range(2):
                at = (2 * i + g) * fw
                outs[k % 2][k // 2, i, g] = grad[:, at : at + fw].astype(bf16)


def in_grad(places, xt, dgus, n, experts, first, number, held, whole=None, group=2):
    d, length = xt.shape
    depth = d // n
    fw = dgus[0].shape[1] // (2 * experts)
    start = first // group
    at = (first % held) // group
    before = [] if whole is None else list(whole)
    sets = len(dgus)
    return list(
        pl.pallas_call(
            functools.partial(in_grad_body, n, group, sets),
            grid=(number // group,),
            in_specs=[SMEM, ANY]
            + [pl.BlockSpec((a.shape[0], 2 * group * fw), lambda s: (0, s + start)) for a in dgus]
            + [ANY] * len(before),
            out_specs=[pl.BlockSpec((n // 2, group, 2, depth, fw), lambda s: (0, at + s, 0, 0, 0))]
            * 2,
            out_shape=[shape((n // 2, held, 2, depth, fw), bf16)] * 2,
            input_output_aliases={2 + sets: 0, 3 + sets: 1} if before else {},
            scratch_shapes=[pltpu.VMEM((d, length), bf16), pltpu.SemaphoreType.DMA((n,))],
            compiler_params=pltpu.CompilerParams(vmem_limit_bytes=VMEM_BYTES),
            cost_estimate=cost(1.5 * number + 3),
            name="in_grad",
        )(places, xt, *dgus, *before)
    )


def out_grad_body(group, count, sets, *refs):
    hws, pieces = refs[:sets], refs[sets : sets + count]
    out, cs, sems = refs[-3:]
    fw = out.shape[1]

    @pl.when(pl.program_id(0) == 0)
    def _():
        for copy in fetch(pieces, cs, sems, 0, flat_rows(pieces)):
            copy.wait()

    turned = jnp.concatenate([ref[...] for ref in hws], axis=0).T
    grad = dot(turned, cs[...])
    for i in range(group):
        out[i] = grad[i * fw : (i + 1) * fw].astype(bf16)


def out_grad(hws, cp, experts, group=2):
    count = len(cp)
    length = sum(h.shape[0] for h in hws)
    d = cp[0].shape[1]
    fw = hws[0].shape[1] // experts
    return pl.pallas_call(
        functools.partial(out_grad_body, group, count, len(hws)),
        grid=(experts // group,),
        in_specs=[pl.BlockSpec((h.shape[0], group * fw), lambda s: (0, s)) for h in hws]
        + [ANY] * count,
        out_specs=pl.BlockSpec((group, fw, d), lambda s: (s, 0, 0)),
        out_shape=shape((experts, fw, d), bf16),
        scratch_shapes=[pltpu.VMEM((length, d), bf16), pltpu.SemaphoreType.DMA((count,))],
        compiler_params=pltpu.CompilerParams(vmem_limit_bytes=VMEM_BYTES),
        cost_estimate=cost(12),
        name="out_grad",
    )(*hws, *cp)


def finish_body(*refs):
    keep, got, more, out = refs[-4:]
    out[...] = keep[0].astype(f32) + got[0].astype(f32) + more[0].astype(f32)


def finish(whole, terms, experts, first):
    number = terms[0].shape[1]
    rest = terms[0].shape[2:]
    zeros = (0,) * len(rest)
    before = [] if whole is None else [whole]
    each = 2
    at = first // each
    return pl.pallas_call(
        finish_body,
        grid=(number // each,),
        in_specs=[ANY] * len(before)
        + [pl.BlockSpec((1, each) + rest, lambda s: (0, s) + zeros)] * 3,
        out_specs=pl.BlockSpec((each,) + rest, lambda s: (at + s,) + zeros),
        out_shape=shape((experts,) + rest, f32),
        input_output_aliases={0: 0} if before else {},
        compiler_params=pltpu.CompilerParams(vmem_limit_bytes=VMEM_BYTES),
        cost_estimate=cost(2),
        name="finish",
    )(*before, *terms)


def place_body(*refs):
    part, out = refs[-2:]
    out[...] = part[...].astype(f32)


def place(part, experts, whole=None):
    rest = part.shape[1:]
    zeros = (0,) * len(rest)
    before = [] if whole is None else [whole]
    return pl.pallas_call(
        place_body,
        grid=(part.shape[0] // 4,),
        in_specs=[ANY] * len(before) + [pl.BlockSpec((4,) + rest, lambda s: (s,) + zeros)],
        out_specs=pl.BlockSpec((4,) + rest, lambda s: (s,) + zeros),
        out_shape=shape((experts,) + rest, f32),
        input_output_aliases={0: 0} if before else {},
        compiler_params=pltpu.CompilerParams(vmem_limit_bytes=VMEM_BYTES),
        cost_estimate=cost(3),
        name="place",
    )(*before, part)


def pack_body(w, out):
    fw = w.shape[3]
    for i in range(w.shape[0]):
        for g in range(2):
            at = (2 * i + g) * fw
            out[:, at : at + fw] = w[i, g]


def pack(gate_up, group=4):
    experts, _, depth, fw = gate_up.shape
    return pl.pallas_call(
        pack_body,
        grid=(experts // group,),
        in_specs=[pl.BlockSpec((group, 2, depth, fw), lambda s: (s, 0, 0, 0))],
        out_specs=pl.BlockSpec((depth, 2 * group * fw), lambda s: (0, s)),
        out_shape=shape((depth, 2 * experts * fw), bf16),
        compiler_params=pltpu.CompilerParams(vmem_limit_bytes=VMEM_BYTES),
        cost_estimate=cost(4),
        name="pack",
    )(gate_up)


def rope_tables(length):
    positions = np.arange(length, dtype=np.float32)
    power = -np.arange(HD // 2, dtype=np.float32) * np.float32(2.0) / np.float32(HD)
    inverse_freq = np.power(np.float32(ROPE_BASE), power)
    phases = positions[:, None] * inverse_freq[None, :]
    cosine, sine = np.cos(phases), np.sin(phases)
    tables = [cosine, cosine], [-sine, sine]
    return [np.concatenate(t, axis=-1).astype(np.float32) for t in tables]


def per_device(
    tokens,
    segments,
    routes,
    gate_values,
    cotangent,
    query_key_value,
    out_weight,
    head_gain,
    layer_gain,
    gate_up,
    down_weight,
):
    groups = lax.axis_size("tensor")
    n = lax.axis_size("dp")
    own_rows, d = tokens.shape
    seq_len = own_rows * groups
    heads = query_key_value.shape[2] // HD
    experts = gate_up.shape[0]
    depth = d // n
    steps = groups // 2
    top = routes.shape[1]

    x = tokens.astype(f32)
    routed = jnp.concatenate([routes.astype(bf16), gate_values], axis=1)
    routed = jnp.pad(routed, ((0, 0), (0, LANES - 2 * top)))
    normed = Gather(jnp.concatenate([tokens, routed], axis=1), groups)
    first = normed.step()

    width = query_key_value.shape[2]
    small = jnp.concatenate([layer_gain.reshape(-1), head_gain.reshape(-1)])
    size = small.shape[0]
    small = jnp.pad(small, (0, -size % (16 * width))).reshape(-1, width)
    outward = split_last(out_weight, max(1, depth // width))
    outward = [jnp.pad(a, ((0, 0), (0, width - a.shape[1]))) for a in outward]
    own = [query_key_value.reshape(-1, width)] + outward + [small]
    attn_weights = lax.all_gather(jnp.concatenate(own, axis=0), "dp", axis=0)

    ring = ring_of(groups)
    orders = [[ring[(ring.index(t) + k) % groups] for k in distances_of(groups)] for t in range(groups)]
    orders = jnp.array(orders, jnp.int32)
    order = lax.dynamic_slice(orders, (lax.axis_index("tensor"), 0), (1, groups)).reshape(groups)
    places = jnp.array([[i ^ k for k in range(n)] for i in range(n)], jnp.int32)
    places = lax.dynamic_slice(places, (lax.axis_index("dp"), 0), (1, n)).reshape(n)
    cosine, sine = rope_tables(seq_len)
    seg_row = segments.reshape(1, seq_len)
    seg_col = segments.reshape(seq_len, 1)
    expert_ids = jnp.arange(experts, dtype=jnp.int32)
    chosen = routes[:, :, None] == expert_ids
    (gate_up,) = tie((gate_up,), first)
    packed = pack(gate_up)

    done = normed.step()
    (packed,) = tie((packed,), done)
    gu = lax.all_gather(packed, "dp", axis=0, tiled=True)
    normed.step(after=[packed])
    normed.step()
    cut = 2 * depth
    small = [w[-small.shape[0] :].reshape(-1)[:size] for w in attn_weights]
    gain = jnp.concatenate([s[:cut].reshape(2, depth) for s in small], axis=1).astype(f32)
    gain_in, gain_mid = gain[0], gain[1]
    head_parts = [s[cut:].reshape(2, heads, HD // n) for s in small]
    gain_head = jnp.concatenate(head_parts, axis=2).reshape(2, heads * HD).astype(f32)
    pieces = normed.pieces()
    inv_in = lax.rsqrt(jnp.mean(x * x, axis=-1, keepdims=True) + EPSILON)
    x_hat = x * inv_in
    q, k, v, q_raw, k_raw, normed_all = attn_proj(
        order, pieces, attn_weights, gain_in[None, :], gain_head, cosine, sine
    )
    d_pieces = Gather(cotangent, groups)
    first = d_pieces.step(after=pieces)
    q, k, v = tie((q, k, v), first)
    context, lse, *attn = attn_core(
        order, attn_weights, q, k, v, seg_row, seg_col, own_rows, d
    )
    second = d_pieces.step(after=[q])
    routed = jnp.concatenate([p[:, d : d + 2 * top] for p in pieces], axis=0)
    named = routed[:, :top].astype(jnp.int32)[:, :, None] == expert_ids
    gate_table = jnp.sum(jnp.where(named, routed[:, top:].astype(f32)[:, :, None], 0.0), axis=1)
    gate_table = jnp.pad(gate_table.astype(bf16), ((0, 0), (0, LANES - experts)))
    attention = Scatter(attn, groups)
    done = attention.step(after=second)
    (down,) = tie((down_weight.reshape(-1, depth),), done)
    dn = lax.all_gather(down, "dp", axis=1, tiled=True)
    middle = x + attention.run().result()
    inv_mid = lax.rsqrt(jnp.mean(middle * middle, axis=-1, keepdims=True) + EPSILON)
    mid_hat = middle * inv_mid
    mid = Gather((mid_hat * gain_mid).astype(bf16), groups)

    hidden_in = []
    mid.step()
    for s in range(1, steps - 1):
        here = [mid.at(s), mid.at(-s)] + ([mid.at(0)] if s == 1 else [])
        mid.step(after=hidden_in[-1:])
        hidden_in.append(moe_in(here, gu))
    mid.step(after=hidden_in[-1:])
    normed_mid = mid.pieces()
    taken = normed_mid[:4]
    hidden_in.append(moe_in(taken, gu))
    d_pieces.step(after=taken)
    d_pieces.step(after=hidden_in[-1:])
    d_pieces = d_pieces.pieces()

    half_rows = hidden_in[-1].shape[0]
    d_far, d_near = d_pieces[:4], d_pieces[4:]
    far_out = list(moe_mid(gate_table[:half_rows], d_far, hidden_in[-1:], gu, dn))
    d_mid, moe, d_in, hidden = far_out[:4], far_out[4:8], far_out[8:9], far_out[9:]
    (mid_far,) = tie(normed_mid[:1], d_mid[:1])
    mid_turned = turn_rows([mid_far] + normed_mid[1:])
    d_normed = Scatter(d_mid, groups)
    done = d_normed.step()
    mixing = Scatter(moe, groups)
    second = d_normed.step(after=[mid_turned], riders=mixing.far)
    mixing.done, mixing.moved = 1, [m[:, :d] for m in d_normed.ridden]
    (table,) = tie((gate_table[half_rows:],), done + [mid_turned])
    near_out = list(moe_mid(table, d_near, hidden_in[:-1][::-1], gu, dn))
    count = len(d_near)
    d_mid, moe = d_mid + near_out[:count], moe + near_out[count : 2 * count]
    d_in, hidden = d_in + near_out[2 * count : -1], hidden + near_out[-1:]
    d_normed.block = dict(zip(distances_of(groups)[1:], d_mid[2:]))
    mixing.block = dict(zip(distances_of(groups)[1:], moe[2:]))
    third = d_normed.step(after=moe[-1:])

    (hidden_far,) = tie(hidden[:1], second + near_out[:1])
    dn_all = out_grad([hidden_far] + hidden[1:], d_pieces, experts)
    (ready,) = tie((dn_all,), third)
    dn_grad = lax.psum_scatter(ready, "dp", scatter_dimension=2, tiled=True)
    fourth = d_normed.step(after=[dn_all])

    def gradient(c, after, whole=None):
        (turned,) = tie((mid_turned,), after)
        return in_grad(places, turned, d_in, n, experts, c * each, each, 2 * each, whole)

    each = experts // CHUNKS
    low = gradient(0, third)
    d_normed_mid = d_normed.result()
    gate_sum = d_normed_mid[:, d:]
    d_normed_mid = d_normed_mid[:, :d]
    d_mid_hat = d_normed_mid * gain_mid
    d_middle = cotangent.astype(f32) + inv_mid * (
        d_mid_hat - mid_hat * jnp.mean(d_mid_hat * mid_hat, axis=-1, keepdims=True)
    )
    branch = Gather(d_middle.astype(bf16), groups)
    moved = branch.step(after=low)
    low = gradient(1, [d_middle], low)
    moved_on = branch.step(after=low)
    low_keep, low_send = low[0], tie(low[1:], moved)[0]
    low_terms = flip_reduce(low_keep, low_send, "dp", n)
    high = gradient(2, moved)
    moved = branch.step(after=high + low_terms[3:])
    high = gradient(3, moved_on, high)
    branch.step(after=high)
    high_keep, high_send = high[0], tie(high[1:], moved)[0]
    high_terms = flip_reduce(high_keep, high_send, "dp", n)
    d_branch = branch.pieces()

    moe_second = mixing.step(after=d_branch + high_terms[3:])
    dq, dk, dv, d_branch_all = attn_back(
        order, d_branch, attn_weights, q, k, v, lse, seg_row, seg_col
    )
    dq, dk, dv = tie((dq, dk, dv), moe_second)
    moe_third = mixing.step()
    d_projected, head_part, in_part, *to_rows = proj_back(
        order, attn_weights, q_raw, k_raw, dq, dk, dv, gain_head, cosine, sine, normed_all, own_rows
    )
    d_normed = Scatter(to_rows, groups)
    late = [d_normed.step(after=moe_third + low_terms[2:3])]
    (projected,) = tie((d_projected,), late[0])
    qkv_keep, qkv_send, out_keep, out_send = attn_grad(
        places, normed_all, projected, context, d_branch_all, n
    )
    late.append(d_normed.step())
    qkv_send, out_send = tie((qkv_send, out_send), late[1])
    qkv_terms = flip_reduce(qkv_keep, qkv_send, "dp", n)
    out_terms = flip_reduce(out_keep, out_send, "dp", n)
    (dn_grad,) = tie((dn_grad,), late[0])
    dn_grad = place(dn_grad, experts)
    late.append(
        d_normed.step(after=[qkv_keep, dn_grad])
    )

    (late_low,) = tie(low_terms[2:3], late[1])
    gu_grad = finish(None, low_terms[:2] + [late_low], experts, 0)
    late.append(d_normed.step(after=[gu_grad] + qkv_terms[3:] + out_terms[3:] + high_terms[2:3]))
    (late_high,) = tie(high_terms[2:3], late[3])
    gu_grad = finish(gu_grad, high_terms[:2] + [late_high], experts, 2 * each)
    late.append(mixing.step(after=late[3]))
    qkv_terms = qkv_terms[:2] + list(tie(qkv_terms[2:3], late[4]))
    d_normed_in = d_normed.result()
    d_x_hat = d_normed_in * gain_in
    input_grad = d_middle + inv_in * (
        d_x_hat - x_hat * jnp.mean(d_x_hat * x_hat, axis=-1, keepdims=True)
    )
    mixed = (middle + mixing.result()).astype(bf16)
    gate_grad = jnp.sum(jnp.where(chosen, gate_sum[:, None, :experts], 0.0), axis=-1)
    out_terms = out_terms[:2] + list(tie(out_terms[2:3], late[4]))
    qkv_grad = sum(t[0].astype(f32) for t in qkv_terms[:3])
    out_weight_grad = sum(t[0].astype(f32) for t in out_terms[:3])

    mid_part = jnp.sum(d_normed_mid * mid_hat, axis=0)
    (in_part,) = tie((in_part,), late[2])
    layer_part = jnp.stack([in_part[0] / gain_in, mid_part]).reshape(2, n, groups, -1)
    layer_part = jnp.stack(relative([layer_part[:, :, t] for t in range(groups)], "tensor"))
    for bit in bits_of(groups):
        pairs = layer_part.reshape((layer_part.shape[0] // 2, 2) + layer_part.shape[1:])
        layer_part = pairs[:, 0] + flip_step(pairs[:, 1], "tensor", groups, bit)
    head_parts = split_last(head_part.reshape(2, heads, HD), n)
    rows = [
        jnp.concatenate([layer_part[0, :, k].reshape(-1), h.reshape(-1)])
        for k, h in enumerate(head_parts)
    ]
    rows = jnp.stack(relative(rows, "dp"))
    summed = flip_reduce_rows(rows, "dp", n)
    cut = 2 * (depth // groups)
    layer_grad = summed[:cut].reshape(2, depth // groups)
    head_grad = summed[cut:].reshape(2, heads, HD // n)

    return (
        mixed,
        input_grad,
        gate_grad,
        qkv_grad,
        out_weight_grad,
        head_grad,
        layer_grad,
        gu_grad,
        dn_grad,
    )


def solution(mesh):
    return jax.shard_map(
        per_device,
        mesh=mesh,
        in_specs=(
            P(("dp", "tensor"), None),
            P("dp", None),
            P(("dp", "tensor"), None),
            P(("dp", "tensor"), None),
            P(("dp", "tensor"), None),
            P(None, "dp", "tensor"),
            P("tensor", "dp"),
            P(None, "tensor", "dp"),
            P(None, "dp"),
            P(None, None, "dp", "tensor"),
            P(None, "tensor", "dp"),
        ),
        out_specs=(
            P(("dp", "tensor"), None),
            P(("dp", "tensor"), None),
            P(("dp", "tensor"), None),
            P(None, "dp", "tensor"),
            P("tensor", "dp"),
            P(None, "tensor", "dp"),
            P(None, ("dp", "tensor")),
            P(None, None, "dp", "tensor"),
            P(None, "tensor", "dp"),
        ),
        check_vma=False,
    )
```

```python
import functools

import jax
import jax.numpy as jnp
import numpy as np
from jax import lax
from jax.experimental import pallas as pl
from jax.experimental.pallas import tpu as pltpu
from jax.sharding import PartitionSpec as P

HD = 128
E = 16
EPSILON = 1e-05
ROPE_BASE = 10000.0
MASKED = -1e30
LANES = 128
CHUNKS = 4
VMEM_BYTES = 60 << 20

f32 = jnp.float32
bf16 = jnp.bfloat16
NT = (((1,), (1,)), ((), ()))
TN = (((0,), (0,)), ((), ()))
ANY = pl.BlockSpec(memory_space=pl.ANY)
SMEM = pl.BlockSpec(memory_space=pltpu.SMEM)
VMEM = pl.BlockSpec(memory_space=pltpu.VMEM)


def dot(a, b):
    return jnp.dot(a, b, preferred_element_type=f32)


def dot_nt(a, b):
    return lax.dot_general(a, b, NT, preferred_element_type=f32)


def dot_tn(a, b):
    return lax.dot_general(a, b, TN, preferred_element_type=f32)


def shape(dims, dtype):
    return jax.ShapeDtypeStruct(dims, dtype)


def ring_of(groups):
    return list(range(0, groups, 2)) + list(range(groups - 1, 0, -2))


def distances_of(groups):
    steps = groups // 2
    near = [s * k for k in range(steps - 1, 0, -1) for s in (1, -1)]
    return [steps] + near + [0]


def ring_step(value, groups, sign):
    ring = ring_of(groups)
    pairs = [(ring[p], ring[(p + sign) % groups]) for p in range(groups)]
    return lax.ppermute(value, "tensor", pairs)


def tie(values, after):
    values, after = tuple(values), tuple(after)
    return lax.optimization_barrier(values + after)[: len(values)]


class Gather:
    def __init__(self, own, groups):
        self.groups, self.steps = groups, groups // 2
        self.below, self.above = [own], [own]

    def step(self, after=()):
        low, high = self.below[-1], self.above[-1]
        if len(self.below) == self.steps:
            half = low.shape[0] // 2
            low, high = low[:half], high[half:]
        if after:
            low, high = tie((low, high), after)
        self.below.append(ring_step(low, self.groups, 1))
        self.above.append(ring_step(high, self.groups, -1))
        return [self.below[-1], self.above[-1]]

    def run(self):
        while len(self.below) <= self.steps:
            self.step()
        return self

    def at(self, distance):
        return self.above[distance] if distance >= 0 else self.below[-distance]

    def far(self):
        return [self.below[self.steps], self.above[self.steps]]

    def pieces(self):
        return self.far() + [self.at(k) for k in distances_of(self.groups)[1:]]


class Scatter:
    def __init__(self, pieces, groups):
        self.groups, self.steps, self.done = groups, groups // 2, 0
        self.far = pieces[:2]
        self.block = dict(zip(distances_of(groups)[1:], pieces[2:]))

    def step(self, after=(), riders=None):
        if self.done == 0:
            sent = self.far
        else:
            distance = self.steps - self.done
            low, high = (v.astype(f32) for v in self.moved)
            if self.done == 1:
                half = low.shape[0]
                low = jnp.pad(low, ((0, half), (0, 0)))
                high = jnp.pad(high, ((half, 0), (0, 0)))
            dtype = self.far[0].dtype
            low = (self.block[distance].astype(f32) + low).astype(dtype)
            high = (self.block[-distance].astype(f32) + high).astype(dtype)
            sent = [low, high]
        rows, columns = sent[0].shape
        if riders:
            riders = [jnp.pad(r, ((0, 0), (0, columns - r.shape[1]))) for r in riders]
            sent = [jnp.concatenate(pair, axis=0) for pair in zip(sent, riders)]
        if after:
            sent = tie(sent, after)
        self.moved = [ring_step(sent[0], self.groups, 1), ring_step(sent[1], self.groups, -1)]
        self.done += 1
        if riders:
            self.ridden = [m[rows:] for m in self.moved]
            self.moved = [m[:rows] for m in self.moved]
        return self.moved

    def run(self):
        while self.done < self.steps:
            self.step()
        return self

    def result(self):
        low, high = self.moved
        return self.block[0].astype(f32) + low.astype(f32) + high.astype(f32)


def bits_of(count):
    return [1 << b for b in range(count.bit_length() - 1)]


def flip_step(value, axis, count, bit):
    return lax.ppermute(value, axis, [(s, s ^ bit) for s in range(count)])


def relative(parts, axis):
    count = len(parts)
    index = lax.axis_index(axis)
    for bit in bits_of(count):
        turned = (index & bit) != 0
        parts = [jnp.where(turned, parts[k ^ bit], parts[k]) for k in range(count)]
    return parts


def split_last(value, count):
    width = value.shape[-1] // count
    return [value[..., k * width : (k + 1) * width] for k in range(count)]


def flip_reduce(keep, sent, axis, count):
    return flip_rest(keep, flip_step(sent, axis, count, 1), axis, count)


def flip_rest(keep, got, axis, count):
    for bit in bits_of(count)[1:]:
        odd = (keep[1::2].astype(f32) + got[1::2].astype(f32)).astype(bf16)
        more = flip_step(odd, axis, count, bit)
        if 2 * bit < count:
            keep = (keep[0::2].astype(f32) + got[0::2].astype(f32)).astype(bf16)
            got = more
    return [keep, got, more, odd]


def flip_reduce_rows(value, axis, count):
    for bit in bits_of(count):
        pairs = value.reshape((value.shape[0] // 2, 2) + value.shape[1:])
        value = pairs[:, 0] + flip_step(pairs[:, 1], axis, count, bit)
    return value[0]


def fetch(sources, target, sems, first, rows_at):
    copies = []
    for number, source in enumerate(sources):
        if source.shape[1] > target.shape[1]:
            source = source.at[:, pl.ds(0, target.shape[1])]
        copy = pltpu.make_async_copy(
            source, target.at[pl.ds(rows_at[number], source.shape[0])], sems.at[first + number]
        )
        copy.start()
        copies.append(copy)
    return copies


def load_projections(weights, wqs, sems, first):
    copies = []
    n, _, width = weights.shape
    depth = wqs.shape[0] // n
    for k in range(n):
        for j in range(3):
            source = weights.at[k, pl.ds(j * depth, depth)]
            target = wqs.at[pl.ds(k * depth, depth), pl.ds(j * width, width)]
            copies.append(pltpu.make_async_copy(source, target, sems.at[first + 3 * k + j]))
    return copies


def load_outputs(weights, wos, sems, first):
    copies = []
    n, _, width = weights.shape
    depth = wos.shape[1] // n
    cuts = max(1, depth // width)
    columns = depth // cuts
    for k in range(n):
        for c in range(cuts):
            source = weights.at[k, pl.ds(3 * depth + c * width, width), pl.ds(0, columns)]
            target = wos.at[:, pl.ds(k * depth + c * columns, columns)]
            copies.append(pltpu.make_async_copy(source, target, sems.at[first + cuts * k + c]))
    return copies


def output_copies(n, depth, width):
    return n * max(1, depth // width)


def piece_shapes(own_rows, columns, count):
    half = shape((own_rows // 2, columns), bf16)
    return [half, half] + [shape((own_rows, columns), bf16)] * (count - 2)


def cost(micros):
    return pl.CostEstimate(flops=int(micros * 6e8), bytes_accessed=1 << 20, transcendentals=0)


def piece_rows(order, half, pieces):
    rows = 2 * half
    starts = [pl.multiple_of(order[0] * rows, rows)]
    starts.append(pl.multiple_of(order[0] * rows + half, half))
    for number in range(2, pieces):
        starts.append(pl.multiple_of(order[number - 1] * rows, rows))
    return starts


def send_out(staged, targets, sems, first, starts):
    copies = []
    for number, target in enumerate(targets):
        copy = pltpu.make_async_copy(
            staged.at[pl.ds(starts[number], target.shape[0])], target, sems.at[first + number]
        )
        copy.start()
        copies.append(copy)
    return copies


def allowed_pairs(seg_col, seg_row, first, rows, width):
    row_pos = first + lax.broadcasted_iota(jnp.int32, (rows, width), 0)
    key_pos = lax.broadcasted_iota(jnp.int32, (rows, width), 1)
    return (seg_col[pl.ds(first, rows), :] == seg_row[:, pl.ds(0, width)]) & (key_pos <= row_pos)


def attn_proj_body(count, *refs):
    it = iter(refs)
    order = next(it)
    pieces = [next(it) for _ in range(count)]
    wq = next(it)
    gain, gains, cosine, sine = (next(it) for _ in range(4))
    q_o, k_o, v_o, qr_o, kr_o, x_o = (next(it) for _ in range(6))
    xs, wqs, sems = (next(it) for _ in range(3))
    block, width = q_o.shape
    heads = width // HD
    step = pl.program_id(0)

    @pl.when(step == 0)
    def _():
        starts = piece_rows(order, pieces[0].shape[0], count)
        copies = load_projections(wq, wqs, sems, count)
        for copy in copies:
            copy.start()
        for copy in fetch(pieces, xs, sems, 0, starts) + copies:
            copy.wait()

    wide = xs[pl.ds(pl.multiple_of(step * block, block), block), :].astype(f32)
    inv = lax.rsqrt(jnp.mean(wide * wide, axis=-1, keepdims=True) + EPSILON)
    x_o[...] = (wide * inv * gain[...]).astype(bf16)
    out = dot(x_o[...], wqs[...])
    v_o[...] = out[:, 2 * width :].astype(bf16)
    for j, (raw_o, hat_o) in enumerate(((qr_o, q_o), (kr_o, k_o))):
        raw = out[:, j * width : (j + 1) * width]
        raw_o[...] = raw
        for h in range(heads):
            cols = slice(h * HD, (h + 1) * HD)
            u = raw[:, cols]
            inv = lax.rsqrt(jnp.mean(u * u, axis=-1, keepdims=True) + EPSILON)
            u = u * inv * gains[j : j + 1, cols]
            u = u * cosine[...] + pltpu.roll(u, HD // 2, 1) * sine[...]
            hat_o[:, cols] = u.astype(bf16)


def attn_proj(order, pieces, wq, gain, gains, cosine, sine):
    n, count = wq.shape[0], len(pieces)
    d = gain.shape[1]
    length = cosine.shape[0]
    width = wq.shape[2]
    block = min(256, length)

    def rows(columns):
        return pl.BlockSpec((block, columns), lambda r: (r, 0))

    def whole(a):
        return pl.BlockSpec(a.shape, lambda r: (0, 0))

    return pl.pallas_call(
        functools.partial(attn_proj_body, count),
        grid=(length // block,),
        in_specs=[SMEM] + [ANY] * (count + 1) + [whole(gain), whole(gains), rows(HD), rows(HD)],
        out_specs=[rows(width)] * 5 + [rows(d)],
        out_shape=[shape((length, width), bf16)] * 3
        + [shape((length, width), f32)] * 2
        + [shape((length, d), bf16)],
        scratch_shapes=[
            pltpu.VMEM((length, d), bf16),
            pltpu.VMEM((d, 3 * width), bf16),
            pltpu.SemaphoreType.DMA((count + 3 * n,)),
        ],
        compiler_params=pltpu.CompilerParams(vmem_limit_bytes=VMEM_BYTES),
        cost_estimate=cost(10),
        name="attn_proj",
    )(order, *pieces, wq, gain, gains, cosine, sine)


def attn_core_body(count, block, *refs):
    it = iter(refs)
    order = next(it)
    wo = next(it)
    q, k_, v, seg_row, seg_col = (next(it) for _ in range(5))
    ctx_o, lse_o = next(it), next(it)
    outs = [next(it) for _ in range(count)]
    wos, stage, sems = (next(it) for _ in range(3))
    length, width = ctx_o.shape
    heads = width // HD
    starts = piece_rows(order, outs[0].shape[0], count)
    copies = load_outputs(wo, wos, sems, count)
    for copy in copies:
        copy.start()
    scale = HD ** (-0.5)
    for b in range(length // block):
        rows = pl.ds(b * block, block)
        hi = (b + 1) * block
        allowed = allowed_pairs(seg_col, seg_row, b * block, block, hi)
        for h in range(heads):
            cols = slice(h * HD, (h + 1) * HD)
            s = dot_nt(q[rows, cols], k_[pl.ds(0, hi), cols]) * scale
            s = jnp.where(allowed, s, MASKED)
            top = jnp.max(s, axis=-1, keepdims=True)
            e = jnp.exp(s - top)
            total = jnp.sum(e, axis=-1, keepdims=True)
            probs = (e * (1.0 / total)).astype(bf16)
            ctx_o[rows, cols] = dot(probs, v[pl.ds(0, hi), cols]).astype(bf16)
            lse_o[h, rows, :] = top + jnp.log(total)
    for copy in copies:
        copy.wait()
    stage[...] = dot(ctx_o[...], wos[...]).astype(bf16)
    for copy in send_out(stage, outs, sems, 0, starts):
        copy.wait()


def attn_core(order, wo, q, k, v, seg_row, seg_col, own_rows, d):
    n = wo.shape[0]
    length, width = q.shape
    count = length // own_rows + 1
    return pl.pallas_call(
        functools.partial(attn_core_body, count, min(256, length)),
        in_specs=[SMEM] + [ANY] + [VMEM] * 5,
        out_specs=[VMEM] * 2 + [ANY] * count,
        out_shape=[shape((length, width), bf16), shape((width // HD, length, 1), f32)]
        + piece_shapes(own_rows, d, count),
        scratch_shapes=[
            pltpu.VMEM((width, d), bf16),
            pltpu.VMEM((length, d), bf16),
            pltpu.SemaphoreType.DMA((count + output_copies(n, d // n, width),)),
        ],
        compiler_params=pltpu.CompilerParams(vmem_limit_bytes=VMEM_BYTES),
        cost_estimate=cost(10),
        name="attn_core",
    )(order, wo, q, k, v, seg_row, seg_col)


def attn_back_body(count, block, *refs):
    it = iter(refs)
    order = next(it)
    pieces = [next(it) for _ in range(count)]
    wo = next(it)
    q, k_, v, lse, seg_row, seg_col = (next(it) for _ in range(6))
    dq_o, dk_o, dv_o, db_o = (next(it) for _ in range(4))
    db, wos, dctx, sems = (next(it) for _ in range(4))
    length, width = q.shape
    heads = width // HD
    starts = piece_rows(order, pieces[0].shape[0], count)
    copies = load_outputs(wo, wos, sems, count)
    for copy in copies:
        copy.start()
    for copy in copies + fetch(pieces, db, sems, 0, starts):
        copy.wait()
    keep = pltpu.make_async_copy(db, db_o, sems.at[0])
    keep.start()
    scale = HD ** (-0.5)
    dctx[...] = dot_nt(db[...], wos[...]).astype(bf16)
    dk_o[...] = jnp.zeros_like(dk_o)
    dv_o[...] = jnp.zeros_like(dv_o)
    for b in range(length // block):
        rows = pl.ds(b * block, block)
        hi = (b + 1) * block
        low = pl.ds(0, hi)
        allowed = allowed_pairs(seg_col, seg_row, b * block, block, hi)
        for h in range(heads):
            cols = slice(h * HD, (h + 1) * HD)
            s = dot_nt(q[rows, cols], k_[low, cols]) * scale
            p = jnp.where(allowed, jnp.exp(s - lse[h, rows, :]), 0.0)
            g = dot_nt(dctx[rows, cols], v[low, cols])
            pg = p * g
            ds = (pg - p * jnp.sum(pg, axis=-1, keepdims=True)).astype(bf16)
            dq_o[rows, cols] = dot(ds, k_[low, cols]) * scale
            dk_o[low, cols] += dot_tn(ds, q[rows, cols]) * scale
            dv_o[low, cols] += dot_tn(p.astype(bf16), dctx[rows, cols])
    keep.wait()


def attn_back(order, pieces, wo, q, k, v, lse, seg_row, seg_col):
    n, count = wo.shape[0], len(pieces)
    d = pieces[0].shape[1]
    length, width = q.shape
    return pl.pallas_call(
        functools.partial(attn_back_body, count, min(256, length)),
        in_specs=[SMEM] + [ANY] * (count + 1) + [VMEM] * 6,
        out_specs=[VMEM] * 3 + [ANY],
        out_shape=[shape((length, width), f32)] * 3 + [shape((length, d), bf16)],
        scratch_shapes=[
            pltpu.VMEM((length, d), bf16),
            pltpu.VMEM((width, d), bf16),
            pltpu.VMEM((length, width), bf16),
            pltpu.SemaphoreType.DMA((count + output_copies(n, d // n, width),)),
        ],
        compiler_params=pltpu.CompilerParams(vmem_limit_bytes=VMEM_BYTES),
        cost_estimate=cost(14),
        name="attn_back",
    )(order, *pieces, wo, q, k, v, lse, seg_row, seg_col)


def proj_back_body(count, steps, *refs):
    it = iter(refs)
    order = next(it)
    wq = next(it)
    qr, kr, dq, dk, dv = (next(it) for _ in range(5))
    gains, cosine, sine, x = (next(it) for _ in range(4))
    dp_o, hg_o, gs_o = (next(it) for _ in range(3))
    outs = [next(it) for _ in range(count)]
    wqs, stage, sems = (next(it) for _ in range(3))
    block, width = qr.shape
    heads = width // HD
    step = pl.program_id(0)

    @pl.when(step == 0)
    def _():
        copies = load_projections(wq, wqs, sems, count)
        for copy in copies:
            copy.start()
        hg_o[...] = jnp.zeros_like(hg_o)
        gs_o[...] = jnp.zeros_like(gs_o)
        for copy in copies:
            copy.wait()

    dp_o[:, 2 * width :] = dv[...].astype(bf16)
    for j, (raw, grad) in enumerate(((qr, dq), (kr, dk))):
        for h in range(heads):
            cols = slice(h * HD, (h + 1) * HD)
            u = raw[:, cols]
            inv = lax.rsqrt(jnp.mean(u * u, axis=-1, keepdims=True) + EPSILON)
            hat = u * inv
            t = grad[:, cols]
            t = t * cosine[...] - pltpu.roll(t, HD // 2, 1) * sine[...]
            hg_o[j : j + 1, cols] += jnp.sum(t * hat, axis=0, keepdims=True)
            w = t * gains[j : j + 1, cols]
            w = inv * (w - hat * jnp.mean(w * hat, axis=-1, keepdims=True))
            dp_o[:, j * width + h * HD : j * width + (h + 1) * HD] = w.astype(bf16)
    out = dot_nt(dp_o[...], wqs[...])
    gs_o[...] += jnp.sum(out * x[...].astype(f32), axis=0, keepdims=True)
    stage[pl.ds(pl.multiple_of(step * block, block), block), :] = out.astype(bf16)

    @pl.when(step == steps - 1)
    def _():
        starts = piece_rows(order, outs[0].shape[0], count)
        for copy in send_out(stage, outs, sems, 0, starts):
            copy.wait()


def proj_back(order, wq, qr, kr, dq, dk, dv, gains, cosine, sine, x, own_rows):
    n = wq.shape[0]
    length, width = qr.shape
    d = x.shape[1]
    count = length // own_rows + 1
    block = min(256, length)
    steps = length // block

    def rows(columns):
        return pl.BlockSpec((block, columns), lambda r: (r, 0))

    def whole(dims):
        return pl.BlockSpec(dims, lambda r: (0, 0))

    return pl.pallas_call(
        functools.partial(proj_back_body, count, steps),
        grid=(steps,),
        in_specs=[SMEM, ANY]
        + [rows(width)] * 5
        + [whole(gains.shape), rows(HD), rows(HD), rows(d)],
        out_specs=[rows(3 * width), whole((2, width)), whole((1, d))] + [ANY] * count,
        out_shape=[
            shape((length, 3 * width), bf16),
            shape((2, width), f32),
            shape((1, d), f32),
        ]
        + piece_shapes(own_rows, d, count),
        scratch_shapes=[
            pltpu.VMEM((d, 3 * width), bf16),
            pltpu.VMEM((length, d), bf16),
            pltpu.SemaphoreType.DMA((count + 3 * n,)),
        ],
        compiler_params=pltpu.CompilerParams(vmem_limit_bytes=VMEM_BYTES),
        cost_estimate=cost(12),
        name="proj_back",
    )(order, wq, qr, kr, dq, dk, dv, gains, cosine, sine, x)


def attn_grad_body(places, xa, xb, dp, ctx, da, db, qkv_keep, qkv_send, out_keep, out_send):
    width = ctx.shape[1]
    for x, d, qkv_o, out_o in ((xa, da, qkv_keep, out_keep), (xb, db, qkv_send, out_send)):
        grad = dot_tn(x[...], dp[...])
        for j in range(3):
            qkv_o[0, j] = grad[:, j * width : (j + 1) * width].astype(bf16)
        out_o[0] = dot_tn(ctx[...], d[...]).astype(bf16)


def attn_grad(places, x, dp, ctx, db, n):
    length, d = x.shape
    width = ctx.shape[1]
    depth = d // n
    even = pl.BlockSpec((length, depth), lambda m, at: (0, at[2 * m]))
    odd = pl.BlockSpec((length, depth), lambda m, at: (0, at[2 * m + 1]))
    return pl.pallas_call(
        attn_grad_body,
        grid_spec=pltpu.PrefetchScalarGridSpec(
            num_scalar_prefetch=1,
            grid=(n // 2,),
            in_specs=[
                even,
                odd,
                pl.BlockSpec((length, 3 * width), lambda m, at: (0, 0)),
                pl.BlockSpec((length, width), lambda m, at: (0, 0)),
                even,
                odd,
            ],
            out_specs=[pl.BlockSpec((1, 3, depth, width), lambda m, at: (m, 0, 0, 0))] * 2
            + [pl.BlockSpec((1, width, depth), lambda m, at: (m, 0, 0))] * 2,
        ),
        out_shape=[shape((n // 2, 3, depth, width), bf16)] * 2
        + [shape((n // 2, width, depth), bf16)] * 2,
        compiler_params=pltpu.CompilerParams(vmem_limit_bytes=VMEM_BYTES),
        cost_estimate=cost(6),
        name="attn_grad",
    )(places, x, x, dp, ctx, db, db)


def flat_rows(pieces):
    starts, at = [], 0
    for piece in pieces:
        starts.append(at)
        at += piece.shape[0]
    return starts


def held(piece):
    return pl.BlockSpec(piece.shape, lambda s: (0, 0))


def stacked(pieces):
    return jnp.concatenate([piece[...] for piece in pieces], axis=0)


def moe_in_body(count, *refs):
    xp, gu, out = refs[:count], *refs[count:]
    out[...] = dot(stacked(xp), gu[...]).astype(bf16)


def moe_in(xp, gate_up, group=4):
    count = len(xp)
    d, columns = gate_up.shape
    rows = sum(p.shape[0] for p in xp)
    wide = 2 * group * LANES
    return pl.pallas_call(
        functools.partial(moe_in_body, count),
        grid=(columns // wide,),
        in_specs=[held(p) for p in xp] + [pl.BlockSpec((d, wide), lambda s: (0, s))],
        out_specs=pl.BlockSpec((rows, wide), lambda s: (0, s)),
        out_shape=shape((rows, columns), bf16),
        compiler_params=pltpu.CompilerParams(vmem_limit_bytes=VMEM_BYTES),
        cost_estimate=cost(rows * 0.02 + 4),
        name="moe_in",
    )(*xp, gate_up)


def moe_mid_body(group, steps, sets, count, *refs):
    it = iter(refs)
    gates = next(it)
    cp = [next(it) for _ in range(count)]
    gus = [next(it) for _ in range(sets)]
    gu_w, dn_w = next(it), next(it)
    d_outs = [next(it) for _ in range(count)]
    m_outs = [next(it) for _ in range(count)]
    dgu_o, hw_o = next(it), next(it)
    cs, d_acc, m_acc, gg, stage, sems = (next(it) for _ in range(6))
    d = cs.shape[1]
    fw = LANES
    step = pl.program_id(0)

    @pl.when(step == 0)
    def _():
        d_acc[...] = jnp.zeros_like(d_acc)
        m_acc[...] = jnp.zeros_like(m_acc)
        gg[...] = jnp.zeros_like(gg)

    d_hid = dot_nt(stacked(cp), dn_w[...])
    at = 0
    for gu in gus:
        rows = gu.shape[0]
        here = pl.ds(at, rows)
        table = gates[here, :].astype(f32)
        lane = lax.broadcasted_iota(jnp.int32, table.shape, 1)
        total = jnp.zeros(table.shape, f32)
        for i in range(group):
            g = gu[:, 2 * i * fw : (2 * i + 1) * fw].astype(f32)
            u = gu[:, (2 * i + 1) * fw : (2 * i + 2) * fw].astype(f32)
            dh = d_hid[at : at + rows, i * fw : (i + 1) * fw]
            z = jax.nn.sigmoid(g)
            swish = g * z
            h = swish * u
            expert = step * group + i
            own = jnp.sum(h * dh, axis=1, keepdims=True)
            total = total + jnp.where(lane == expert, own, 0.0)
            gate = jnp.sum(jnp.where(lane == expert, table, 0.0), axis=1, keepdims=True)
            dw = dh * gate
            d_g = dw * u * z * (1.0 + g * (1.0 - z))
            hw_o[here, i * fw : (i + 1) * fw] = (h * gate).astype(bf16)
            dgu_o[here, 2 * i * fw : (2 * i + 1) * fw] = d_g.astype(bf16)
            dgu_o[here, (2 * i + 1) * fw : (2 * i + 2) * fw] = (dw * swish).astype(bf16)
        gg[here, :] += total
        at += rows
    d_acc[...] += dot_nt(dgu_o[...], gu_w[...])
    m_acc[...] += dot(hw_o[...], dn_w[...])

    @pl.when(step == steps - 1)
    def _():
        stage[:, pl.ds(0, d)] = d_acc[...].astype(bf16)
        stage[:, pl.ds(d, LANES)] = gg[...].astype(bf16)
        copies = send_out(stage, d_outs, sems, 0, flat_rows(d_outs))
        cs[...] = m_acc[...].astype(bf16)
        copies = copies + send_out(cs, m_outs, sems, count, flat_rows(m_outs))
        for copy in copies:
            copy.wait()


def moe_mid(gates, cp, gus, gate_up, down, group=4):
    count = len(cp)
    hidden, d = down.shape
    rows = sum(p.shape[0] for p in cp)
    half = group * LANES
    steps = hidden // half
    return pl.pallas_call(
        functools.partial(moe_mid_body, group, steps, len(gus), count),
        grid=(steps,),
        in_specs=[pl.BlockSpec((rows, LANES), lambda s: (0, 0))]
        + [held(p) for p in cp]
        + [pl.BlockSpec((g.shape[0], 2 * half), lambda s: (0, s)) for g in gus]
        + [
            pl.BlockSpec((d, 2 * half), lambda s: (0, s)),
            pl.BlockSpec((half, d), lambda s: (s, 0)),
        ],
        out_specs=[ANY] * (2 * count)
        + [
            pl.BlockSpec((rows, 2 * half), lambda s: (0, s)),
            pl.BlockSpec((rows, half), lambda s: (0, s)),
        ],
        out_shape=[shape((p.shape[0], d + LANES), bf16) for p in cp]
        + [shape(p.shape, bf16) for p in cp]
        + [shape((rows, 2 * hidden), bf16), shape((rows, hidden), bf16)],
        scratch_shapes=[
            pltpu.VMEM((rows, d), bf16),
            pltpu.VMEM((rows, d), f32),
            pltpu.VMEM((rows, d), f32),
            pltpu.VMEM((rows, LANES), f32),
            pltpu.VMEM((rows, d + LANES), bf16),
            pltpu.SemaphoreType.DMA((2 * count,)),
        ],
        compiler_params=pltpu.CompilerParams(vmem_limit_bytes=VMEM_BYTES),
        cost_estimate=cost(rows * 0.04 + 6),
        name="moe_mid",
    )(gates, *cp, *gus, gate_up, down)


def turn_body(count, *refs):
    pieces, out, xs, sems = refs[:count], refs[count], refs[count + 1], refs[count + 2]
    for copy in fetch(pieces, xs, sems, 0, flat_rows(pieces)):
        copy.wait()
    d = xs.shape[1]
    size = 256
    eye = (
        lax.broadcasted_iota(jnp.int32, (size, size), 0)
        == lax.broadcasted_iota(jnp.int32, (size, size), 1)
    ).astype(bf16)
    for at in range(0, d, size):
        out[pl.ds(at, size), :] = dot_nt(eye, xs[:, pl.ds(at, size)]).astype(bf16)


def turn_rows(pieces):
    count = len(pieces)
    length = sum(p.shape[0] for p in pieces)
    d = pieces[0].shape[1]
    return pl.pallas_call(
        functools.partial(turn_body, count),
        in_specs=[ANY] * count,
        out_specs=VMEM,
        out_shape=shape((d, length), bf16),
        scratch_shapes=[pltpu.VMEM((length, d), bf16), pltpu.SemaphoreType.DMA((count,))],
        compiler_params=pltpu.CompilerParams(vmem_limit_bytes=VMEM_BYTES),
        cost_estimate=cost(4),
        name="turn_rows",
    )(*pieces)


def in_grad_body(n, group, sets, places, xt, *refs):
    dgus = refs[:sets]
    *outs, xs, sems = refs[-4:]
    depth, fw = outs[0].shape[3:]
    step = pl.program_id(0)

    def part(k):
        source = xt.at[pl.ds(pl.multiple_of(places[k] * depth, depth), depth)]
        return pltpu.make_async_copy(source, xs.at[pl.ds(k * depth, depth)], sems.at[k])

    @pl.when(step == 0)
    def _():
        for k in range(n):
            part(k).start()

    dgu = jnp.concatenate([ref[...] for ref in dgus], axis=0)
    for k in range(n):

        @pl.when(step == 0)
        def _(k=k):
            part(k).wait()

        grad = dot(xs[pl.ds(k * depth, depth), :], dgu)
        for i in range(group):
            for g in range(2):
                at = (2 * i + g) * fw
                outs[k % 2][k // 2, i, g] = grad[:, at : at + fw].astype(bf16)


def in_grad(places, xt, dgus, n, experts, first, number, held, whole=None, group=2):
    d, length = xt.shape
    depth = d // n
    fw = dgus[0].shape[1] // (2 * experts)
    start = first // group
    at = (first % held) // group
    before = [] if whole is None else list(whole)
    sets = len(dgus)
    return list(
        pl.pallas_call(
            functools.partial(in_grad_body, n, group, sets),
            grid=(number // group,),
            in_specs=[SMEM, ANY]
            + [pl.BlockSpec((a.shape[0], 2 * group * fw), lambda s: (0, s + start)) for a in dgus]
            + [ANY] * len(before),
            out_specs=[pl.BlockSpec((n // 2, group, 2, depth, fw), lambda s: (0, at + s, 0, 0, 0))]
            * 2,
            out_shape=[shape((n // 2, held, 2, depth, fw), bf16)] * 2,
            input_output_aliases={2 + sets: 0, 3 + sets: 1} if before else {},
            scratch_shapes=[pltpu.VMEM((d, length), bf16), pltpu.SemaphoreType.DMA((n,))],
            compiler_params=pltpu.CompilerParams(vmem_limit_bytes=VMEM_BYTES),
            cost_estimate=cost(1.5 * number + 3),
            name="in_grad",
        )(places, xt, *dgus, *before)
    )


def out_grad_body(group, count, sets, *refs):
    hws, pieces = refs[:sets], refs[sets : sets + count]
    out, cs, sems = refs[-3:]
    fw = out.shape[1]

    @pl.when(pl.program_id(0) == 0)
    def _():
        for copy in fetch(pieces, cs, sems, 0, flat_rows(pieces)):
            copy.wait()

    turned = jnp.concatenate([ref[...] for ref in hws], axis=0).T
    grad = dot(turned, cs[...])
    for i in range(group):
        out[i] = grad[i * fw : (i + 1) * fw].astype(bf16)


def out_grad(hws, cp, experts, group=2):
    count = len(cp)
    length = sum(h.shape[0] for h in hws)
    d = cp[0].shape[1]
    fw = hws[0].shape[1] // experts
    return pl.pallas_call(
        functools.partial(out_grad_body, group, count, len(hws)),
        grid=(experts // group,),
        in_specs=[pl.BlockSpec((h.shape[0], group * fw), lambda s: (0, s)) for h in hws]
        + [ANY] * count,
        out_specs=pl.BlockSpec((group, fw, d), lambda s: (s, 0, 0)),
        out_shape=shape((experts, fw, d), bf16),
        scratch_shapes=[pltpu.VMEM((length, d), bf16), pltpu.SemaphoreType.DMA((count,))],
        compiler_params=pltpu.CompilerParams(vmem_limit_bytes=VMEM_BYTES),
        cost_estimate=cost(12),
        name="out_grad",
    )(*hws, *cp)


def finish_body(*refs):
    keep, got, more, out = refs[-4:]
    out[...] = keep[0].astype(f32) + got[0].astype(f32) + more[0].astype(f32)


def finish(whole, terms, experts, first):
    number = terms[0].shape[1]
    rest = terms[0].shape[2:]
    zeros = (0,) * len(rest)
    before = [] if whole is None else [whole]
    each = 2
    at = first // each
    return pl.pallas_call(
        finish_body,
        grid=(number // each,),
        in_specs=[ANY] * len(before)
        + [pl.BlockSpec((1, each) + rest, lambda s: (0, s) + zeros)] * 3,
        out_specs=pl.BlockSpec((each,) + rest, lambda s: (at + s,) + zeros),
        out_shape=shape((experts,) + rest, f32),
        input_output_aliases={0: 0} if before else {},
        compiler_params=pltpu.CompilerParams(vmem_limit_bytes=VMEM_BYTES),
        cost_estimate=cost(2),
        name="finish",
    )(*before, *terms)


def place_body(*refs):
    part, out = refs[-2:]
    out[...] = part[...].astype(f32)


def place(part, experts, whole=None):
    rest = part.shape[1:]
    zeros = (0,) * len(rest)
    before = [] if whole is None else [whole]
    return pl.pallas_call(
        place_body,
        grid=(part.shape[0] // 4,),
        in_specs=[ANY] * len(before) + [pl.BlockSpec((4,) + rest, lambda s: (s,) + zeros)],
        out_specs=pl.BlockSpec((4,) + rest, lambda s: (s,) + zeros),
        out_shape=shape((experts,) + rest, f32),
        input_output_aliases={0: 0} if before else {},
        compiler_params=pltpu.CompilerParams(vmem_limit_bytes=VMEM_BYTES),
        cost_estimate=cost(3),
        name="place",
    )(*before, part)


def pack_body(w, out):
    fw = w.shape[3]
    for i in range(w.shape[0]):
        for g in range(2):
            at = (2 * i + g) * fw
            out[:, at : at + fw] = w[i, g]


def pack(gate_up, group=4):
    experts, _, depth, fw = gate_up.shape
    return pl.pallas_call(
        pack_body,
        grid=(experts // group,),
        in_specs=[pl.BlockSpec((group, 2, depth, fw), lambda s: (s, 0, 0, 0))],
        out_specs=pl.BlockSpec((depth, 2 * group * fw), lambda s: (0, s)),
        out_shape=shape((depth, 2 * experts * fw), bf16),
        compiler_params=pltpu.CompilerParams(vmem_limit_bytes=VMEM_BYTES),
        cost_estimate=cost(4),
        name="pack",
    )(gate_up)


def rope_tables(length):
    positions = np.arange(length, dtype=np.float32)
    power = -np.arange(HD // 2, dtype=np.float32) * np.float32(2.0) / np.float32(HD)
    inverse_freq = np.power(np.float32(ROPE_BASE), power)
    phases = positions[:, None] * inverse_freq[None, :]
    cosine, sine = np.cos(phases), np.sin(phases)
    tables = [cosine, cosine], [-sine, sine]
    return [np.concatenate(t, axis=-1).astype(np.float32) for t in tables]


def per_device(
    tokens,
    segments,
    routes,
    gate_values,
    cotangent,
    query_key_value,
    out_weight,
    head_gain,
    layer_gain,
    gate_up,
    down_weight,
):
    groups = lax.axis_size("tensor")
    n = lax.axis_size("dp")
    own_rows, d = tokens.shape
    seq_len = own_rows * groups
    heads = query_key_value.shape[2] // HD
    experts = gate_up.shape[0]
    depth = d // n
    steps = groups // 2
    top = routes.shape[1]

    x = tokens.astype(f32)
    routed = jnp.concatenate([routes.astype(bf16), gate_values], axis=1)
    routed = jnp.pad(routed, ((0, 0), (0, LANES - 2 * top)))
    normed = Gather(jnp.concatenate([tokens, routed], axis=1), groups)
    first = normed.step()

    width = query_key_value.shape[2]
    small = jnp.concatenate([layer_gain.reshape(-1), head_gain.reshape(-1)])
    size = small.shape[0]
    small = jnp.pad(small, (0, -size % (16 * width))).reshape(-1, width)
    outward = split_last(out_weight, max(1, depth // width))
    outward = [jnp.pad(a, ((0, 0), (0, width - a.shape[1]))) for a in outward]
    own = [query_key_value.reshape(-1, width)] + outward + [small]
    attn_weights = lax.all_gather(jnp.concatenate(own, axis=0), "dp", axis=0)

    ring = ring_of(groups)
    orders = [[ring[(ring.index(t) + k) % groups] for k in distances_of(groups)] for t in range(groups)]
    orders = jnp.array(orders, jnp.int32)
    order = lax.dynamic_slice(orders, (lax.axis_index("tensor"), 0), (1, groups)).reshape(groups)
    places = jnp.array([[i ^ k for k in range(n)] for i in range(n)], jnp.int32)
    places = lax.dynamic_slice(places, (lax.axis_index("dp"), 0), (1, n)).reshape(n)
    cosine, sine = rope_tables(seq_len)
    seg_row = segments.reshape(1, seq_len)
    seg_col = segments.reshape(seq_len, 1)
    expert_ids = jnp.arange(experts, dtype=jnp.int32)
    chosen = routes[:, :, None] == expert_ids
    (gate_up,) = tie((gate_up,), first)
    packed = pack(gate_up)

    done = normed.step()
    (packed,) = tie((packed,), done)
    gu = lax.all_gather(packed, "dp", axis=0, tiled=True)
    normed.step(after=[packed])
    normed.step()
    cut = 2 * depth
    small = [w[-small.shape[0] :].reshape(-1)[:size] for w in attn_weights]
    gain = jnp.concatenate([s[:cut].reshape(2, depth) for s in small], axis=1).astype(f32)
    gain_in, gain_mid = gain[0], gain[1]
    head_parts = [s[cut:].reshape(2, heads, HD // n) for s in small]
    gain_head = jnp.concatenate(head_parts, axis=2).reshape(2, heads * HD).astype(f32)
    pieces = normed.pieces()
    inv_in = lax.rsqrt(jnp.mean(x * x, axis=-1, keepdims=True) + EPSILON)
    x_hat = x * inv_in
    q, k, v, q_raw, k_raw, normed_all = attn_proj(
        order, pieces, attn_weights, gain_in[None, :], gain_head, cosine, sine
    )
    d_pieces = Gather(cotangent, groups)
    first = d_pieces.step(after=pieces)
    q, k, v = tie((q, k, v), first)
    context, lse, *attn = attn_core(
        order, attn_weights, q, k, v, seg_row, seg_col, own_rows, d
    )
    second = d_pieces.step(after=[q])
    routed = jnp.concatenate([p[:, d : d + 2 * top] for p in pieces], axis=0)
    named = routed[:, :top].astype(jnp.int32)[:, :, None] == expert_ids
    gate_table = jnp.sum(jnp.where(named, routed[:, top:].astype(f32)[:, :, None], 0.0), axis=1)
    gate_table = jnp.pad(gate_table.astype(bf16), ((0, 0), (0, LANES - experts)))
    attention = Scatter(attn, groups)
    done = attention.step(after=second)
    (down,) = tie((down_weight.reshape(-1, depth),), done)
    dn = lax.all_gather(down, "dp", axis=1, tiled=True)
    middle = x + attention.run().result()
    inv_mid = lax.rsqrt(jnp.mean(middle * middle, axis=-1, keepdims=True) + EPSILON)
    mid_hat = middle * inv_mid
    mid = Gather((mid_hat * gain_mid).astype(bf16), groups)

    hidden_in = []
    mid.step()
    for s in range(1, steps - 1):
        here = [mid.at(s), mid.at(-s)] + ([mid.at(0)] if s == 1 else [])
        mid.step(after=hidden_in[-1:])
        hidden_in.append(moe_in(here, gu))
    mid.step(after=hidden_in[-1:])
    normed_mid = mid.pieces()
    taken = normed_mid[:4]
    hidden_in.append(moe_in(taken, gu))
    d_pieces.step(after=taken)
    d_pieces.step(after=hidden_in[-1:])
    d_pieces = d_pieces.pieces()

    half_rows = hidden_in[-1].shape[0]
    d_far, d_near = d_pieces[:4], d_pieces[4:]
    far_out = list(moe_mid(gate_table[:half_rows], d_far, hidden_in[-1:], gu, dn))
    d_mid, moe, d_in, hidden = far_out[:4], far_out[4:8], far_out[8:9], far_out[9:]
    (mid_far,) = tie(normed_mid[:1], d_mid[:1])
    mid_turned = turn_rows([mid_far] + normed_mid[1:])
    d_normed = Scatter(d_mid, groups)
    done = d_normed.step()
    mixing = Scatter(moe, groups)
    second = d_normed.step(after=[mid_turned], riders=mixing.far)
    mixing.done, mixing.moved = 1, [m[:, :d] for m in d_normed.ridden]
    (table,) = tie((gate_table[half_rows:],), done + [mid_turned])
    near_out = list(moe_mid(table, d_near, hidden_in[:-1][::-1], gu, dn))
    count = len(d_near)
    d_mid, moe = d_mid + near_out[:count], moe + near_out[count : 2 * count]
    d_in, hidden = d_in + near_out[2 * count : -1], hidden + near_out[-1:]
    d_normed.block = dict(zip(distances_of(groups)[1:], d_mid[2:]))
    mixing.block = dict(zip(distances_of(groups)[1:], moe[2:]))
    third = d_normed.step(after=moe[-1:])

    (hidden_far,) = tie(hidden[:1], second + near_out[:1])
    dn_all = out_grad([hidden_far] + hidden[1:], d_pieces, experts)
    (ready,) = tie((dn_all,), third)
    dn_grad = lax.psum_scatter(ready, "dp", scatter_dimension=2, tiled=True)
    fourth = d_normed.step()

    def gradient(c, after, whole=None):
        (turned,) = tie((mid_turned,), after)
        return in_grad(places, turned, d_in, n, experts, c * each, each, 2 * each, whole)

    each = experts // CHUNKS
    low = gradient(0, third)
    d_normed_mid = d_normed.result()
    gate_sum = d_normed_mid[:, d:]
    d_normed_mid = d_normed_mid[:, :d]
    d_mid_hat = d_normed_mid * gain_mid
    d_middle = cotangent.astype(f32) + inv_mid * (
        d_mid_hat - mid_hat * jnp.mean(d_mid_hat * mid_hat, axis=-1, keepdims=True)
    )
    branch = Gather(d_middle.astype(bf16), groups)
    moved = branch.step(after=low)
    low = gradient(1, [d_middle], low)
    moved_on = branch.step(after=low)
    low_keep, low_send = low[0], tie(low[1:], moved)[0]
    low_terms = flip_reduce(low_keep, low_send, "dp", n)
    high = gradient(2, moved)
    moved = branch.step(after=high + low_terms[3:])
    high = gradient(3, moved_on, high)
    branch.step(after=high)
    high_keep, high_send = high[0], tie(high[1:], moved)[0]
    high_terms = flip_reduce(high_keep, high_send, "dp", n)
    d_branch = branch.pieces()

    moe_second = mixing.step(after=d_branch + high_terms[3:])
    dq, dk, dv, d_branch_all = attn_back(
        order, d_branch, attn_weights, q, k, v, lse, seg_row, seg_col
    )
    dq, dk, dv = tie((dq, dk, dv), moe_second)
    moe_third = mixing.step()
    d_projected, head_part, in_part, *to_rows = proj_back(
        order, attn_weights, q_raw, k_raw, dq, dk, dv, gain_head, cosine, sine, normed_all, own_rows
    )
    d_normed = Scatter(to_rows, groups)
    late = [d_normed.step(after=moe_third + low_terms[2:3])]
    (projected,) = tie((d_projected,), late[0])
    qkv_keep, qkv_send, out_keep, out_send = attn_grad(
        places, normed_all, projected, context, d_branch_all, n
    )
    late.append(d_normed.step())
    qkv_send, out_send = tie((qkv_send, out_send), late[1])
    qkv_terms = flip_reduce(qkv_keep, qkv_send, "dp", n)
    out_terms = flip_reduce(out_keep, out_send, "dp", n)
    (dn_grad,) = tie((dn_grad,), late[0])
    dn_grad = place(dn_grad, experts)
    late.append(
        d_normed.step(after=[qkv_keep, dn_grad])
    )

    (late_low,) = tie(low_terms[2:3], late[1])
    gu_grad = finish(None, low_terms[:2] + [late_low], experts, 0)
    late.append(d_normed.step(after=[gu_grad] + qkv_terms[3:] + out_terms[3:] + high_terms[2:3]))
    (late_high,) = tie(high_terms[2:3], late[3])
    gu_grad = finish(gu_grad, high_terms[:2] + [late_high], experts, 2 * each)
    late.append(mixing.step(after=late[3]))
    qkv_terms = qkv_terms[:2] + list(tie(qkv_terms[2:3], late[4]))
    d_normed_in = d_normed.result()
    d_x_hat = d_normed_in * gain_in
    input_grad = d_middle + inv_in * (
        d_x_hat - x_hat * jnp.mean(d_x_hat * x_hat, axis=-1, keepdims=True)
    )
    mixed = (middle + mixing.result()).astype(bf16)
    gate_grad = jnp.sum(jnp.where(chosen, gate_sum[:, None, :experts], 0.0), axis=-1)
    out_terms = out_terms[:2] + list(tie(out_terms[2:3], late[4]))
    qkv_grad = sum(t[0].astype(f32) for t in qkv_terms[:3])
    out_weight_grad = sum(t[0].astype(f32) for t in out_terms[:3])

    mid_part = jnp.sum(d_normed_mid * mid_hat, axis=0)
    (in_part,) = tie((in_part,), late[2])
    layer_part = jnp.stack([in_part[0] / gain_in, mid_part]).reshape(2, n, groups, -1)
    layer_part = jnp.stack(relative([layer_part[:, :, t] for t in range(groups)], "tensor"))
    for bit in bits_of(groups):
        pairs = layer_part.reshape((layer_part.shape[0] // 2, 2) + layer_part.shape[1:])
        layer_part = pairs[:, 0] + flip_step(pairs[:, 1], "tensor", groups, bit)
    head_parts = split_last(head_part.reshape(2, heads, HD), n)
    rows = [
        jnp.concatenate([layer_part[0, :, k].reshape(-1), h.reshape(-1)])
        for k, h in enumerate(head_parts)
    ]
    rows = jnp.stack(relative(rows, "dp"))
    summed = flip_reduce_rows(rows, "dp", n)
    cut = 2 * (depth // groups)
    layer_grad = summed[:cut].reshape(2, depth // groups)
    head_grad = summed[cut:].reshape(2, heads, HD // n)

    return (
        mixed,
        input_grad,
        gate_grad,
        qkv_grad,
        out_weight_grad,
        head_grad,
        layer_grad,
        gu_grad,
        dn_grad,
    )


def solution(mesh):
    return jax.shard_map(
        per_device,
        mesh=mesh,
        in_specs=(
            P(("dp", "tensor"), None),
            P("dp", None),
            P(("dp", "tensor"), None),
            P(("dp", "tensor"), None),
            P(("dp", "tensor"), None),
            P(None, "dp", "tensor"),
            P("tensor", "dp"),
            P(None, "tensor", "dp"),
            P(None, "dp"),
            P(None, None, "dp", "tensor"),
            P(None, "tensor", "dp"),
        ),
        out_specs=(
            P(("dp", "tensor"), None),
            P(("dp", "tensor"), None),
            P(("dp", "tensor"), None),
            P(None, "dp", "tensor"),
            P("tensor", "dp"),
            P(None, "tensor", "dp"),
            P(None, ("dp", "tensor")),
            P(None, None, "dp", "tensor"),
            P(None, "tensor", "dp"),
        ),
        check_vma=False,
    )
```
